32 devices in a mesh: seq: 8 (over z, core), batch: 4 (over y, x).
Axes of the slice: x: 2, y: 2, z: 4, core: 2. Of those that a mesh axis runs over, the one named last changes fastest.
Arguments:
- block_input: bfloat16 [128, 1024, 512], P('batch', 'seq'), may hold values from -6 to 6
- window_lengths: int32 [128], P('batch'), may hold values from 256 to 1024, as said below
- conv_weight: bfloat16 [9, 512, 512], replicated, may hold values from -0.09375 to 0.09375
- conv_bias: float32 [512], replicated, may hold values from -3 to 3
- norm1_gain: float32 [512], replicated, may hold values from 0.1 to 1.9
- norm1_bias: float32 [512], replicated, may hold values from -3 to 3
- up_weight: bfloat16 [512, 2048], replicated, may hold values from -0.25 to 0.25
- up_bias: float32 [2048], replicated, may hold values from -3 to 3
- down_weight: bfloat16 [2048, 512], replicated, may hold values from -0.125 to 0.125
- down_bias: float32 [512], replicated, may hold values from -3 to 3
- norm2_gain: float32 [512], replicated, may hold values from 0.1 to 1.9
- norm2_bias: float32 [512], replicated, may hold values from -3 to 3
- out_cotangent: bfloat16 [128, 1024, 512], P('batch', 'seq'), may hold values from -6 to 6
Outputs:
- block_output: bfloat16 [128, 1024, 512], P('batch', 'seq')
- input_grad: bfloat16 [128, 1024, 512], P('batch', 'seq')
- conv_weight_grad: float32 [9, 512, 512], replicated
- conv_bias_grad: float32 [512], replicated
- norm1_gain_grad: float32 [512], replicated
- norm1_bias_grad: float32 [512], replicated
- up_weight_grad: float32 [512, 2048], replicated
- up_bias_grad: float32 [2048], replicated
- down_weight_grad: float32 [2048, 512], replicated
- down_bias_grad: float32 [512], replicated
- norm2_gain_grad: float32 [512], replicated
- norm2_bias_grad: float32 [512], replicated
The draws below stay inside these ranges and needn't reach their ends.
Inputs may be any that keep to these rules, and one draw needn't show every extreme that they name: `window_lengths`: each window's length is 256, 512 or 1024; among each 32 consecutive windows at least one has length 1024.
All inputs are finite; a program needn't handle non-finite values.
Results may differ from the reference program's by a relative error of at most 0.0075.
Values may be sent and summed in bfloat16 or wider, within the bound.
A program may use at most 320 MiB of HBM per device.

```python
import math
import jax
import jax.numpy as jnp
from jax import lax

D = 512
FF = 2048
KERNEL = 9
DILATION = 32
L = 1024
W_DEV = 32
WINDOWS = 128


def draw_window_lengths(key, part):
    key = jax.random.fold_in(key, 11)
    key_class, key_pick = jax.random.split(key)
    classes = jax.random.randint(key_class, (WINDOWS,), 0, 10)
    lengths = jnp.where(classes < 4, L // 4, jnp.where(classes < 7, L // 2, L))
    picked = jax.random.randint(key_pick, (WINDOWS // W_DEV,), 0, W_DEV)
    indices = jnp.arange(WINDOWS, dtype=jnp.int32)
    forced = indices % W_DEV == jnp.repeat(picked, W_DEV)
    return jnp.where(forced, L, lengths).astype(jnp.int32)


def shard_levels(rng, extent, cuts, low, top_value):
    factor_of, own = 1.0, jax.random.fold_in(rng, 6)
    for dim, shards_of in cuts:
        steps = jnp.exp(jax.random.uniform(jax.random.fold_in(own, dim), (shards_of,), jnp.float32, low / len(cuts), top_value / len(cuts)))
        factor_of = factor_of * jnp.repeat(steps, extent[dim] // shards_of).reshape([-1 if axis == dim else 1 for axis in range(len(extent))])
    return factor_of


def gaussian(key, shape, scale, most, cuts=(), held_as=jnp.bfloat16):
    array = jax.random.normal(key, shape, jnp.float32) * scale
    if len(cuts) > 0:
        array = shard_levels(key, shape, cuts, -0.22, 0.18) * array
    return jnp.clip(array, min=-most, max=most).astype(held_as)


def setup_inputs(seed: int = 0) -> dict:
    key_list = jax.random.split(jax.random.key(seed), 14)
    block_input = gaussian(key_list[0], (WINDOWS, L, D), 1.0, 6.0, ((0, 4), (1, 8)))
    window_lengths = draw_window_lengths(jax.random.fold_in(key_list[13], 71), 0)
    conv_weight = gaussian(key_list[2], (KERNEL, D, D), (KERNEL * D) ** -0.5, 0.09375)
    conv_bias = gaussian(key_list[3], (D,), 0.5, 3.0, (), jnp.float32)
    norm1_gain = jnp.clip(1.0 + 0.18 * jax.random.normal(key_list[4], (D,), jnp.float32), 0.1, 1.9)
    norm1_bias = gaussian(key_list[5], (D,), 0.5, 3.0, (), jnp.float32)
    up_weight = gaussian(key_list[6], (D, FF), D ** -0.5, 0.25)
    up_bias = gaussian(key_list[7], (FF,), 0.5, 3.0, (), jnp.float32)
    down_weight = gaussian(key_list[8], (FF, D), FF ** -0.5, 0.125)
    down_bias = gaussian(key_list[9], (D,), 0.5, 3.0, (), jnp.float32)
    norm2_gain = jnp.clip(1.0 + 0.18 * jax.random.normal(key_list[10], (D,), jnp.float32), 0.1, 1.9)
    norm2_bias = gaussian(key_list[11], (D,), 0.5, 3.0, (), jnp.float32)
    out_cotangent = gaussian(key_list[12], (WINDOWS, L, D), 1.0, 6.0, ((0, 4), (1, 8)))
    return {"block_input": block_input, "window_lengths": window_lengths, "conv_weight": conv_weight, "conv_bias": conv_bias, "norm1_gain": norm1_gain, "norm1_bias": norm1_bias, "up_weight": up_weight, "up_bias": up_bias, "down_weight": down_weight, "down_bias": down_bias, "norm2_gain": norm2_gain, "norm2_bias": norm2_bias, "out_cotangent": out_cotangent}


@jax.custom_vjp
def low(v):
    return lax.optimization_barrier(v.astype(jnp.bfloat16)).astype(jnp.float32)

@jax.custom_vjp
def low_back(v):
    return v

def low_keep(v):
    return (low(v), None)

def low_pass(kept, grad):
    return (grad,)

def back_keep(v):
    return (v, None)

def back_low(kept, grad):
    return (low(grad),)
low.defvjp(low_keep, low_pass)
low_back.defvjp(back_keep, back_low)

def product(left, right):
    return jnp.einsum('wld,de->wle', left, right, precision=lax.Precision.HIGHEST)

def layer_norm(values, gain, shift):
    center = lax.optimization_barrier(jnp.mean(values, axis=-1, keepdims=True))
    centered = values - center
    spread = lax.optimization_barrier(jnp.mean(centered * centered, axis=-1, keepdims=True))
    return centered * lax.rsqrt(spread + 1e-05) * gain + shift

def forward(params, block, mask_rows):
    conv_weight, conv_bias, norm1_gain, norm1_bias, up_weight, up_bias, down_weight, down_bias, norm2_gain, norm2_bias = params
    keep_mask = mask_rows[..., None]
    start_rows = keep_mask * block
    rounded = low_back(low(start_rows))
    reach = DILATION * (KERNEL // 2)
    padded = jnp.pad(rounded, ((0, 0), (reach, reach), (0, 0)))
    window_len = block.shape[1]
    conv_out = conv_bias + jnp.zeros_like(block)
    for tap_index in range(KERNEL):
        offset = tap_index * DILATION
        conv_out = conv_out + product(padded[:, offset:offset + window_len], conv_weight[tap_index])
    activated = jax.nn.gelu(low_back(conv_out), approximate=False)
    branch = low_back(low(layer_norm(activated, norm1_gain, norm1_bias)))
    middle = start_rows + branch
    upper = low_back(product(low(middle), up_weight) + up_bias)
    lower = low_back(product(low(jax.nn.gelu(upper, approximate=False)), down_weight) + down_bias)
    return keep_mask * (middle + layer_norm(lower, norm2_gain, norm2_bias))

def reference(block_input, window_lengths, conv_weight, conv_bias, norm1_gain, norm1_bias, up_weight, up_bias, down_weight, down_bias, norm2_gain, norm2_bias, out_cotangent):
    params = (conv_weight.astype(jnp.float32), conv_bias.astype(jnp.float32), norm1_gain.astype(jnp.float32), norm1_bias.astype(jnp.float32), up_weight.astype(jnp.float32), up_bias.astype(jnp.float32), down_weight.astype(jnp.float32), down_bias.astype(jnp.float32), norm2_gain.astype(jnp.float32), norm2_bias.astype(jnp.float32))
    positions = jnp.arange(L, dtype=jnp.int32)
    mask_all = (positions[None, :] < window_lengths[:, None]).astype(jnp.float32)
    group_size = math.gcd(WINDOWS, max(1, 4096 // L))
    group_count = WINDOWS // group_size
    inputs = block_input.astype(jnp.float32).reshape((group_count, group_size, L, D))
    cotangents = out_cotangent.astype(jnp.float32).reshape((group_count, group_size, L, D))
    masks = mask_all.reshape((group_count, group_size, L))

    def step_fn(totals, item):
        block, cotangent, mask_rows = item
        result, pullback = jax.vjp(lambda weights, rows: forward(weights, rows, mask_rows), params, block)
        grads, back_rows = pullback(cotangent)
        totals = jax.tree.map(jnp.add, totals, grads)
        return (totals, (result.astype(jnp.bfloat16), back_rows.astype(jnp.bfloat16)))
    zeros_init = jax.tree.map(jnp.zeros_like, params)
    totals, (results, backs) = lax.scan(step_fn, zeros_init, (inputs, cotangents, masks))
    block_output = results.reshape((WINDOWS, L, D))
    input_grad = backs.reshape((WINDOWS, L, D))
    return (block_output, input_grad, totals[0], totals[1], totals[2], totals[3], totals[4], totals[5], totals[6], totals[7], totals[8], totals[9])
```

```python
import functools
import math

import jax
import jax.numpy as jnp
from jax import lax
from jax.experimental import pallas as pl
from jax.experimental.pallas import tpu as pltpu
from jax.sharding import PartitionSpec as P

KERNEL = 9
DILATION = 32
REACH = DILATION * (KERNEL // 2)
TILE_ROWS = 512
FF_TILE = 512
EPS = 1e-05
VMEM_BYTES = 62 * 2**20


def passed_along(shard, axis, by):
    size = lax.axis_size(axis)
    pairs = [(i, i + by) for i in range(size) if 0 <= i + by < size]
    return lax.ppermute(shard, axis, pairs)


def dot(left, right):
    return jnp.dot(left, right, preferred_element_type=jnp.float32)


def gelu_parts(values):
    cumulative = 0.5 + 0.5 * lax.erf(values * (1.0 / math.sqrt(2.0)))
    density = jnp.exp(-0.5 * values * values) * (1.0 / math.sqrt(2.0 * math.pi))
    return values * cumulative, cumulative + values * density


def normalize(values):
    center = jnp.mean(values, axis=-1, keepdims=True)
    centered = values - center
    inverse = lax.rsqrt(jnp.mean(centered * centered, axis=-1, keepdims=True) + EPS)
    return centered * inverse, inverse


def normalize_back(upstream, normed, inverse, gain):
    inner = upstream * gain
    return inverse * (
        inner
        - jnp.mean(inner, axis=-1, keepdims=True)
        - normed * jnp.mean(inner * normed, axis=-1, keepdims=True)
    )


def col_sum(values):
    return jnp.sum(values, axis=0, keepdims=True)


def block_kernel(depth, *refs):
    pieces = 2 * depth + 1
    keeps = refs[0]
    parts = refs[1 : 1 + pieces]
    (
        cot,
        conv_w,
        conv_b,
        gain1,
        bias1,
        up_w,
        up_wt,
        up_b,
        down_w,
        down_wt,
        down_b,
        gain2,
        bias2,
        out,
        pre_out,
        mid_out,
        d_up,
        d_down,
        d_vec,
        d_upb,
        ext,
        hidden,
        slope,
    ) = refs[1 + pieces :]
    step = pl.program_id(0)
    group, rows_here, width = cot.shape
    rows = group * rows_here
    ff = up_w.shape[1]
    tile = min(FF_TILE, ff)
    base = depth * rows_here - REACH

    @pl.when(step == 0)
    def _():
        d_up[...] = jnp.zeros_like(d_up)
        d_down[...] = jnp.zeros_like(d_down)
        d_vec[...] = jnp.zeros_like(d_vec)
        d_upb[...] = jnp.zeros_like(d_upb)

    keep_here = []
    for g in range(group):
        window = step * group + g
        for i in range(pieces):
            keep = keeps[i, window]
            if i == depth:
                keep_here.append(keep)
            ext[g, i * rows_here : (i + 1) * rows_here, :] = parts[i][g] * keep.astype(jnp.bfloat16)

    pre = jnp.broadcast_to(conv_b[...], (rows, width))
    for tap in range(KERNEL):
        begin = base + tap * DILATION
        taken = ext[:, begin : begin + rows_here, :].reshape(rows, width)
        pre = pre + dot(taken, conv_w[tap])
    act, slope1 = gelu_parts(pre)
    n1, s1 = normalize(act)
    branch = (n1 * gain1[...] + bias1[...]).astype(jnp.bfloat16)
    start = ext[:, depth * rows_here : (depth + 1) * rows_here, :].reshape(rows, width)
    middle = start.astype(jnp.float32) + branch.astype(jnp.float32)
    middle_low = middle.astype(jnp.bfloat16)

    lower = jnp.broadcast_to(down_b[...], (rows, width))
    for j in range(ff // tile):
        cols = slice(j * tile, (j + 1) * tile)
        upper = dot(middle_low, up_w[:, cols]) + up_b[:, cols]
        h, sl = gelu_parts(upper)
        h = h.astype(jnp.bfloat16)
        hidden[:, cols] = h
        slope[:, cols] = sl
        lower = lower + dot(h, down_w[cols, :])
    n2, s2 = normalize(lower)
    shaped = (n2 * gain2[...] + bias2[...] + middle).reshape(group, rows_here, width)
    incoming = []
    for g in range(group):
        out[g] = (shaped[g] * keep_here[g]).astype(jnp.bfloat16)
        incoming.append(cot[g].astype(jnp.float32) * keep_here[g])
    incoming = jnp.concatenate(incoming, axis=0)
    d_vec[0:1, :] += col_sum(incoming * n2)
    d_vec[1:2, :] += col_sum(incoming)
    lower_low = normalize_back(incoming, n2, s2, gain2[...]).astype(jnp.bfloat16)
    d_vec[2:3, :] += col_sum(lower_low.astype(jnp.float32))
    lower_t = lower_low.T
    middle_t = middle_low.T
    middle_grad = incoming
    for j in range(ff // tile):
        cols = slice(j * tile, (j + 1) * tile)
        hidden_grad = dot(lower_low, down_wt[:, cols])
        upper_grad = hidden_grad * slope[:, cols]
        upper_low = upper_grad.astype(jnp.bfloat16)
        d_upb[:, cols] += col_sum(upper_low.astype(jnp.float32))
        d_down[:, cols] += dot(lower_t, hidden[:, cols])
        d_up[:, cols] += dot(middle_t, upper_low)
        middle_grad = middle_grad + dot(upper_low, up_wt[cols, :])
    branch_low = middle_grad.astype(jnp.bfloat16)
    mid_out[...] = branch_low.reshape(group, rows_here, width)
    branch_grad = branch_low.astype(jnp.float32)
    d_vec[3:4, :] += col_sum(branch_grad * n1)
    d_vec[4:5, :] += col_sum(branch_grad)
    pre_low = (normalize_back(branch_grad, n1, s1, gain1[...]) * slope1).astype(jnp.bfloat16)
    d_vec[5:6, :] += col_sum(pre_low.astype(jnp.float32))
    pre_out[...] = pre_low.reshape(group, rows_here, width)


def blocks(keeps, parts, cot, conv_w, conv_b, gain1, bias1, up_w, up_wt, up_b, down_w, down_wt, down_b, gain2, bias2):
    windows, rows_here, width = cot.shape
    depth = len(parts) // 2
    ff = up_w.shape[1]
    group = max(1, TILE_ROWS // rows_here)
    rows = group * rows_here
    tile = pl.BlockSpec((group, rows_here, width), lambda i: (i, 0, 0))
    whole = pl.BlockSpec(memory_space=pltpu.VMEM)
    whole_params = [conv_w, conv_b, gain1, bias1, up_w, up_wt, up_b, down_w, down_wt, down_b, gain2, bias2]
    return pl.pallas_call(
        functools.partial(block_kernel, depth),
        grid=(windows // group,),
        in_specs=[pl.BlockSpec(memory_space=pltpu.SMEM)] + [tile] * (len(parts) + 1) + [whole] * len(whole_params),
        out_specs=[tile, tile, tile, whole, whole, whole, whole],
        out_shape=[jax.ShapeDtypeStruct(cot.shape, jnp.bfloat16)] * 3
        + [
            jax.ShapeDtypeStruct((width, ff), jnp.float32),
            jax.ShapeDtypeStruct((width, ff), jnp.float32),
            jax.ShapeDtypeStruct((8, width), jnp.float32),
            jax.ShapeDtypeStruct((1, ff), jnp.float32),
        ],
        scratch_shapes=[
            pltpu.VMEM((group, (2 * depth + 1) * rows_here, width), jnp.bfloat16),
            pltpu.VMEM((rows, ff), jnp.bfloat16),
            pltpu.VMEM((rows, ff), jnp.float32),
        ],
        compiler_params=pltpu.CompilerParams(vmem_limit_bytes=VMEM_BYTES),
        name="block",
    )(keeps, *parts, cot, *whole_params)


def back_kernel(depth, *refs):
    pieces = 2 * depth + 1
    keeps = refs[0]
    parts = refs[1 : 1 + pieces]
    start_in, mid_in, conv_wt, out, d_conv, ext = refs[1 + pieces :]
    step = pl.program_id(0)
    group, rows_here, width = start_in.shape
    rows = group * rows_here
    base = depth * rows_here - REACH

    @pl.when(step == 0)
    def _():
        d_conv[...] = jnp.zeros_like(d_conv)

    start = []
    for g in range(group):
        start.append(start_in[g] * keeps[depth, step * group + g].astype(jnp.bfloat16))
        for i in range(pieces):
            ext[g, i * rows_here : (i + 1) * rows_here, :] = parts[i][g]
    start_t = jnp.concatenate(start, axis=0).T
    grad = jnp.zeros((rows, width), jnp.float32)
    for tap in range(KERNEL):
        begin = base + (KERNEL - 1 - tap) * DILATION
        taken = ext[:, begin : begin + rows_here, :].reshape(rows, width)
        d_conv[tap] += dot(start_t, taken)
        grad = grad + dot(taken, conv_wt[tap])
    grad = grad.astype(jnp.bfloat16).astype(jnp.float32) + mid_in[...].reshape(rows, width).astype(jnp.float32)
    grad = grad.reshape(group, rows_here, width)
    for g in range(group):
        out[g] = (grad[g] * keeps[depth, step * group + g]).astype(jnp.bfloat16)


def conv_back(keeps, parts, start, mid, conv_wt):
    windows, rows_here, width = start.shape
    depth = len(parts) // 2
    group = max(1, TILE_ROWS // rows_here)
    tile = pl.BlockSpec((group, rows_here, width), lambda i: (i, 0, 0))
    whole = pl.BlockSpec(memory_space=pltpu.VMEM)
    return pl.pallas_call(
        functools.partial(back_kernel, depth),
        grid=(windows // group,),
        in_specs=[pl.BlockSpec(memory_space=pltpu.SMEM)] + [tile] * (len(parts) + 2) + [whole],
        out_specs=[tile, whole],
        out_shape=[
            jax.ShapeDtypeStruct(start.shape, jnp.bfloat16),
            jax.ShapeDtypeStruct((KERNEL, width, width), jnp.float32),
        ],
        scratch_shapes=[pltpu.VMEM((group, (2 * depth + 1) * rows_here, width), jnp.bfloat16)],
        compiler_params=pltpu.CompilerParams(vmem_limit_bytes=VMEM_BYTES),
        name="conv_back",
    )(keeps, *parts, start, mid, conv_wt)


def spread(shard, depth):
    return [
        shard if offset == 0 else passed_along(shard, "seq", offset)
        for offset in range(depth, -depth - 1, -1)
    ]


def per_device(
    block_input,
    window_lengths,
    conv_weight,
    conv_bias,
    norm1_gain,
    norm1_bias,
    up_weight,
    up_bias,
    down_weight,
    down_bias,
    norm2_gain,
    norm2_bias,
    out_cotangent,
):
    windows, rows_here, width = block_input.shape
    depth = -(-REACH // rows_here)
    parts = spread(block_input, depth)
    first = (lax.axis_index("seq") + jnp.arange(-depth, depth + 1, dtype=jnp.int32)) * rows_here
    keeps = (first[:, None] < window_lengths[None, :]).astype(jnp.float32)
    row = lambda v: v.reshape(1, -1)
    conv_wt = conv_weight.transpose(0, 2, 1)
    out, pre_low, mid_low, d_up, d_down_t, d_vec, d_upb = blocks(
        keeps,
        parts,
        out_cotangent,
        conv_weight,
        row(conv_bias),
        row(norm1_gain),
        row(norm1_bias),
        up_weight,
        up_weight.T,
        row(up_bias),
        down_weight,
        down_weight.T,
        row(down_bias),
        row(norm2_gain),
        row(norm2_bias),
    )
    input_grad, d_conv = conv_back(keeps, spread(pre_low, depth), block_input, mid_low, conv_wt)
    d_conv, d_up, d_down_t, d_vec, d_upb = lax.psum((d_conv, d_up, d_down_t, d_vec, d_upb), ("seq", "batch"))
    return (
        out,
        input_grad,
        d_conv,
        d_vec[5],
        d_vec[3],
        d_vec[4],
        d_up,
        d_upb[0],
        d_down_t.T,
        d_vec[2],
        d_vec[0],
        d_vec[1],
    )


def solution(mesh):
    rows = P("batch", "seq", None)
    return jax.shard_map(
        per_device,
        mesh=mesh,
        in_specs=(rows, P("batch")) + (P(),) * 10 + (rows,),
        out_specs=(rows, rows) + (P(),) * 10,
        check_vma=False,
    )
```

```python
import functools
import math

import jax
import jax.numpy as jnp
from jax import lax
from jax.experimental import pallas as pl
from jax.experimental.pallas import tpu as pltpu
from jax.sharding import PartitionSpec as P

KERNEL = 9
DILATION = 32
REACH = DILATION * (KERNEL // 2)
TILE_ROWS = 512
FF_TILE = 512
EPS = 1e-05
VMEM_BYTES = 63 * 2**20
MESH = pl.DeviceIdType.MESH
RING = 4


def passed_along(shard, axis, by):
    size = lax.axis_size(axis)
    pairs = [(i, i + by) for i in range(size) if 0 <= i + by < size]
    return lax.ppermute(shard, axis, pairs)


def product(left, right, over_left, over_right):
    return lax.dot_general(
        left, right, (((over_left,), (over_right,)), ((), ())), preferred_element_type=jnp.float32
    )


def dot(left, right):
    return product(left, right, 1, 0)


def dot_nt(left, right):
    return product(left, right, 1, 1)


def dot_tn(left, right):
    return product(left, right, 0, 0)


def gelu_parts(values):
    cumulative = 0.5 + 0.5 * lax.erf(values * (1.0 / math.sqrt(2.0)))
    density = jnp.exp(-0.5 * values * values) * (1.0 / math.sqrt(2.0 * math.pi))
    return values * cumulative, cumulative + values * density


def normalize(values):
    center = jnp.mean(values, axis=-1, keepdims=True)
    centered = values - center
    inverse = lax.rsqrt(jnp.mean(centered * centered, axis=-1, keepdims=True) + EPS)
    return centered * inverse, inverse


def normalize_back(upstream, normed, inverse, gain):
    inner = upstream * gain
    return inverse * (
        inner
        - jnp.mean(inner, axis=-1, keepdims=True)
        - normed * jnp.mean(inner * normed, axis=-1, keepdims=True)
    )


def col_sum(values):
    return jnp.sum(values, axis=0, keepdims=True)


def remote(src, dst, send_sem, recv_sem, device):
    return pltpu.make_async_remote_copy(
        src_ref=src,
        dst_ref=dst,
        send_sem=send_sem,
        recv_sem=recv_sem,
        device_id=device,
        device_id_type=MESH,
    )


def block_compute(step, depth, keeps, parts, refs):
    (
        cot,
        conv_w,
        conv_b,
        gain1,
        bias1,
        up_w,
        up_b,
        down_w,
        down_b,
        gain2,
        bias2,
        out,
        ext,
        pre_out,
        mid_out,
        d_ffn,
        d_vec,
        hidden,
        slope,
    ) = refs
    pieces = 2 * depth + 1
    group, rows_here, width = cot.shape
    rows = group * rows_here
    ff = up_w.shape[1]
    tile = min(FF_TILE, ff)
    tiles = ff // tile
    base = depth * rows_here - REACH

    @pl.when(step == 0)
    def _():
        d_ffn[...] = jnp.zeros_like(d_ffn)
        d_vec[...] = jnp.zeros_like(d_vec)

    keep_here = []
    for g in range(group):
        window = step * group + g
        for i in range(pieces):
            keep = keeps[i, window]
            if i == depth:
                keep_here.append(keep)
            ext[g, i * rows_here : (i + 1) * rows_here, :] = parts[i][g] * keep.astype(jnp.bfloat16)

    pre = jnp.broadcast_to(conv_b[...], (rows, width))
    for tap in range(KERNEL):
        begin = base + tap * DILATION
        taken = ext[:, begin : begin + rows_here, :].reshape(rows, width)
        pre = pre + dot(taken, conv_w[tap])
    act, slope1 = gelu_parts(pre)
    n1, s1 = normalize(act)
    branch = (n1 * gain1[...] + bias1[...]).astype(jnp.bfloat16)
    start = ext[:, depth * rows_here : (depth + 1) * rows_here, :].reshape(rows, width)
    middle = start.astype(jnp.float32) + branch.astype(jnp.float32)
    middle_low = middle.astype(jnp.bfloat16)

    lower = jnp.broadcast_to(down_b[...], (rows, width))
    for j in range(tiles):
        cols = slice(j * tile, (j + 1) * tile)
        upper = dot(middle_low, up_w[:, cols]) + up_b[:, cols]
        h, sl = gelu_parts(upper)
        h = h.astype(jnp.bfloat16)
        hidden[:, cols] = h
        slope[:, cols] = sl
        lower = lower + dot(h, down_w[cols, :])
    n2, s2 = normalize(lower)
    shaped = (n2 * gain2[...] + bias2[...] + middle).reshape(group, rows_here, width)
    incoming = []
    for g in range(group):
        out[g] = (shaped[g] * keep_here[g]).astype(jnp.bfloat16)
        incoming.append(cot[g].astype(jnp.float32) * keep_here[g])
    incoming = jnp.concatenate(incoming, axis=0)
    d_vec[0:1, :] += col_sum(incoming * n2)
    d_vec[1:2, :] += col_sum(incoming)
    lower_low = normalize_back(incoming, n2, s2, gain2[...]).astype(jnp.bfloat16)
    d_vec[2:3, :] += col_sum(lower_low.astype(jnp.float32))
    middle_grad = incoming
    for j in range(tiles):
        cols = slice(j * tile, (j + 1) * tile)
        hidden_grad = dot_nt(lower_low, down_w[cols, :])
        upper_low = (hidden_grad * slope[:, cols]).astype(jnp.bfloat16)
        d_vec[8 + j : 9 + j, :] += col_sum(upper_low.astype(jnp.float32))
        d_ffn[tiles + j] += dot_tn(hidden[:, cols], lower_low)
        d_ffn[j] += dot_tn(middle_low, upper_low)
        middle_grad = middle_grad + dot_nt(upper_low, up_w[:, cols])
    branch_low = middle_grad.astype(jnp.bfloat16)
    mid_out[...] = branch_low.reshape(group, rows_here, width)
    branch_grad = branch_low.astype(jnp.float32)
    d_vec[3:4, :] += col_sum(branch_grad * n1)
    d_vec[4:5, :] += col_sum(branch_grad)
    pre_low = (normalize_back(branch_grad, n1, s1, gain1[...]) * slope1).astype(jnp.bfloat16)
    d_vec[5:6, :] += col_sum(pre_low.astype(jnp.float32))
    pre_low = pre_low.reshape(group, rows_here, width)
    pre_out[...] = pre_low
    return pre_low


def block_kernel(depth, *refs):
    pieces = 2 * depth + 1
    block_compute(pl.program_id(0), depth, refs[0], refs[1 : 1 + pieces], refs[1 + pieces :])


def block_halo_kernel(steps, *refs):
    keeps, x_hbm, x_mid = refs[:3]
    inner = list(refs[3 : 3 + 15])
    pre_l, pre_r = refs[18:20]
    d_ffn, d_vec = refs[20:22]
    hidden, slope, from_l, from_r, pre_keep, fs, fr, bs, br = refs[22:]
    cot = inner[0]
    group = cot.shape[0]
    step = pl.program_id(0)
    s = lax.axis_index("seq")
    b = lax.axis_index("batch")
    last = lax.axis_size("seq") - 1
    has = (s > 0, s < last)
    other = ((s - 1, b), (s + 1, b))

    def halo(i, side):
        rows = pl.ds(i * group, group)
        land = (from_r, from_l)[side]
        return remote(x_hbm.at[rows], land.at[rows], fs.at[i, side], fr.at[i, side], other[side])

    def halo_in(i, side):
        rows = pl.ds(i * group, group)
        land = (from_l, from_r)[side]
        return remote(x_hbm.at[rows], land.at[rows], fs.at[i, side], fr.at[i, 1 - side], other[side])

    def back(i, side):
        rows = pl.ds(i * group, group)
        land = (pre_r, pre_l)[side]
        return remote(pre_keep.at[lax.rem(i, 2)], land.at[rows], bs.at[i, side], br.at[i, side], other[side])

    def back_in(i, side):
        rows = pl.ds(i * group, group)
        land = (pre_l, pre_r)[side]
        return remote(pre_keep.at[lax.rem(i, 2)], land.at[rows], bs.at[i, side], br.at[i, 1 - side], other[side])

    @pl.when(step == 0)
    def _():
        barrier = pltpu.get_barrier_semaphore()
        for side in range(2):

            @pl.when(has[side])
            def _():
                pl.semaphore_signal(barrier, inc=1, device_id=other[side], device_id_type=MESH)

        pl.semaphore_wait(barrier, (s > 0).astype(jnp.int32) + (s < last).astype(jnp.int32))
        for side in range(2):

            @pl.when(has[side])
            def _():
                halo(0, side).start()

            @pl.when(jnp.logical_not(has[side]))
            def _():
                land = (from_l, from_r)[side]
                land[...] = jnp.zeros_like(land)

    for side in range(2):

        @pl.when(has[side])
        def _():
            halo_in(step, side).wait_recv()

            @pl.when(step + 1 < steps)
            def _():
                halo(step + 1, side).start()

    rows = pl.ds(step * group, group)
    parts = (from_l.at[rows], x_mid, from_r.at[rows])
    refs_in = inner[:11] + inner[11:15] + [d_ffn, d_vec, hidden, slope]
    pre_low = block_compute(step, 1, keeps, parts, refs_in)
    for side in range(2):

        @pl.when(has[side] & (step >= 2))
        def _():
            back(step - 2, side).wait_send()

    pre_keep[lax.rem(step, 2)] = pre_low
    for side in range(2):

        @pl.when(has[side])
        def _():
            back(step, side).start()

    @pl.when(step == steps - 1)
    def _():
        for side in range(2):

            @pl.when(has[side])
            def _():
                for i in range(steps):
                    halo(i, side).wait_send()
                    back_in(i, side).wait_recv()
                for i in range(max(0, steps - 2), steps):
                    back(i, side).wait_send()


def block_params(conv_w, conv_b, gain1, bias1, up_w, up_b, down_w, down_b, gain2, bias2):
    row = lambda v: v.reshape(1, -1)
    return [conv_w, row(conv_b), row(gain1), row(bias1), up_w, row(up_b), down_w, row(down_b), row(gain2), row(bias2)]


def blocks_halo(keeps, x, cot, params):
    windows, rows_here, width = cot.shape
    ff = params[4].shape[1]
    group = TILE_ROWS // rows_here
    steps = windows // group
    rows = group * rows_here
    tile = pl.BlockSpec((group, rows_here, width), lambda i: (i, 0, 0))
    wide = pl.BlockSpec((group, 3 * rows_here, width), lambda i: (i, 0, 0))
    whole = pl.BlockSpec(memory_space=pltpu.VMEM)
    anywhere = pl.BlockSpec(memory_space=pl.ANY)
    like = jax.ShapeDtypeStruct(cot.shape, jnp.bfloat16)
    return pl.pallas_call(
        functools.partial(block_halo_kernel, steps),
        grid=(steps,),
        in_specs=[pl.BlockSpec(memory_space=pltpu.SMEM), anywhere, tile, tile] + [whole] * len(params),
        out_specs=[tile, wide, tile, tile, anywhere, anywhere, whole, whole],
        out_shape=[
            like,
            jax.ShapeDtypeStruct((windows, 3 * rows_here, width), jnp.bfloat16),
            like,
            like,
            like,
            like,
            jax.ShapeDtypeStruct((2 * ff // FF_TILE, width, FF_TILE), jnp.float32),
            jax.ShapeDtypeStruct((16, width), jnp.float32),
        ],
        scratch_shapes=[
            pltpu.VMEM((rows, ff), jnp.bfloat16),
            pltpu.VMEM((rows, ff), jnp.float32),
            pltpu.VMEM(cot.shape, jnp.bfloat16),
            pltpu.VMEM(cot.shape, jnp.bfloat16),
            pltpu.VMEM((2, group, rows_here, width), jnp.bfloat16),
            pltpu.SemaphoreType.DMA((steps, 2)),
            pltpu.SemaphoreType.DMA((steps, 2)),
            pltpu.SemaphoreType.DMA((steps, 2)),
            pltpu.SemaphoreType.DMA((steps, 2)),
        ],
        compiler_params=pltpu.CompilerParams(
            vmem_limit_bytes=VMEM_BYTES, collective_id=0, has_side_effects=True
        ),
        name="block",
    )(keeps, x, x, cot, *params)


def blocks(keeps, parts, cot, params):
    windows, rows_here, width = cot.shape
    depth = len(parts) // 2
    ff = params[4].shape[1]
    group = max(1, TILE_ROWS // rows_here)
    rows = group * rows_here
    tile = pl.BlockSpec((group, rows_here, width), lambda i: (i, 0, 0))
    wide = pl.BlockSpec((group, (2 * depth + 1) * rows_here, width), lambda i: (i, 0, 0))
    whole = pl.BlockSpec(memory_space=pltpu.VMEM)
    like = jax.ShapeDtypeStruct(cot.shape, jnp.bfloat16)
    return pl.pallas_call(
        functools.partial(block_kernel, depth),
        grid=(windows // group,),
        in_specs=[pl.BlockSpec(memory_space=pltpu.SMEM)] + [tile] * (len(parts) + 1) + [whole] * len(params),
        out_specs=[tile, wide, tile, tile, whole, whole],
        out_shape=[
            like,
            jax.ShapeDtypeStruct((windows, (2 * depth + 1) * rows_here, width), jnp.bfloat16),
            like,
            like,
            jax.ShapeDtypeStruct((2 * ff // FF_TILE, width, FF_TILE), jnp.float32),
            jax.ShapeDtypeStruct((16, width), jnp.float32),
        ],
        scratch_shapes=[pltpu.VMEM((rows, ff), jnp.bfloat16), pltpu.VMEM((rows, ff), jnp.float32)],
        compiler_params=pltpu.CompilerParams(vmem_limit_bytes=VMEM_BYTES),
        name="block_general",
    )(keeps, *parts, cot, *params)


def back_kernel(depth, *refs):
    pieces = 2 * depth + 1
    keeps = refs[0]
    parts = refs[1 : 1 + pieces]
    start_in, mid_in, conv_w, out, d_conv, ext = refs[1 + pieces :]
    step = pl.program_id(0)
    group, rows_here, width = start_in.shape
    rows = group * rows_here
    base = depth * rows_here - REACH

    @pl.when(step == 0)
    def _():
        d_conv[...] = jnp.zeros_like(d_conv)

    start = []
    for g in range(group):
        start.append(start_in[g] * keeps[depth, step * group + g].astype(jnp.bfloat16))
        for i in range(pieces):
            ext[g, i * rows_here : (i + 1) * rows_here, :] = parts[i][g]
    start = jnp.concatenate(start, axis=0)
    grad = jnp.zeros((rows, width), jnp.float32)
    for tap in range(KERNEL):
        begin = base + (KERNEL - 1 - tap) * DILATION
        taken = ext[:, begin : begin + rows_here, :].reshape(rows, width)
        d_conv[tap] += dot_tn(start, taken)
        grad = grad + dot_nt(taken, conv_w[tap])
    grad = grad.astype(jnp.bfloat16).astype(jnp.float32) + mid_in[...].reshape(rows, width).astype(jnp.float32)
    grad = grad.reshape(group, rows_here, width)
    for g in range(group):
        out[g] = (grad[g] * keeps[depth, step * group + g]).astype(jnp.bfloat16)


def conv_back(keeps, parts, start, mid, conv_w):
    windows, rows_here, width = start.shape
    depth = len(parts) // 2
    group = max(1, TILE_ROWS // rows_here)
    tile = pl.BlockSpec((group, rows_here, width), lambda i: (i, 0, 0))
    whole = pl.BlockSpec(memory_space=pltpu.VMEM)
    return pl.pallas_call(
        functools.partial(back_kernel, depth),
        grid=(windows // group,),
        in_specs=[pl.BlockSpec(memory_space=pltpu.SMEM)] + [tile] * (len(parts) + 2) + [whole],
        out_specs=[tile, whole],
        out_shape=[
            jax.ShapeDtypeStruct(start.shape, jnp.bfloat16),
            jax.ShapeDtypeStruct((KERNEL, width, width), jnp.float32),
        ],
        scratch_shapes=[pltpu.VMEM((group, (2 * depth + 1) * rows_here, width), jnp.bfloat16)],
        compiler_params=pltpu.CompilerParams(vmem_limit_bytes=VMEM_BYTES),
        name="conv_back_general",
    )(keeps, *parts, start, mid, conv_w)


class Reducer:
    stages = 8

    def __init__(self, count, acc, res, res_out, bufs, sems):
        self.count, self.acc, self.res, self.res_out = count, acc, res, res_out
        self.core_in, self.send1, self.recv1, self.kept1 = bufs[:4]
        self.send2, self.recv2, self.kept2 = bufs[4:7]
        self.send3, self.recv3, self.kept3, self.fin = bufs[7:11]
        (
            self.c_s, self.c_r, self.a_s, self.a_r, self.b_s, self.b_r, self.z_s, self.z_r,
            self.zg_s, self.zg_r, self.bg_s, self.bg_r, self.ag_s, self.ag_r, self.cg_s, self.cg_r, self.out_s,
        ) = sems
        s, b = lax.axis_index("seq"), lax.axis_index("batch")
        self.core, self.z = lax.rem(s, 2), lax.div(s, 2)
        self.x, self.y = lax.rem(b, 2), lax.div(b, 2)
        self.core_peer = (s + 1 - 2 * self.core, b)
        x_peer = (s, b + 1 - 2 * self.x)
        y_peer = (s, b + 2 - 4 * self.y)
        self.first_peer, self.second_peer = (x_peer, y_peer), (y_peer, x_peer)
        self.z_to = [(lax.rem(self.z + d, 4) * 2 + self.core, b) for d in (1, 2, 3)]
        self.z_of = [lax.rem(self.z + d, 4) for d in (1, 2, 3)]
        self.first, self.second = (self.x, self.y), (self.y, self.x)
        self.half = acc.shape[1] // 2
        self.own = self.core * self.half
        self.cols = (slice(0, 256), slice(256, 512))
        self.vec_peers = [
            self.core_peer,
            x_peer,
            y_peer,
            (s + 2 - 4 * lax.rem(self.z, 2), b),
            (s + 4 - 8 * lax.div(self.z, 2), b),
        ]

    def peers(self):
        return [self.core_peer, self.first_peer[0], self.first_peer[1]] + self.z_to

    def rows(self, base, count):
        return pl.ds(pl.multiple_of(base, 16), count)

    def core_copy(self, c):
        r = lax.rem(c, RING)
        away = self.rows((1 - self.core) * self.half, self.half)
        return remote(self.acc.at[r, away], self.core_in.at[r], self.c_s.at[r], self.c_r.at[r], self.core_peer)

    def copy1(self, c, h):
        r = lax.rem(c, RING)
        at = (r, slice(None), self.cols[h])
        return remote(self.send1.at[at], self.recv1.at[at], self.a_s.at[r, h], self.a_r.at[r, h], self.first_peer[h])

    def copy2(self, c, h):
        r = lax.rem(c, RING)
        at = (r, slice(None), self.cols[h])
        return remote(self.send2.at[at], self.recv2.at[at], self.b_s.at[r, h], self.b_r.at[r, h], self.second_peer[h])

    def copy3(self, c, d):
        r = lax.rem(c, RING)
        return remote(self.send3.at[r, d], self.recv3.at[r, d], self.z_s.at[r, d], self.z_r.at[r, d], self.z_to[d])

    def base1(self, h):
        return self.own + self.first[h] * 128

    def base2(self, h):
        return self.base1(h) + self.second[h] * 64

    def spread_z(self, c, d, h):
        r = lax.rem(c, RING)
        land = self.res.at[c, self.rows(self.base2(h) + self.z * 16, 16), self.cols[h]]
        return remote(
            self.fin.at[r, :, self.cols[h]], land, self.zg_s.at[r, d, h], self.zg_r.at[r, d, h], self.z_to[d]
        )

    def spread_same(self, c, base, count, cols, s, r, peer):
        part = self.res.at[c, self.rows(base, count), cols]
        return remote(part, part, s, r, peer)

    def spread2(self, c, h):
        r = lax.rem(c, RING)
        return self.spread_same(
            c, self.base2(h), 64, self.cols[h], self.bg_s.at[r, h], self.bg_r.at[r, h], self.second_peer[h]
        )

    def spread1(self, c, h):
        r = lax.rem(c, RING)
        return self.spread_same(
            c, self.base1(h), 128, self.cols[h], self.ag_s.at[r, h], self.ag_r.at[r, h], self.first_peer[h]
        )

    def spread_core(self, c):
        r = lax.rem(c, RING)
        return self.spread_same(
            c, self.own, self.half, slice(0, 512), self.cg_s.at[r], self.cg_r.at[r], self.core_peer
        )

    def write_out(self, c, act):
        up_out, down_out, conv_out = self.res_out
        width, tiles = self.acc.shape[1], up_out.shape[1] // self.acc.shape[1]
        wide = lambda i: pl.ds(pl.multiple_of(i * width, width), width)

        def copy(to):
            return lambda: act(pltpu.make_async_copy(self.res.at[c], to, self.out_s.at[lax.rem(c, 2)]))

        pl.when(c < tiles)(copy(up_out.at[:, wide(c)]))
        pl.when((c >= tiles) & (c < 2 * tiles))(copy(down_out.at[wide(c - tiles), :]))
        pl.when(c >= 2 * tiles)(copy(conv_out.at[c - 2 * tiles]))

    def stage0(self, c):
        self.core_copy(c).start()

    def stage1(self, c):
        self.core_copy(c).wait()
        r = lax.rem(c, RING)
        for h in range(2):
            cols = self.cols[h]
            keep, give = self.first[h] * 128, (1 - self.first[h]) * 128
            self.send1[r, :, cols] = (
                self.acc[r, self.rows(self.own + give, 128), cols] + self.core_in[r, self.rows(give, 128), cols]
            ).astype(jnp.bfloat16)
            self.copy1(c, h).start()
            self.kept1[r, :, cols] = (
                self.acc[r, self.rows(self.own + keep, 128), cols] + self.core_in[r, self.rows(keep, 128), cols]
            )

    def stage2(self, c):
        r = lax.rem(c, RING)
        for h in range(2):
            self.copy1(c, h).wait()
            cols = self.cols[h]
            keep, give = self.second[h] * 64, (1 - self.second[h]) * 64
            self.send2[r, :, cols] = (
                self.kept1[r, self.rows(give, 64), cols]
                + self.recv1[r, self.rows(give, 64), cols].astype(jnp.float32)
            ).astype(jnp.bfloat16)
            self.copy2(c, h).start()
            self.kept2[r, :, cols] = self.kept1[r, self.rows(keep, 64), cols] + self.recv1[
                r, self.rows(keep, 64), cols
            ].astype(jnp.float32)

    def stage3(self, c):
        r = lax.rem(c, RING)
        for h in range(2):
            self.copy2(c, h).wait()
        for d in range(3):
            at = self.rows(self.z_of[d] * 16, 16)
            self.send3[r, d] = (self.kept2[r, at, :] + self.recv2[r, at, :].astype(jnp.float32)).astype(jnp.bfloat16)
            self.copy3(c, d).start()
        at = self.rows(self.z * 16, 16)
        self.kept3[r] = self.kept2[r, at, :] + self.recv2[r, at, :].astype(jnp.float32)

    def stage4(self, c):
        r = lax.rem(c, RING)
        total = self.kept3[r]
        for d in range(3):
            self.copy3(c, d).wait()
            total = total + self.recv3[r, d].astype(jnp.float32)
        total = total.astype(jnp.bfloat16)
        self.fin[r] = total
        for h in range(2):
            for d in range(3):
                self.spread_z(c, d, h).start()
            self.res[c, self.rows(self.base2(h) + self.z * 16, 16), self.cols[h]] = total[:, self.cols[h]]

    def stage5(self, c):
        for h in range(2):
            for d in range(3):
                self.spread_z(c, d, h).wait()
            self.spread2(c, h).start()

    def stage6(self, c):
        for h in range(2):
            self.spread2(c, h).wait()
            self.spread1(c, h).start()

    def stage7(self, c):
        for h in range(2):
            self.spread1(c, h).wait()
        self.spread_core(c).start()

    def stage8(self, c):
        self.spread_core(c).wait()

        @pl.when(c >= 2)
        def _():
            self.write_out(c - 2, lambda copy: copy.wait())

        self.write_out(c, lambda copy: copy.start())

    def tick(self, t):
        for stage in range(self.stages, -1, -1):
            c = t - stage

            @pl.when((c >= 0) & (c < self.count))
            def _():
                getattr(self, "stage%d" % stage)(c)

    def finish(self):
        for c in range(max(0, self.count - 2), self.count):
            self.write_out(jnp.int32(c), lambda copy: copy.wait())


def reduce_kernel(steps, *refs):
    (
        keeps, ffn, vec_in, ext_hbm, pre_hbm, pre_l, pre_r, mid_hbm, conv_w,
        grad_out, up_out, down_out, conv_out, vec_out,
        ext, pre, acc, res, pext, midb, gout, vsend, vrecv,
    ) = refs[:23]
    bufs = refs[23:34]
    sems = refs[34:51]
    load_s, ffn_s, in_s, gout_s, v_s, v_r = refs[51:]
    ffn_count = ffn.shape[0]
    count = ffn_count + KERNEL
    group, rows_here, width = gout.shape[1:]
    rows = group * rows_here
    red = Reducer(count, acc, res, (up_out, down_out, conv_out), bufs, sems)
    s = lax.axis_index("seq")
    last = lax.axis_size("seq") - 1

    barrier = pltpu.get_barrier_semaphore()
    for peer in red.peers():
        pl.semaphore_signal(barrier, inc=1, device_id=peer, device_id_type=MESH)

    load_ext = pltpu.make_async_copy(ext_hbm, ext, load_s.at[0])
    load_pre = pltpu.make_async_copy(pre_hbm, pre, load_s.at[1])

    def load_ffn(c):
        r = lax.rem(c, RING)
        return pltpu.make_async_copy(ffn.at[c], acc.at[r], ffn_s.at[r])

    def load_rows(i):
        slot = lax.rem(i, 2)
        at = pl.ds(i * group, group)
        return (
            pltpu.make_async_copy(pre_l.at[at], pext.at[slot, :, pl.ds(0, rows_here)], in_s.at[slot, 0]),
            pltpu.make_async_copy(pre_hbm.at[at], pext.at[slot, :, pl.ds(rows_here, rows_here)], in_s.at[slot, 1]),
            pltpu.make_async_copy(pre_r.at[at], pext.at[slot, :, pl.ds(2 * rows_here, rows_here)], in_s.at[slot, 2]),
            pltpu.make_async_copy(mid_hbm.at[at], midb.at[slot], in_s.at[slot, 3]),
        )

    def each_load(i, act):
        a, m, z, d = load_rows(i)
        pl.when(s > 0)(lambda: act(a))
        act(m)
        pl.when(s < last)(lambda: act(z))
        act(d)

    def store_rows(i):
        slot = lax.rem(i, 2)
        return pltpu.make_async_copy(gout.at[slot], grad_out.at[pl.ds(i * group, group)], gout_s.at[slot])

    load_ffn(0).start()
    each_load(0, lambda copy: copy.start())
    load_ext.start()
    load_pre.start()
    for side, at in ((s > 0, 0), (s < last, 2)):

        @pl.when(jnp.logical_not(side))
        def _():
            pext[:, :, at * rows_here : (at + 1) * rows_here, :] = jnp.zeros(
                (2, group, rows_here, width), jnp.bfloat16
            )

    pl.semaphore_wait(barrier, len(red.peers()))

    def vec_copy(q):
        return remote(vsend.at[q], vrecv.at[q], v_s.at[q], v_r.at[q], red.vec_peers[q])

    def row_block(i):
        each_load(i, lambda copy: copy.wait())

        @pl.when(i + 1 < steps)
        def _():
            each_load(i + 1, lambda copy: copy.start())

        slot = lax.rem(i, 2)
        grad = jnp.zeros((rows, width), jnp.float32)
        for tap in range(KERNEL):
            begin = (KERNEL - 1 - tap) * DILATION
            taken = pext[slot, :, begin : begin + rows_here, :].reshape(rows, width)
            grad = grad + dot_nt(taken, conv_w[tap])
        grad = grad.astype(jnp.bfloat16).astype(jnp.float32)
        grad = (grad + midb[slot].reshape(rows, width).astype(jnp.float32)).reshape(group, rows_here, width)

        @pl.when(i >= 2)
        def _():
            store_rows(i - 2).wait()

        for g in range(group):
            gout[slot, g] = (grad[g] * keeps[1, i * group + g]).astype(jnp.bfloat16)
        store_rows(i).start()

    def tap_grad(tap):
        r = lax.rem(ffn_count + tap, RING)
        begin = pl.multiple_of(tap * DILATION, DILATION)

        def part(i, first):
            at = pl.ds(i * 2 * group, 2 * group)
            taken = ext[at, pl.ds(begin, rows_here), :].reshape(2 * rows, width)
            grads = pre[at].reshape(2 * rows, width)
            value = dot_tn(taken, grads)
            acc[r] = value if first else acc[r] + value

        part(0, True)
        lax.fori_loop(1, steps // 2, lambda i, _: (part(i, False), 0)[1], 0)

    def tick(t, _):
        @pl.when(t < ffn_count)
        def _():
            load_ffn(t).wait()

        red.tick(t)
        for q in range(6):

            @pl.when(t == q)
            def _():
                if q == 0:
                    value = vec_in[...]
                else:
                    vec_copy(q - 1).wait()
                    value = vsend[q - 1] + vrecv[q - 1]
                if q < 5:
                    vsend[q] = value
                    vec_copy(q).start()
                else:
                    vec_out[...] = value

        @pl.when(t + 1 < ffn_count)
        def _():
            load_ffn(t + 1).start()

        @pl.when(t < steps)
        def _():
            row_block(t)

        @pl.when(t == ffn_count - 1)
        def _():
            load_ext.wait()
            load_pre.wait()

        tap = t + 1 - ffn_count

        @pl.when((tap >= 0) & (tap < KERNEL))
        def _():
            tap_grad(tap)

        return 0

    lax.fori_loop(0, count + red.stages, tick, 0)
    red.finish()
    for i in range(max(0, steps - 2), steps):
        store_rows(i).wait()


def reduce_all(keeps, ffn, vec, ext, pre, pre_l, pre_r, mid, conv_w):
    windows, rows_here, width = pre.shape
    group = TILE_ROWS // rows_here
    steps = windows // group
    count = ffn.shape[0] + KERNEL
    whole = pl.BlockSpec(memory_space=pltpu.VMEM)
    anywhere = pl.BlockSpec(memory_space=pl.ANY)
    dma = pltpu.SemaphoreType.DMA
    half = width // 2
    return pl.pallas_call(
        functools.partial(reduce_kernel, steps),
        in_specs=[pl.BlockSpec(memory_space=pltpu.SMEM), anywhere, whole] + [anywhere] * 5 + [whole],
        out_specs=[anywhere] * 4 + [whole],
        out_shape=[
            jax.ShapeDtypeStruct(pre.shape, jnp.bfloat16),
            jax.ShapeDtypeStruct((width, ffn.shape[0] // 2 * width), jnp.bfloat16),
            jax.ShapeDtypeStruct((ffn.shape[0] // 2 * width, width), jnp.bfloat16),
            jax.ShapeDtypeStruct((KERNEL, width, width), jnp.bfloat16),
            jax.ShapeDtypeStruct(vec.shape, jnp.float32),
        ],
        scratch_shapes=[
            pltpu.VMEM(ext.shape, jnp.bfloat16),
            pltpu.VMEM(pre.shape, jnp.bfloat16),
            pltpu.VMEM((RING, width, width), jnp.float32),
            pltpu.VMEM((count, width, width), jnp.bfloat16),
            pltpu.VMEM((2, group, 3 * rows_here, width), jnp.bfloat16),
            pltpu.VMEM((2, group, rows_here, width), jnp.bfloat16),
            pltpu.VMEM((2, group, rows_here, width), jnp.bfloat16),
            pltpu.VMEM((5,) + vec.shape, jnp.float32),
            pltpu.VMEM((5,) + vec.shape, jnp.float32),
            pltpu.VMEM((RING, half, width), jnp.float32),
            pltpu.VMEM((RING, half // 2, width), jnp.bfloat16),
            pltpu.VMEM((RING, half // 2, width), jnp.bfloat16),
            pltpu.VMEM((RING, half // 2, width), jnp.float32),
            pltpu.VMEM((RING, half // 4, width), jnp.bfloat16),
            pltpu.VMEM((RING, half // 4, width), jnp.bfloat16),
            pltpu.VMEM((RING, half // 4, width), jnp.float32),
            pltpu.VMEM((RING, 3, half // 16, width), jnp.bfloat16),
            pltpu.VMEM((RING, 3, half // 16, width), jnp.bfloat16),
            pltpu.VMEM((RING, half // 16, width), jnp.float32),
            pltpu.VMEM((RING, half // 16, width), jnp.bfloat16),
        ]
        + [
            dma((RING,)), dma((RING,)), dma((RING, 2)), dma((RING, 2)), dma((RING, 2)), dma((RING, 2)),
            dma((RING, 3)), dma((RING, 3)), dma((RING, 3, 2)), dma((RING, 3, 2)), dma((RING, 2)), dma((RING, 2)),
            dma((RING, 2)), dma((RING, 2)), dma((RING,)), dma((RING,)), dma((2,)),
        ]
        + [dma((2,)), dma((RING,)), dma((2, 4)), dma((2,)), dma((5,)), dma((5,))],
        compiler_params=pltpu.CompilerParams(
            vmem_limit_bytes=VMEM_BYTES, collective_id=1, has_side_effects=True
        ),
        name="reduce",
    )(keeps, ffn, vec, ext, pre, pre_l, pre_r, mid, conv_w)


def spread(shard, depth):
    return [
        shard if offset == 0 else passed_along(shard, "seq", offset)
        for offset in range(depth, -depth - 1, -1)
    ]


def per_device(
    block_input,
    window_lengths,
    conv_weight,
    conv_bias,
    norm1_gain,
    norm1_bias,
    up_weight,
    up_bias,
    down_weight,
    down_bias,
    norm2_gain,
    norm2_bias,
    out_cotangent,
):
    windows, rows_here, width = block_input.shape
    ff = up_weight.shape[1]
    depth = -(-REACH // rows_here)
    first = (lax.axis_index("seq") + jnp.arange(-depth, depth + 1, dtype=jnp.int32)) * rows_here
    keeps = (first[:, None] < window_lengths[None, :]).astype(jnp.float32)
    params = block_params(
        conv_weight, conv_bias, norm1_gain, norm1_bias, up_weight, up_bias, down_weight, down_bias, norm2_gain, norm2_bias
    )
    tiles = ff // FF_TILE
    if (lax.axis_size("seq"), lax.axis_size("batch"), rows_here) == (8, 4, REACH):
        out, ext, pre_low, mid_low, pre_l, pre_r, d_ffn, d_vec = blocks_halo(keeps, block_input, out_cotangent, params)
        input_grad, d_up, d_down, d_conv, d_vec = reduce_all(
            keeps, d_ffn, d_vec, ext, pre_low, pre_l, pre_r, mid_low, conv_weight
        )
        d_up, d_down, d_conv = (d.astype(jnp.float32) for d in (d_up, d_down, d_conv))
    else:
        parts = spread(block_input, depth)
        out, _, pre_low, mid_low, d_ffn, d_vec = blocks(keeps, parts, out_cotangent, params)
        input_grad, d_conv = conv_back(keeps, spread(pre_low, depth), block_input, mid_low, conv_weight)
        d_ffn, d_conv, d_vec = lax.psum((d_ffn, d_conv, d_vec), ("seq", "batch"))
        d_up = d_ffn[:tiles].transpose(1, 0, 2).reshape(width, ff)
        d_down = d_ffn[tiles:].reshape(ff, width)
    return (
        out,
        input_grad,
        d_conv,
        d_vec[5],
        d_vec[3],
        d_vec[4],
        d_up,
        d_vec[8 : 8 + tiles].reshape(ff),
        d_down,
        d_vec[2],
        d_vec[0],
        d_vec[1],
    )


def solution(mesh):
    rows = P("batch", "seq", None)
    return jax.shard_map(
        per_device,
        mesh=mesh,
        in_specs=(rows, P("batch")) + (P(),) * 10 + (rows,),
        out_specs=(rows, rows) + (P(),) * 10,
        check_vma=False,
    )
```

```python
import functools
import math

import jax
import jax.numpy as jnp
from jax import lax
from jax.experimental import pallas as pl
from jax.experimental.pallas import tpu as pltpu
from jax.sharding import PartitionSpec as P

KERNEL = 9
DILATION = 32
REACH = DILATION * (KERNEL // 2)
TILE_ROWS = 512
FF_TILE = 512
EPS = 1e-05
VMEM_BYTES = 63 * 2**20
MESH = pl.DeviceIdType.MESH
RING = 4
EARLY = 4
AHEAD = 3


def passed_along(shard, axis, by):
    size = lax.axis_size(axis)
    pairs = [(i, i + by) for i in range(size) if 0 <= i + by < size]
    return lax.ppermute(shard, axis, pairs)


def product(left, right, over_left, over_right):
    return lax.dot_general(
        left, right, (((over_left,), (over_right,)), ((), ())), preferred_element_type=jnp.float32
    )


def dot(left, right):
    return product(left, right, 1, 0)


def dot_nt(left, right):
    return product(left, right, 1, 1)


def dot_tn(left, right):
    return product(left, right, 0, 0)


def gelu_parts(values):
    cumulative = 0.5 + 0.5 * lax.erf(values * (1.0 / math.sqrt(2.0)))
    density = jnp.exp(-0.5 * values * values) * (1.0 / math.sqrt(2.0 * math.pi))
    return values * cumulative, cumulative + values * density


def normalize(values):
    center = jnp.mean(values, axis=-1, keepdims=True)
    centered = values - center
    inverse = lax.rsqrt(jnp.mean(centered * centered, axis=-1, keepdims=True) + EPS)
    return centered * inverse, inverse


def normalize_back(upstream, normed, inverse, gain):
    inner = upstream * gain
    return inverse * (
        inner
        - jnp.mean(inner, axis=-1, keepdims=True)
        - normed * jnp.mean(inner * normed, axis=-1, keepdims=True)
    )


def col_sum(values):
    return jnp.sum(values, axis=0, keepdims=True)


def remote(src, dst, send_sem, recv_sem, device):
    return pltpu.make_async_remote_copy(
        src_ref=src,
        dst_ref=dst,
        send_sem=send_sem,
        recv_sem=recv_sem,
        device_id=device,
        device_id_type=MESH,
    )


def block_compute(step, depth, keeps, parts, refs):
    (
        cot,
        conv_w,
        conv_b,
        gain1,
        bias1,
        up_w,
        up_b,
        down_w,
        down_b,
        gain2,
        bias2,
        out,
        ext,
        pre_out,
        mid_out,
        hidden,
        upper_out,
        lower_out,
        middle_out,
        d_vec,
        slope,
    ) = refs
    pieces = 2 * depth + 1
    group, rows_here, width = cot.shape
    rows = group * rows_here
    ff = up_w.shape[1]
    tile = min(FF_TILE, ff)
    tiles = ff // tile
    base = depth * rows_here - REACH

    @pl.when(step == 0)
    def _():
        d_vec[...] = jnp.zeros_like(d_vec)

    keep_here = []
    for g in range(group):
        window = step * group + g
        for i in range(pieces):
            keep = keeps[i, window]
            if i == depth:
                keep_here.append(keep)
            ext[g, i * rows_here : (i + 1) * rows_here, :] = parts[i][g] * keep.astype(jnp.bfloat16)

    pre = jnp.broadcast_to(conv_b[...], (rows, width))
    for tap in range(KERNEL):
        begin = base + tap * DILATION
        taken = ext[:, begin : begin + rows_here, :].reshape(rows, width)
        pre = pre + dot(taken, conv_w[tap])
    act, slope1 = gelu_parts(pre)
    n1, s1 = normalize(act)
    branch = (n1 * gain1[...] + bias1[...]).astype(jnp.bfloat16)
    start = ext[:, depth * rows_here : (depth + 1) * rows_here, :].reshape(rows, width)
    middle = start.astype(jnp.float32) + branch.astype(jnp.float32)
    middle_low = middle.astype(jnp.bfloat16)
    middle_out[...] = middle_low

    lower = jnp.broadcast_to(down_b[...], (rows, width))
    for j in range(tiles):
        cols = slice(j * tile, (j + 1) * tile)
        upper = dot(middle_low, up_w[:, cols]) + up_b[:, cols]
        h, sl = gelu_parts(upper)
        h = h.astype(jnp.bfloat16)
        hidden[:, cols] = h
        slope[:, cols] = sl
        lower = lower + dot(h, down_w[cols, :])
    n2, s2 = normalize(lower)
    shaped = (n2 * gain2[...] + bias2[...] + middle).reshape(group, rows_here, width)
    incoming = []
    for g in range(group):
        out[g] = (shaped[g] * keep_here[g]).astype(jnp.bfloat16)
        incoming.append(cot[g].astype(jnp.float32) * keep_here[g])
    incoming = jnp.concatenate(incoming, axis=0)
    d_vec[0:1, :] += col_sum(incoming * n2)
    d_vec[1:2, :] += col_sum(incoming)
    lower_low = normalize_back(incoming, n2, s2, gain2[...]).astype(jnp.bfloat16)
    lower_out[...] = lower_low
    d_vec[2:3, :] += col_sum(lower_low.astype(jnp.float32))
    middle_grad = incoming
    for j in range(tiles):
        cols = slice(j * tile, (j + 1) * tile)
        hidden_grad = dot_nt(lower_low, down_w[cols, :])
        upper_low = (hidden_grad * slope[:, cols]).astype(jnp.bfloat16)
        d_vec[8 + j : 9 + j, :] += col_sum(upper_low.astype(jnp.float32))
        upper_out[:, cols] = upper_low
        middle_grad = middle_grad + dot_nt(upper_low, up_w[:, cols])
    branch_low = middle_grad.astype(jnp.bfloat16)
    mid_out[...] = branch_low.reshape(group, rows_here, width)
    branch_grad = branch_low.astype(jnp.float32)
    d_vec[3:4, :] += col_sum(branch_grad * n1)
    d_vec[4:5, :] += col_sum(branch_grad)
    pre_low = (normalize_back(branch_grad, n1, s1, gain1[...]) * slope1).astype(jnp.bfloat16)
    d_vec[5:6, :] += col_sum(pre_low.astype(jnp.float32))
    pre_low = pre_low.reshape(group, rows_here, width)
    pre_out[...] = pre_low
    return pre_low


def block_kernel(depth, *refs):
    pieces = 2 * depth + 1
    block_compute(pl.program_id(0), depth, refs[0], refs[1 : 1 + pieces], refs[1 + pieces :])


def interleave(units, pieces):
    done = 0
    for n, unit in enumerate(units):
        unit()
        upto = (n + 1) * len(pieces) // len(units)
        for piece in pieces[done:upto]:
            piece()
        done = upto
    for piece in pieces[done:]:
        piece()


def halves(count, size=256):
    return [slice(k * size, (k + 1) * size) for k in range(count // size)]


def rows_in_eights(values):
    return jnp.sum(values.reshape(-1, 8, values.shape[-1]), axis=0)


def block_halo_kernel(blocks, *refs):
    (
        keeps, x_hbm, x_mid, cot, conv_w, conv_b, gain1, bias1, up_w, up_b, down_w, down_b, gain2, bias2,
        out_hbm, ext_hbm, pre_hbm, mid_hbm, hidden_hbm, upper_hbm, lower_hbm, middle_hbm, pre_l, pre_r, d_vec,
        out, ext, mid_out, hidden, upper_out, lower_out,
        slope, conv_acc, n1_all, q1_all, middle, middle_low, lower, mid_grad, vec_acc, upb_acc,
        from_l, from_r, pre_keep, fs, fr, bs, br, ps,
    ) = refs
    group, rows_here, width = cot.shape
    rows = group * rows_here
    ff = up_w.shape[1]
    fine, side_tile = 16, 256
    per_side = side_tile // rows_here
    step = pl.program_id(0)
    s = lax.axis_index("seq")
    b = lax.axis_index("batch")
    last = lax.axis_size("seq") - 1
    has = (s > 0, s < last)
    other = ((s - 1, b), (s + 1, b))

    core = lax.rem(s, 2)

    def near_first(act):
        for side in range(2):
            pl.when(has[1 - side] & (core == 0))(lambda side=1 - side: act(side))
            pl.when(has[side] & (core == 1))(lambda side=side: act(side))

    def place(i, part):
        if part is None:
            return pl.ds(i * group, group), i + 1
        return pl.ds(part * (group // 2), group // 2), part

    def halo(i, side, part=None):
        at, k = place(i, part)
        land = (from_r, from_l)[side]
        return remote(x_hbm.at[at], land.at[at], fs.at[k, side], fr.at[k, side], other[side])

    def halo_in(i, side, part=None):
        at, k = place(i, part)
        land = (from_l, from_r)[side]
        return remote(x_hbm.at[at], land.at[at], fs.at[k, side], fr.at[k, 1 - side], other[side])

    def put(k, block):
        at = pl.ds(block * group, group)
        flat = pl.ds(block * rows, rows)
        source, target = (
            lambda: (ext, ext_hbm.at[at]),
            lambda: (hidden, hidden_hbm.at[flat]),
            lambda: (pre_keep.at[lax.rem(block, 2)], pre_hbm.at[at]),
            lambda: (mid_out, mid_hbm.at[at]),
            lambda: (out, out_hbm.at[at]),
            lambda: (lower_out, lower_hbm.at[flat]),
            lambda: (upper_out, upper_hbm.at[flat]),
            lambda: (middle_low, middle_hbm.at[flat]),
        )[k]()
        return pltpu.make_async_copy(source, target, ps.at[k])

    def puts(start, *pairs):
        for k, block in pairs:

            @pl.when((block >= 0) & (block < blocks))
            def _():
                if start:
                    put(k, block).start()
                else:
                    put(k, block).wait()

    def back(i, side):
        at = pl.ds(i * group, group)
        land = (pre_r, pre_l)[side]
        return remote(pre_keep.at[lax.rem(i, 2)], land.at[at], bs.at[i, side], br.at[i, side], other[side])

    def back_in(i, side):
        at = pl.ds(i * group, group)
        land = (pre_l, pre_r)[side]
        return remote(pre_keep.at[lax.rem(i, 2)], land.at[at], bs.at[i, side], br.at[i, 1 - side], other[side])

    conv_slot = lax.rem(step, 2)
    back_slot = lax.rem(step, 2)
    keep_slot = lax.rem(step, 2)
    fine_rows = [slice(k * fine, (k + 1) * fine) for k in range(rows // fine)]
    sides = halves(rows)
    tiles = halves(ff)
    outs = halves(width)

    def add_vec(k, values):
        vec_acc[k] += rows_in_eights(values)

    def build_ext(w):
        parts = (from_l, x_mid, from_r)

        def piece():
            for k in range(3):
                keep = keeps[k, step * group + w].astype(jnp.bfloat16)
                rows_of = x_mid[w] if k == 1 else parts[k][step * group + w]
                ext[w, k * rows_here : (k + 1) * rows_here, :] = rows_of * keep

        return piece

    def conv_units():
        units = []
        for m, side in enumerate(sides):
            for cols in outs:
                held = {}

                def unit(tap, m=m, side=side, cols=cols, held=held):
                    def run():
                        begin = tap * DILATION
                        taken = ext[m * per_side : (m + 1) * per_side, begin : begin + rows_here, :]
                        value = dot(taken.reshape(side_tile, width), conv_w[tap, :, cols])
                        held["acc"] = value if tap == 0 else held["acc"] + value
                        if tap == KERNEL - 1:
                            conv_acc[side, cols] = held["acc"]

                    return run

                units += [unit(tap) for tap in range(KERNEL)]
        return units

    def first_norm(r):
        def piece():
            act, slope1 = gelu_parts(conv_acc[r, :] + conv_b[...])
            n1, s1 = normalize(act)
            branch = (n1 * gain1[...] + bias1[...]).astype(jnp.bfloat16)
            w, at = r.start // rows_here, r.start % rows_here
            start = ext[w, rows_here + at : rows_here + at + fine, :]
            value = start.astype(jnp.float32) + branch.astype(jnp.float32)
            middle[r, :] = value
            low = value.astype(jnp.bfloat16)
            middle_low[r, :] = low
            n1_all[conv_slot, r, :] = n1
            q1_all[conv_slot, r, :] = s1 * slope1

        return piece

    def forward_slots(extra):
        ups, lowers = {}, {}

        def up(j, m):
            def run():
                ups[j, m] = dot(middle_low[sides[m], :], up_w[:, tiles[j]])

            return run

        def act(j, m, k):
            def run():
                at = slice(k * 64, (k + 1) * 64)
                r = slice(m * side_tile + k * 64, m * side_tile + (k + 1) * 64)
                h, sl = gelu_parts(ups[j, m][at] + up_b[:, tiles[j]])
                hidden[r, tiles[j]] = h.astype(jnp.bfloat16)
                slope[r, tiles[j]] = sl

            return run

        def down(j, m, n):
            def run():
                value = dot(hidden[sides[m], tiles[j]], down_w[tiles[j], outs[n]])
                lowers[m, n] = lowers[m, n] + value if j > 0 else value
                if j == len(tiles) - 1:
                    lower[sides[m], outs[n]] = lowers[m, n]

            return run

        count = len(tiles)
        for m in range(len(sides)):
            up(0, m)()
        taken = 0
        for j in range(count + 1):
            units, pieces = [], []
            if j >= 1:
                units += [down(j - 1, m, n) for m in range(len(sides)) for n in range(len(outs))]
            if j + 1 < count:
                units += [up(j + 1, m) for m in range(len(sides))]
            if j < count:
                pieces += [act(j, m, k) for m in range(len(sides)) for k in range(side_tile // 64)]
            upto = len(extra) * (j + 1) // (count + 1)
            pieces += extra[taken:upto]
            taken = upto
            interleave(units, pieces)

    def second_norm(r):
        def piece():
            w, at = r.start // rows_here, r.start % rows_here
            window = pl.ds(at, fine)
            keep = keeps[1, jnp.maximum(step - 1, 0) * group + w]
            n2, s2 = normalize(lower[r, :] + down_b[...])
            value = middle[r, :] + (n2 * gain2[...] + bias2[...])
            out[w, window, :] = (value * keep).astype(jnp.bfloat16)
            incoming = cot[w, window, :].astype(jnp.float32) * keep
            low = normalize_back(incoming, n2, s2, gain2[...]).astype(jnp.bfloat16)
            lower_out[r, :] = low
            mid_grad[r, :] = incoming
            add_vec(0, incoming * n2)
            add_vec(1, incoming)
            add_vec(2, low.astype(jnp.float32))

        return piece

    def backward_slots(extra):
        hids, mids = {}, {}

        def hid(j, m):
            def run():
                hids[j, m] = dot_nt(lower_out[sides[m], :], down_w[tiles[j], :])

            return run

        def act(j, m, k):
            def run():
                at = slice(k * 64, (k + 1) * 64)
                r = slice(m * side_tile + k * 64, m * side_tile + (k + 1) * 64)
                low = (hids[j, m][at] * slope[r, tiles[j]]).astype(jnp.bfloat16)
                upper_out[r, tiles[j]] = low
                upb_acc[:, tiles[j]] += rows_in_eights(low.astype(jnp.float32))

            return run

        def mid(j, m, n):
            def run():
                value = dot_nt(upper_out[sides[m], tiles[j]], up_w[outs[n], tiles[j]])
                mids[m, n] = mids[m, n] + value if j > 0 else value
                if j == len(tiles) - 1:
                    mid_grad[sides[m], outs[n]] += mids[m, n]

            return run

        count = len(tiles)
        for m in range(len(sides)):
            hid(0, m)()
        taken = 0
        for j in range(count + 1):
            units, pieces = [], []
            if j >= 1:
                units += [mid(j - 1, m, n) for m in range(len(sides)) for n in range(len(outs))]
            if j + 1 < count:
                units += [hid(j + 1, m) for m in range(len(sides))]
            if j < count:
                pieces += [act(j, m, k) for m in range(len(sides)) for k in range(side_tile // 64)]
            upto = len(extra) * (j + 1) // (count + 1)
            pieces += extra[taken:upto]
            taken = upto
            interleave(units, pieces)

    def first_back(r):
        def piece():
            w, at = r.start // rows_here, r.start % rows_here
            window = pl.ds(at, fine)
            low = mid_grad[r, :].astype(jnp.bfloat16)
            mid_out[w, window, :] = low
            grad = low.astype(jnp.float32)
            n1 = n1_all[back_slot, r, :]
            add_vec(3, grad * n1)
            add_vec(4, grad)
            pre_low = normalize_back(grad, n1, q1_all[back_slot, r, :], gain1[...]).astype(jnp.bfloat16)
            pre_keep[keep_slot, w, window, :] = pre_low
            add_vec(5, pre_low.astype(jnp.float32))

        return piece

    @pl.when(step == 0)
    def _():
        barrier = pltpu.get_barrier_semaphore()
        for side in range(2):

            @pl.when(has[side])
            def _():
                pl.semaphore_signal(barrier, inc=1, device_id=other[side], device_id_type=MESH)

        vec_acc[...] = jnp.zeros_like(vec_acc)
        upb_acc[...] = jnp.zeros_like(upb_acc)
        mid_grad[...] = jnp.zeros_like(mid_grad)
        n1_all[...] = jnp.zeros_like(n1_all)
        q1_all[...] = jnp.zeros_like(q1_all)
        pl.semaphore_wait(barrier, (s > 0).astype(jnp.int32) + (s < last).astype(jnp.int32))
        near_first(lambda side: halo(0, side, 0).start())
        near_first(lambda side: halo(0, side, 1).start())
        for i in range(1, AHEAD):
            near_first(lambda side: halo(i, side).start())
        for side in range(2):

            @pl.when(jnp.logical_not(has[side]))
            def _():
                land = (from_l, from_r)[side]
                land[...] = jnp.zeros_like(land)

    @pl.when(step + AHEAD < blocks)
    def _():
        near_first(lambda side: halo(step + AHEAD, side).start())

    for side in range(2):

        @pl.when(has[side] & (step > 0) & (step < blocks))
        def _():
            halo_in(step, side).wait_recv()

        @pl.when(has[side] & (step >= 4) & (step - 4 < EARLY))
        def _():
            back(step - 4, side).wait_send()

    puts(False, (0, step - 1), (1, step - 2), (2, step - 3), (3, step - 3))

    @pl.when((step > 0) & (step < blocks))
    def _():
        forward_slots([build_ext(w) for w in range(group)] + [first_back(r) for r in fine_rows])
        puts(True, (0, step), (1, step - 1), (2, step - 2), (3, step - 2))
        near_first(lambda side: pl.when((step >= 2) & (step - 2 < EARLY))(lambda: back(step - 2, side).start()))
        puts(False, (4, step - 2), (5, step - 2))
        interleave(conv_units(), [second_norm(r) for r in fine_rows])
        puts(True, (4, step - 1), (5, step - 1))
        puts(False, (6, step - 2), (7, step - 1))
        backward_slots([first_norm(r) for r in fine_rows])
        puts(True, (6, step - 1), (7, step))

    @pl.when(step == 0)
    def _():
        units = conv_units()
        for part in range(2):
            for side in range(2):
                pl.when(has[side])(lambda: halo_in(0, side, part).wait_recv())
            for w in range(part * per_side, (part + 1) * per_side):
                build_ext(w)()
            half = len(units) // 2
            pieces = [first_norm(r) for r in fine_rows[: len(fine_rows) // 2]] if part else []
            interleave(units[part * half : (part + 1) * half], pieces)
        for r in fine_rows[len(fine_rows) // 2 :]:
            first_norm(r)()
        puts(True, (0, step), (7, step))

    @pl.when(step == blocks)
    def _():
        forward_slots([first_back(r) for r in fine_rows])
        puts(True, (1, step - 1), (2, step - 2), (3, step - 2))
        puts(False, (4, step - 2), (5, step - 2))
        for r in fine_rows:
            second_norm(r)()
        puts(True, (4, step - 1), (5, step - 1))
        puts(False, (6, step - 2), (7, step - 1))
        backward_slots([])
        puts(True, (6, step - 1))

    @pl.when(step == blocks + 1)
    def _():
        for r in fine_rows:
            first_back(r)()
        puts(True, (2, step - 2), (3, step - 2))
        puts(False, (4, step - 2), (5, step - 2), (6, step - 2))

    @pl.when(step == blocks + 1)
    def _():
        for k in range(6):
            d_vec[k : k + 1, :] = col_sum(vec_acc[k])
        d_vec[6:8, :] = jnp.zeros((2, width), jnp.float32)
        for k in range(ff // width):
            d_vec[8 + k : 9 + k, :] = col_sum(upb_acc[:, k * width : (k + 1) * width])
        for k in range(8 + ff // width, d_vec.shape[0]):
            d_vec[k : k + 1, :] = jnp.zeros((1, width), jnp.float32)
        put(2, blocks - 1).wait()
        put(3, blocks - 1).wait()
        for side in range(2):

            @pl.when(has[side])
            def _():
                for part in range(2):
                    halo(0, side, part).wait_send()
                for i in range(1, blocks):
                    halo(i, side).wait_send()
                for i in range(EARLY):
                    back_in(i, side).wait_recv()


def block_params(conv_w, conv_b, gain1, bias1, up_w, up_b, down_w, down_b, gain2, bias2):
    row = lambda v: v.reshape(1, -1)
    return [conv_w, row(conv_b), row(gain1), row(bias1), up_w, row(up_b), down_w, row(down_b), row(gain2), row(bias2)]


def flat_specs(rows, ff, width):
    return [pl.BlockSpec((rows, w), lambda i: (i, 0)) for w in (ff, ff, width, width)]


def flat_shapes(rows, ff, width):
    return [jax.ShapeDtypeStruct((rows, w), jnp.bfloat16) for w in (ff, ff, width, width)]


def blocks_halo(keeps, x, cot, params):
    windows, rows_here, width = cot.shape
    ff = params[4].shape[1]
    group = TILE_ROWS // rows_here
    count = windows // group
    rows = group * rows_here

    def late(by):
        return lambda i: jnp.clip(i - by, 0, count - 1)

    def tile(by):
        return pl.BlockSpec((group, rows_here, width), lambda i: (late(by)(i), 0, 0))

    whole = pl.BlockSpec(memory_space=pltpu.VMEM)
    anywhere = pl.BlockSpec(memory_space=pl.ANY)
    like = jax.ShapeDtypeStruct(cot.shape, jnp.bfloat16)
    square = pltpu.VMEM((rows, width), jnp.float32)
    block = pltpu.VMEM((group, rows_here, width), jnp.bfloat16)
    dma = pltpu.SemaphoreType.DMA((count + 1, 2))
    return pl.pallas_call(
        functools.partial(block_halo_kernel, count),
        grid=(count + 2,),
        in_specs=[pl.BlockSpec(memory_space=pltpu.SMEM), anywhere, tile(0), tile(1)] + [whole] * len(params),
        out_specs=[anywhere] * 10 + [whole],
        out_shape=[like, jax.ShapeDtypeStruct((windows, 3 * rows_here, width), jnp.bfloat16), like, like]
        + flat_shapes(windows * rows_here, ff, width)
        + [like, like, jax.ShapeDtypeStruct((16, width), jnp.float32)],
        scratch_shapes=[
            block,
            pltpu.VMEM((group, 3 * rows_here, width), jnp.bfloat16),
            block,
            pltpu.VMEM((rows, ff), jnp.bfloat16),
            pltpu.VMEM((rows, ff), jnp.bfloat16),
            pltpu.VMEM((rows, width), jnp.bfloat16),
            pltpu.VMEM((rows, ff), jnp.float32),
            square,
            pltpu.VMEM((2, rows, width), jnp.float32),
            pltpu.VMEM((2, rows, width), jnp.float32),
            square,
            pltpu.VMEM((rows, width), jnp.bfloat16),
            square,
            square,
            pltpu.VMEM((6, 8, width), jnp.float32),
            pltpu.VMEM((8, ff), jnp.float32),
            pltpu.VMEM(cot.shape, jnp.bfloat16),
            pltpu.VMEM(cot.shape, jnp.bfloat16),
            pltpu.VMEM((2, group, rows_here, width), jnp.bfloat16),
            dma,
            dma,
            dma,
            dma,
            pltpu.SemaphoreType.DMA((8,)),
        ],
        compiler_params=pltpu.CompilerParams(
            vmem_limit_bytes=VMEM_BYTES, collective_id=0, has_side_effects=True
        ),
        name="block",
    )(keeps, x, x, cot, *params)


def blocks(keeps, parts, cot, params):
    windows, rows_here, width = cot.shape
    depth = len(parts) // 2
    ff = params[4].shape[1]
    group = max(1, TILE_ROWS // rows_here)
    rows = group * rows_here
    tile = pl.BlockSpec((group, rows_here, width), lambda i: (i, 0, 0))
    wide = pl.BlockSpec((group, (2 * depth + 1) * rows_here, width), lambda i: (i, 0, 0))
    whole = pl.BlockSpec(memory_space=pltpu.VMEM)
    like = jax.ShapeDtypeStruct(cot.shape, jnp.bfloat16)
    return pl.pallas_call(
        functools.partial(block_kernel, depth),
        grid=(windows // group,),
        in_specs=[pl.BlockSpec(memory_space=pltpu.SMEM)] + [tile] * (len(parts) + 1) + [whole] * len(params),
        out_specs=[tile, wide, tile, tile] + flat_specs(rows, ff, width) + [whole],
        out_shape=[like, jax.ShapeDtypeStruct((windows, (2 * depth + 1) * rows_here, width), jnp.bfloat16), like, like]
        + flat_shapes(windows * rows_here, ff, width)
        + [jax.ShapeDtypeStruct((16, width), jnp.float32)],
        scratch_shapes=[pltpu.VMEM((rows, ff), jnp.float32)],
        compiler_params=pltpu.CompilerParams(vmem_limit_bytes=VMEM_BYTES),
        name="block_general",
    )(keeps, *parts, cot, *params)


def back_kernel(depth, *refs):
    pieces = 2 * depth + 1
    keeps = refs[0]
    parts = refs[1 : 1 + pieces]
    start_in, mid_in, conv_w, out, d_conv, ext = refs[1 + pieces :]
    step = pl.program_id(0)
    group, rows_here, width = start_in.shape
    rows = group * rows_here
    base = depth * rows_here - REACH

    @pl.when(step == 0)
    def _():
        d_conv[...] = jnp.zeros_like(d_conv)

    start = []
    for g in range(group):
        start.append(start_in[g] * keeps[depth, step * group + g].astype(jnp.bfloat16))
        for i in range(pieces):
            ext[g, i * rows_here : (i + 1) * rows_here, :] = parts[i][g]
    start = jnp.concatenate(start, axis=0)
    grad = jnp.zeros((rows, width), jnp.float32)
    for tap in range(KERNEL):
        begin = base + (KERNEL - 1 - tap) * DILATION
        taken = ext[:, begin : begin + rows_here, :].reshape(rows, width)
        d_conv[tap] += dot_tn(start, taken)
        grad = grad + dot_nt(taken, conv_w[tap])
    grad = grad.astype(jnp.bfloat16).astype(jnp.float32) + mid_in[...].reshape(rows, width).astype(jnp.float32)
    grad = grad.reshape(group, rows_here, width)
    for g in range(group):
        out[g] = (grad[g] * keeps[depth, step * group + g]).astype(jnp.bfloat16)


def conv_back(keeps, parts, start, mid, conv_w):
    windows, rows_here, width = start.shape
    depth = len(parts) // 2
    group = max(1, TILE_ROWS // rows_here)
    tile = pl.BlockSpec((group, rows_here, width), lambda i: (i, 0, 0))
    whole = pl.BlockSpec(memory_space=pltpu.VMEM)
    return pl.pallas_call(
        functools.partial(back_kernel, depth),
        grid=(windows // group,),
        in_specs=[pl.BlockSpec(memory_space=pltpu.SMEM)] + [tile] * (len(parts) + 2) + [whole],
        out_specs=[tile, whole],
        out_shape=[
            jax.ShapeDtypeStruct(start.shape, jnp.bfloat16),
            jax.ShapeDtypeStruct((KERNEL, width, width), jnp.float32),
        ],
        scratch_shapes=[pltpu.VMEM((group, (2 * depth + 1) * rows_here, width), jnp.bfloat16)],
        compiler_params=pltpu.CompilerParams(vmem_limit_bytes=VMEM_BYTES),
        name="conv_back_general",
    )(keeps, *parts, start, mid, conv_w)


class Reducer:
    stages = 8
    gap = 2

    def __init__(self, count, acc, res, res_out, bufs, sems):
        self.count, self.acc, self.res, self.res_out = count, acc, res, res_out
        self.core_in, self.send1, self.recv1, self.kept1 = bufs[:4]
        self.send2, self.recv2, self.kept2 = bufs[4:7]
        self.send3, self.recv3, self.kept3, self.fin = bufs[7:11]
        (
            self.c_s, self.c_r, self.a_s, self.a_r, self.b_s, self.b_r, self.z_s, self.z_r,
            self.zg_s, self.zg_r, self.bg_s, self.bg_r, self.ag_s, self.ag_r, self.cg_s, self.cg_r, self.out_s,
        ) = sems
        s, b = lax.axis_index("seq"), lax.axis_index("batch")
        self.core, self.z = lax.rem(s, 2), lax.div(s, 2)
        self.x, self.y = lax.rem(b, 2), lax.div(b, 2)
        self.core_peer = (s + 1 - 2 * self.core, b)
        x_peer = (s, b + 1 - 2 * self.x)
        y_peer = (s, b + 2 - 4 * self.y)
        self.first_peer, self.second_peer = (x_peer, y_peer), (y_peer, x_peer)
        self.z_to = [(lax.rem(self.z + d, 4) * 2 + self.core, b) for d in (1, 2, 3)]
        self.z_of = [lax.rem(self.z + d, 4) for d in (1, 2, 3)]
        self.first, self.second = (self.x, self.y), (self.y, self.x)
        self.half = acc.shape[1] // 2
        self.own = self.core * self.half
        self.cols = (slice(0, 256), slice(256, 512))
        self.vec_peers = [
            self.core_peer,
            x_peer,
            y_peer,
            (s + 2 - 4 * lax.rem(self.z, 2), b),
            (s + 4 - 8 * lax.div(self.z, 2), b),
        ]

    def peers(self):
        return [self.core_peer, self.first_peer[0], self.first_peer[1]] + self.z_to

    def rows(self, base, count):
        return pl.ds(pl.multiple_of(base, 16), count)

    def core_copy(self, c):
        r = lax.rem(c, RING)
        away = self.rows((1 - self.core) * self.half, self.half)
        return remote(self.acc.at[r, away], self.core_in.at[r], self.c_s.at[r], self.c_r.at[r], self.core_peer)

    def copy1(self, c, h):
        r = lax.rem(c, RING)
        at = (r, slice(None), self.cols[h])
        return remote(self.send1.at[at], self.recv1.at[at], self.a_s.at[r, h], self.a_r.at[r, h], self.first_peer[h])

    def copy2(self, c, h):
        r = lax.rem(c, RING)
        at = (r, slice(None), self.cols[h])
        return remote(self.send2.at[at], self.recv2.at[at], self.b_s.at[r, h], self.b_r.at[r, h], self.second_peer[h])

    def copy3(self, c, d):
        r = lax.rem(c, RING)
        return remote(self.send3.at[r, d], self.recv3.at[r, d], self.z_s.at[r, d], self.z_r.at[r, d], self.z_to[d])

    def base1(self, h):
        return self.own + self.first[h] * 128

    def base2(self, h):
        return self.base1(h) + self.second[h] * 64

    def spread_z(self, c, d, h):
        r = lax.rem(c, RING)
        land = self.res.at[c, self.rows(self.base2(h) + self.z * 16, 16), self.cols[h]]
        return remote(
            self.fin.at[r, :, self.cols[h]], land, self.zg_s.at[r, d, h], self.zg_r.at[r, d, h], self.z_to[d]
        )

    def spread_same(self, c, base, count, cols, s, r, peer):
        part = self.res.at[c, self.rows(base, count), cols]
        return remote(part, part, s, r, peer)

    def spread2(self, c, h):
        r = lax.rem(c, RING)
        return self.spread_same(
            c, self.base2(h), 64, self.cols[h], self.bg_s.at[r, h], self.bg_r.at[r, h], self.second_peer[h]
        )

    def spread1(self, c, h):
        r = lax.rem(c, RING)
        return self.spread_same(
            c, self.base1(h), 128, self.cols[h], self.ag_s.at[r, h], self.ag_r.at[r, h], self.first_peer[h]
        )

    def spread_core(self, c):
        r = lax.rem(c, RING)
        return self.spread_same(
            c, self.own, self.half, slice(0, 512), self.cg_s.at[r], self.cg_r.at[r], self.core_peer
        )

    def write_out(self, c, act):
        up_out, down_out, conv_out = self.res_out
        width, tiles = self.acc.shape[1], up_out.shape[1] // self.acc.shape[1]
        wide = lambda i: pl.ds(pl.multiple_of(i * width, width), width)

        def copy(to):
            return lambda: act(pltpu.make_async_copy(self.res.at[c], to, self.out_s.at[lax.rem(c, 2)]))

        pl.when(c < tiles)(copy(up_out.at[:, wide(c)]))
        pl.when((c >= tiles) & (c < 2 * tiles))(copy(down_out.at[wide(c - tiles), :]))
        pl.when(c >= 2 * tiles)(copy(conv_out.at[c - 2 * tiles]))

    def stage0(self, c):
        self.core_copy(c).start()

    def stage1(self, c):
        self.core_copy(c).wait()
        r = lax.rem(c, RING)
        for h in range(2):
            cols = self.cols[h]
            keep, give = self.first[h] * 128, (1 - self.first[h]) * 128
            self.send1[r, :, cols] = (
                self.acc[r, self.rows(self.own + give, 128), cols] + self.core_in[r, self.rows(give, 128), cols]
            ).astype(jnp.bfloat16)
            self.copy1(c, h).start()
            self.kept1[r, :, cols] = (
                self.acc[r, self.rows(self.own + keep, 128), cols] + self.core_in[r, self.rows(keep, 128), cols]
            )

    def stage2(self, c):
        r = lax.rem(c, RING)
        for h in range(2):
            self.copy1(c, h).wait()
            cols = self.cols[h]
            keep, give = self.second[h] * 64, (1 - self.second[h]) * 64
            self.send2[r, :, cols] = (
                self.kept1[r, self.rows(give, 64), cols]
                + self.recv1[r, self.rows(give, 64), cols].astype(jnp.float32)
            ).astype(jnp.bfloat16)
            self.copy2(c, h).start()
            self.kept2[r, :, cols] = self.kept1[r, self.rows(keep, 64), cols] + self.recv1[
                r, self.rows(keep, 64), cols
            ].astype(jnp.float32)

    def stage3(self, c):
        r = lax.rem(c, RING)
        for h in range(2):
            self.copy2(c, h).wait()
        for d in range(3):
            at = self.rows(self.z_of[d] * 16, 16)
            self.send3[r, d] = (self.kept2[r, at, :] + self.recv2[r, at, :].astype(jnp.float32)).astype(jnp.bfloat16)
            self.copy3(c, d).start()
        at = self.rows(self.z * 16, 16)
        self.kept3[r] = self.kept2[r, at, :] + self.recv2[r, at, :].astype(jnp.float32)

    def stage4(self, c):
        r = lax.rem(c, RING)
        total = self.kept3[r]
        for d in range(3):
            self.copy3(c, d).wait()
            total = total + self.recv3[r, d].astype(jnp.float32)
        total = total.astype(jnp.bfloat16)
        self.fin[r] = total
        for h in range(2):
            for d in range(3):
                self.spread_z(c, d, h).start()
            self.res[c, self.rows(self.base2(h) + self.z * 16, 16), self.cols[h]] = total[:, self.cols[h]]

    def stage5(self, c):
        for h in range(2):
            for d in range(3):
                self.spread_z(c, d, h).wait()
            self.spread2(c, h).start()

    def stage6(self, c):
        for h in range(2):
            self.spread2(c, h).wait()
            self.spread1(c, h).start()

    def stage7(self, c):
        for h in range(2):
            self.spread1(c, h).wait()
        self.spread_core(c).start()

    def stage8(self, c):
        self.spread_core(c).wait()

        @pl.when(c >= 2)
        def _():
            self.write_out(c - 2, lambda copy: copy.wait())

        self.write_out(c, lambda copy: copy.start())

    def tick(self, t):
        for stage in range(self.stages, -1, -1):
            c = t - stage * self.gap

            @pl.when((c >= 0) & (c < self.count))
            def _():
                getattr(self, "stage%d" % stage)(c)

    def finish(self):
        for c in range(max(0, self.count - 2), self.count):
            self.write_out(jnp.int32(c), lambda copy: copy.wait())


def hidden_width(tiles):
    return tiles.shape[2]


def reduce_kernel(steps, *refs):
    (
        keeps, hidden, upper, lower_hbm, middle_hbm, vec_in, ext_hbm, pre_hbm, pre_l, pre_r, mid_hbm, conv_w,
        grad_out, up_out, down_out, conv_out, vec_out, late_l, late_r,
        ext, pre, lower, middle, tiles, acc, res, pext, midb, gout, vsend, vrecv,
    ) = refs[:31]
    bufs = refs[31:42]
    sems = refs[42:59]
    load_s, ffn_s, in_s, gout_s, v_s, v_r, late_s, late_q = refs[59:]
    ff_tiles = hidden.shape[1] // hidden_width(tiles)
    ffn_count = 2 * ff_tiles
    count = ffn_count + KERNEL
    group, rows_here, width = gout.shape[1:]
    rows = group * rows_here
    red = Reducer(count, acc, res, (up_out, down_out, conv_out), bufs, sems)
    s = lax.axis_index("seq")
    last = lax.axis_size("seq") - 1

    b = lax.axis_index("batch")
    has = (s > 0, s < last)
    other = ((s - 1, b), (s + 1, b))
    beyond = jnp.where(red.core == 0, s - 1, s + 1)
    has_beyond = (beyond >= 0) & (beyond <= last)

    barrier = pltpu.get_barrier_semaphore()
    for peer in red.peers():
        pl.semaphore_signal(barrier, inc=1, device_id=peer, device_id_type=MESH)

    @pl.when(has_beyond)
    def _():
        pl.semaphore_signal(barrier, inc=1, device_id=(beyond, b), device_id_type=MESH)

    def late(i, side):
        at = pl.ds((i - EARLY) * group, group)
        land = (late_r, late_l)[side]
        k = i - EARLY
        return remote(
            pre_hbm.at[pl.ds(i * group, group)], land.at[at], late_s.at[k, side], late_q.at[k, side], other[side]
        )

    def late_in(i, side):
        at = pl.ds((i - EARLY) * group, group)
        land = (late_l, late_r)[side]
        k = i - EARLY
        return remote(
            pre_hbm.at[pl.ds(i * group, group)], land.at[at], late_s.at[k, side], late_q.at[k, 1 - side], other[side]
        )

    load_ext = pltpu.make_async_copy(ext_hbm, ext, load_s.at[0])
    load_pre = pltpu.make_async_copy(pre_hbm, pre, load_s.at[1])

    load_lower = pltpu.make_async_copy(lower_hbm, lower, load_s.at[2])
    load_middle = pltpu.make_async_copy(middle_hbm, middle, load_s.at[3])
    tile_rows = tiles.shape[1]
    per_chunk = lower.shape[0] // tile_rows

    def load_tile(i, act):
        r = lax.rem(i, 2)
        c = lax.div(i, per_chunk)
        at = pl.ds(pl.multiple_of(lax.rem(i, per_chunk) * tile_rows, tile_rows), tile_rows)

        def copy(source, first):
            cols = pl.ds(pl.multiple_of((c - first) * width, width), width)
            return lambda: act(pltpu.make_async_copy(source.at[at, cols], tiles.at[r], ffn_s.at[r]))

        pl.when(c < ff_tiles)(copy(upper, 0))
        pl.when((c >= ff_tiles) & (c < ffn_count))(copy(hidden, ff_tiles))

    def ffn_grad(c):
        r = lax.rem(c, RING)

        def part(i):
            tile = c * per_chunk + i
            load_tile(tile, lambda copy: copy.wait())
            load_tile(tile + 1, lambda copy: copy.start())
            at = pl.ds(pl.multiple_of(i * tile_rows, tile_rows), tile_rows)
            slot = lax.rem(tile, 2)

            def add(value):
                @pl.when(i == 0)
                def _():
                    acc[r] = value

                @pl.when(i > 0)
                def _():
                    acc[r] += value

            pl.when(c < ff_tiles)(lambda: add(dot_tn(middle[at], tiles[slot])))
            pl.when(c >= ff_tiles)(lambda: add(dot_tn(tiles[slot], lower[at])))

        lax.fori_loop(0, per_chunk, lambda i, _: (part(i), 0)[1], 0)

    def each_load(i, act, fresh=False):
        slot = lax.rem(i, 2)
        at = pl.ds(i * group, group)
        at_late = pl.ds((i - EARLY) * group, group)
        for side, early_ref, late_ref in ((0, pre_l, late_l), (1, pre_r, late_r)):
            to = pext.at[slot, :, pl.ds(2 * side * rows_here, rows_here)]
            sem = in_s.at[slot, side]

            @pl.when(has[side] & (i < EARLY))
            def _():
                act(pltpu.make_async_copy(early_ref.at[at], to, sem))

            @pl.when(has[side] & (i >= EARLY))
            def _():
                if fresh:
                    late_in(i, side).wait_recv()
                act(pltpu.make_async_copy(late_ref.at[at_late], to, sem))

        act(pltpu.make_async_copy(pre_hbm.at[at], pext.at[slot, :, pl.ds(rows_here, rows_here)], in_s.at[slot, 2]))
        act(pltpu.make_async_copy(mid_hbm.at[at], midb.at[slot], in_s.at[slot, 3]))

    def store_rows(i):
        slot = lax.rem(i, 2)
        return pltpu.make_async_copy(gout.at[slot], grad_out.at[pl.ds(i * group, group)], gout_s.at[slot])

    load_middle.start()
    for i in range(1):
        load_tile(jnp.int32(i), lambda copy: copy.start())
    load_lower.start()
    load_ext.start()
    load_pre.start()
    each_load(0, lambda copy: copy.start())
    for side, at in ((s > 0, 0), (s < last, 2)):

        @pl.when(jnp.logical_not(side))
        def _():
            pext[:, :, at * rows_here : (at + 1) * rows_here, :] = jnp.zeros(
                (2, group, rows_here, width), jnp.bfloat16
            )

    pl.semaphore_wait(barrier, len(red.peers()) + has_beyond.astype(jnp.int32))
    for i in range(EARLY, steps):
        for side in range(2):
            pl.when(has[side])(lambda: late(i, side).start())

    def vec_copy(q):
        return remote(vsend.at[q], vrecv.at[q], v_s.at[q], v_r.at[q], red.vec_peers[q])

    def row_block(i):
        each_load(i, lambda copy: copy.wait())

        @pl.when(i + 1 < steps)
        def _():
            each_load(i + 1, lambda copy: copy.start(), True)

        slot = lax.rem(i, 2)
        grad = jnp.zeros((rows, width), jnp.float32)
        for tap in range(KERNEL):
            begin = (KERNEL - 1 - tap) * DILATION
            taken = pext[slot, :, begin : begin + rows_here, :].reshape(rows, width)
            grad = grad + dot_nt(taken, conv_w[tap])
        grad = grad.astype(jnp.bfloat16).astype(jnp.float32)
        grad = (grad + midb[slot].reshape(rows, width).astype(jnp.float32)).reshape(group, rows_here, width)

        @pl.when(i >= 2)
        def _():
            store_rows(i - 2).wait()

        for g in range(group):
            gout[slot, g] = (grad[g] * keeps[1, i * group + g]).astype(jnp.bfloat16)
        store_rows(i).start()

    def tap_grad(tap):
        r = lax.rem(ffn_count + tap, RING)
        begin = pl.multiple_of(tap * DILATION, DILATION)

        taken = ext[:, pl.ds(begin, rows_here), :].reshape(steps * rows, width)
        acc[r] = dot_tn(taken, pre[...].reshape(steps * rows, width))

    load_middle.wait()

    def tick(t, _):
        red.tick(t)
        for q in range(6):

            @pl.when(t == q)
            def _():
                if q == 0:
                    value = vec_in[...]
                else:
                    vec_copy(q - 1).wait()
                    value = vsend[q - 1] + vrecv[q - 1]
                if q < 5:
                    vsend[q] = value
                    vec_copy(q).start()
                else:
                    vec_out[...] = value

        chunk = t + 1

        @pl.when(chunk == ff_tiles)
        def _():
            load_lower.wait()

        @pl.when(chunk < ffn_count)
        def _():
            ffn_grad(chunk)

        @pl.when(chunk == ffn_count)
        def _():
            load_ext.wait()
            load_pre.wait()

        rest = t - (count - 1)

        @pl.when((rest >= 0) & (rest < steps))
        def _():
            row_block(rest)

        tap = chunk - ffn_count

        @pl.when((tap >= 0) & (tap < KERNEL))
        def _():
            tap_grad(tap)

        return 0

    lax.fori_loop(-1, count + red.stages * red.gap, tick, 0)
    red.finish()
    for i in range(EARLY, steps):
        for side in range(2):
            pl.when(has[side])(lambda: late(i, side).wait_send())
    for i in range(max(0, steps - 2), steps):
        store_rows(i).wait()


def reduce_all(keeps, hidden, upper, lower, middle, vec, ext, pre, pre_l, pre_r, mid, conv_w):
    windows, rows_here, width = pre.shape
    ff = hidden.shape[1]
    group = TILE_ROWS // rows_here
    steps = windows // group
    count = 2 * ff // width + KERNEL
    whole = pl.BlockSpec(memory_space=pltpu.VMEM)
    anywhere = pl.BlockSpec(memory_space=pl.ANY)
    dma = pltpu.SemaphoreType.DMA
    half = width // 2
    rows = group * rows_here
    return pl.pallas_call(
        functools.partial(reduce_kernel, steps),
        in_specs=[pl.BlockSpec(memory_space=pltpu.SMEM), anywhere, anywhere, anywhere, anywhere, whole] + [anywhere] * 5 + [whole],
        out_specs=[anywhere] * 4 + [whole, anywhere, anywhere],
        out_shape=[
            jax.ShapeDtypeStruct(pre.shape, jnp.bfloat16),
            jax.ShapeDtypeStruct((width, ff), jnp.bfloat16),
            jax.ShapeDtypeStruct((ff, width), jnp.bfloat16),
            jax.ShapeDtypeStruct((KERNEL, width, width), jnp.bfloat16),
            jax.ShapeDtypeStruct(vec.shape, jnp.float32),
        ]
        + [jax.ShapeDtypeStruct(((steps - EARLY) * group, rows_here, width), jnp.bfloat16)] * 2,
        scratch_shapes=[
            pltpu.VMEM(ext.shape, jnp.bfloat16),
            pltpu.VMEM(pre.shape, jnp.bfloat16),
            pltpu.VMEM(lower.shape, jnp.bfloat16),
            pltpu.VMEM(middle.shape, jnp.bfloat16),
            pltpu.VMEM((2, 4 * rows, width), jnp.bfloat16),
            pltpu.VMEM((RING, width, width), jnp.float32),
            pltpu.VMEM((count, width, width), jnp.bfloat16),
            pltpu.VMEM((2, group, 3 * rows_here, width), jnp.bfloat16),
            pltpu.VMEM((2, group, rows_here, width), jnp.bfloat16),
            pltpu.VMEM((2, group, rows_here, width), jnp.bfloat16),
            pltpu.VMEM((5,) + vec.shape, jnp.float32),
            pltpu.VMEM((5,) + vec.shape, jnp.float32),
            pltpu.VMEM((RING, half, width), jnp.float32),
            pltpu.VMEM((RING, half // 2, width), jnp.bfloat16),
            pltpu.VMEM((RING, half // 2, width), jnp.bfloat16),
            pltpu.VMEM((RING, half // 2, width), jnp.float32),
            pltpu.VMEM((RING, half // 4, width), jnp.bfloat16),
            pltpu.VMEM((RING, half // 4, width), jnp.bfloat16),
            pltpu.VMEM((RING, half // 4, width), jnp.float32),
            pltpu.VMEM((RING, 3, half // 16, width), jnp.bfloat16),
            pltpu.VMEM((RING, 3, half // 16, width), jnp.bfloat16),
            pltpu.VMEM((RING, half // 16, width), jnp.float32),
            pltpu.VMEM((RING, half // 16, width), jnp.bfloat16),
        ]
        + [
            dma((RING,)), dma((RING,)), dma((RING, 2)), dma((RING, 2)), dma((RING, 2)), dma((RING, 2)),
            dma((RING, 3)), dma((RING, 3)), dma((RING, 3, 2)), dma((RING, 3, 2)), dma((RING, 2)), dma((RING, 2)),
            dma((RING, 2)), dma((RING, 2)), dma((RING,)), dma((RING,)), dma((2,)),
        ]
        + [dma((4,)), dma((RING,)), dma((2, 4)), dma((2,)), dma((5,)), dma((5,))]
        + [dma((steps - EARLY, 2)), dma((steps - EARLY, 2))],
        compiler_params=pltpu.CompilerParams(
            vmem_limit_bytes=VMEM_BYTES, collective_id=1, has_side_effects=True
        ),
        name="reduce",
    )(keeps, hidden, upper, lower, middle, vec, ext, pre, pre_l, pre_r, mid, conv_w)


def spread(shard, depth):
    return [
        shard if offset == 0 else passed_along(shard, "seq", offset)
        for offset in range(depth, -depth - 1, -1)
    ]


def per_device(
    block_input,
    window_lengths,
    conv_weight,
    conv_bias,
    norm1_gain,
    norm1_bias,
    up_weight,
    up_bias,
    down_weight,
    down_bias,
    norm2_gain,
    norm2_bias,
    out_cotangent,
):
    windows, rows_here, width = block_input.shape
    ff = up_weight.shape[1]
    depth = -(-REACH // rows_here)
    first = (lax.axis_index("seq") + jnp.arange(-depth, depth + 1, dtype=jnp.int32)) * rows_here
    keeps = (first[:, None] < window_lengths[None, :]).astype(jnp.float32)
    params = block_params(
        conv_weight, conv_bias, norm1_gain, norm1_bias, up_weight, up_bias, down_weight, down_bias, norm2_gain, norm2_bias
    )
    tiles = ff // FF_TILE
    if (lax.axis_size("seq"), lax.axis_size("batch"), rows_here) == (8, 4, REACH):
        out, ext, pre_low, mid_low, hidden, upper, lower, middle, pre_l, pre_r, d_vec = blocks_halo(
            keeps, block_input, out_cotangent, params
        )
        input_grad, d_up, d_down, d_conv, d_vec, _, _ = reduce_all(
            keeps, hidden, upper, lower, middle, d_vec, ext, pre_low, pre_l, pre_r, mid_low, conv_weight
        )
        d_up, d_down, d_conv = (d.astype(jnp.float32) for d in (d_up, d_down, d_conv))
    else:
        parts = spread(block_input, depth)
        out, _, pre_low, mid_low, hidden, upper, lower, middle, d_vec = blocks(keeps, parts, out_cotangent, params)
        input_grad, d_conv = conv_back(keeps, spread(pre_low, depth), block_input, mid_low, conv_weight)
        d_up, d_down = dot_tn(middle, upper), dot_tn(hidden, lower)
        d_up, d_down, d_conv, d_vec = lax.psum((d_up, d_down, d_conv, d_vec), ("seq", "batch"))
    return (
        out,
        input_grad,
        d_conv,
        d_vec[5],
        d_vec[3],
        d_vec[4],
        d_up,
        d_vec[8 : 8 + tiles].reshape(ff),
        d_down,
        d_vec[2],
        d_vec[0],
        d_vec[1],
    )


def solution(mesh):
    rows = P("batch", "seq", None)
    return jax.shard_map(
        per_device,
        mesh=mesh,
        in_specs=(rows, P("batch")) + (P(),) * 10 + (rows,),
        out_specs=(rows, rows) + (P(),) * 10,
        check_vma=False,
    )
```

```python
import functools
import math

import jax
import jax.numpy as jnp
from jax import lax
from jax.experimental import pallas as pl
from jax.experimental.pallas import tpu as pltpu
from jax.sharding import PartitionSpec as P

KERNEL = 9
DILATION = 32
REACH = DILATION * (KERNEL // 2)
TILE_ROWS = 512
FF_TILE = 512
EPS = 1e-05
VMEM_BYTES = 63 * 2**20
MESH = pl.DeviceIdType.MESH
RING = 4
EARLY = 4
AHEAD = 3


def passed_along(shard, axis, by):
    size = lax.axis_size(axis)
    pairs = [(i, i + by) for i in range(size) if 0 <= i + by < size]
    return lax.ppermute(shard, axis, pairs)


def product(left, right, over_left, over_right):
    return lax.dot_general(
        left, right, (((over_left,), (over_right,)), ((), ())), preferred_element_type=jnp.float32
    )


def dot(left, right):
    return product(left, right, 1, 0)


def dot_nt(left, right):
    return product(left, right, 1, 1)


def dot_tn(left, right):
    return product(left, right, 0, 0)


def gelu_parts(values):
    cumulative = 0.5 + 0.5 * lax.erf(values * (1.0 / math.sqrt(2.0)))
    density = jnp.exp(-0.5 * values * values) * (1.0 / math.sqrt(2.0 * math.pi))
    return values * cumulative, cumulative + values * density


def normalize(values):
    center = jnp.mean(values, axis=-1, keepdims=True)
    centered = values - center
    inverse = lax.rsqrt(jnp.mean(centered * centered, axis=-1, keepdims=True) + EPS)
    return centered * inverse, inverse


def normalize_back(upstream, normed, inverse, gain):
    inner = upstream * gain
    return inverse * (
        inner
        - jnp.mean(inner, axis=-1, keepdims=True)
        - normed * jnp.mean(inner * normed, axis=-1, keepdims=True)
    )


def col_sum(values):
    return jnp.sum(values, axis=0, keepdims=True)


def remote(src, dst, send_sem, recv_sem, device):
    return pltpu.make_async_remote_copy(
        src_ref=src,
        dst_ref=dst,
        send_sem=send_sem,
        recv_sem=recv_sem,
        device_id=device,
        device_id_type=MESH,
    )


def block_compute(step, depth, keeps, parts, refs):
    (
        cot,
        conv_w,
        conv_b,
        gain1,
        bias1,
        up_w,
        up_b,
        down_w,
        down_b,
        gain2,
        bias2,
        out,
        ext,
        pre_out,
        mid_out,
        hidden,
        upper_out,
        lower_out,
        middle_out,
        d_vec,
        slope,
    ) = refs
    pieces = 2 * depth + 1
    group, rows_here, width = cot.shape
    rows = group * rows_here
    ff = up_w.shape[1]
    tile = min(FF_TILE, ff)
    tiles = ff // tile
    base = depth * rows_here - REACH

    @pl.when(step == 0)
    def _():
        d_vec[...] = jnp.zeros_like(d_vec)

    keep_here = []
    for g in range(group):
        window = step * group + g
        for i in range(pieces):
            keep = keeps[i, window]
            if i == depth:
                keep_here.append(keep)
            ext[g, i * rows_here : (i + 1) * rows_here, :] = parts[i][g] * keep.astype(jnp.bfloat16)

    pre = jnp.broadcast_to(conv_b[...], (rows, width))
    for tap in range(KERNEL):
        begin = base + tap * DILATION
        taken = ext[:, begin : begin + rows_here, :].reshape(rows, width)
        pre = pre + dot(taken, conv_w[tap])
    act, slope1 = gelu_parts(pre)
    n1, s1 = normalize(act)
    branch = (n1 * gain1[...] + bias1[...]).astype(jnp.bfloat16)
    start = ext[:, depth * rows_here : (depth + 1) * rows_here, :].reshape(rows, width)
    middle = start.astype(jnp.float32) + branch.astype(jnp.float32)
    middle_low = middle.astype(jnp.bfloat16)
    middle_out[...] = middle_low

    lower = jnp.broadcast_to(down_b[...], (rows, width))
    for j in range(tiles):
        cols = slice(j * tile, (j + 1) * tile)
        upper = dot(middle_low, up_w[:, cols]) + up_b[:, cols]
        h, sl = gelu_parts(upper)
        h = h.astype(jnp.bfloat16)
        hidden[:, cols] = h
        slope[:, cols] = sl
        lower = lower + dot(h, down_w[cols, :])
    n2, s2 = normalize(lower)
    shaped = (n2 * gain2[...] + bias2[...] + middle).reshape(group, rows_here, width)
    incoming = []
    for g in range(group):
        out[g] = (shaped[g] * keep_here[g]).astype(jnp.bfloat16)
        incoming.append(cot[g].astype(jnp.float32) * keep_here[g])
    incoming = jnp.concatenate(incoming, axis=0)
    d_vec[0:1, :] += col_sum(incoming * n2)
    d_vec[1:2, :] += col_sum(incoming)
    lower_low = normalize_back(incoming, n2, s2, gain2[...]).astype(jnp.bfloat16)
    lower_out[...] = lower_low
    d_vec[2:3, :] += col_sum(lower_low.astype(jnp.float32))
    middle_grad = incoming
    for j in range(tiles):
        cols = slice(j * tile, (j + 1) * tile)
        hidden_grad = dot_nt(lower_low, down_w[cols, :])
        upper_low = (hidden_grad * slope[:, cols]).astype(jnp.bfloat16)
        d_vec[8 + j : 9 + j, :] += col_sum(upper_low.astype(jnp.float32))
        upper_out[:, cols] = upper_low
        middle_grad = middle_grad + dot_nt(upper_low, up_w[:, cols])
    branch_low = middle_grad.astype(jnp.bfloat16)
    mid_out[...] = branch_low.reshape(group, rows_here, width)
    branch_grad = branch_low.astype(jnp.float32)
    d_vec[3:4, :] += col_sum(branch_grad * n1)
    d_vec[4:5, :] += col_sum(branch_grad)
    pre_low = (normalize_back(branch_grad, n1, s1, gain1[...]) * slope1).astype(jnp.bfloat16)
    d_vec[5:6, :] += col_sum(pre_low.astype(jnp.float32))
    pre_low = pre_low.reshape(group, rows_here, width)
    pre_out[...] = pre_low
    return pre_low


def block_kernel(depth, *refs):
    pieces = 2 * depth + 1
    block_compute(pl.program_id(0), depth, refs[0], refs[1 : 1 + pieces], refs[1 + pieces :])


def interleave(units, pieces):
    done = 0
    for n, unit in enumerate(units):
        unit()
        upto = (n + 1) * len(pieces) // len(units)
        for piece in pieces[done:upto]:
            piece()
        done = upto
    for piece in pieces[done:]:
        piece()


def halves(count, size=256):
    return [slice(k * size, (k + 1) * size) for k in range(count // size)]


def rows_in_eights(values):
    return jnp.sum(values.reshape(-1, 8, values.shape[-1]), axis=0)


def block_halo_kernel(blocks, *refs):
    (
        keeps, x_hbm, x_mid, cot, conv_w, conv_b, gain1, bias1, up_w, up_b, down_w, down_b, gain2, bias2,
        out_hbm, ext_hbm, pre_hbm, mid_hbm, hidden_hbm, upper_hbm, lower_hbm, middle_hbm, pre_l, pre_r, d_vec,
        out, ext, mid_out, hidden, upper_out, lower_out,
        slope, conv_acc, n1_all, q1_all, middle, middle_low, lower, mid_grad, vec_acc, upb_acc,
        from_l, from_r, pre_keep, fs, fr, bs, br, ps,
    ) = refs
    group, rows_here, width = cot.shape
    rows = group * rows_here
    ff = up_w.shape[1]
    fine, side_tile = 16, 256
    per_side = side_tile // rows_here
    step = pl.program_id(0)
    s = lax.axis_index("seq")
    b = lax.axis_index("batch")
    last = lax.axis_size("seq") - 1
    has = (s > 0, s < last)
    other = ((s - 1, b), (s + 1, b))

    core = lax.rem(s, 2)

    def near_first(act):
        for side in range(2):
            pl.when(has[1 - side] & (core == 0))(lambda side=1 - side: act(side))
            pl.when(has[side] & (core == 1))(lambda side=side: act(side))

    def place(i, part):
        if part is None:
            return pl.ds(i * group, group), i + 1
        return pl.ds(part * (group // 2), group // 2), part

    def halo(i, side, part=None):
        at, k = place(i, part)
        land = (from_r, from_l)[side]
        return remote(x_hbm.at[at], land.at[at], fs.at[k, side], fr.at[k, side], other[side])

    def halo_in(i, side, part=None):
        at, k = place(i, part)
        land = (from_l, from_r)[side]
        return remote(x_hbm.at[at], land.at[at], fs.at[k, side], fr.at[k, 1 - side], other[side])

    def put(k, block):
        at = pl.ds(block * group, group)
        flat = pl.ds(block * rows, rows)
        source, target = (
            lambda: (ext, ext_hbm.at[at]),
            lambda: (hidden, hidden_hbm.at[flat]),
            lambda: (pre_keep.at[lax.rem(block, 2)], pre_hbm.at[at]),
            lambda: (mid_out, mid_hbm.at[at]),
            lambda: (out, out_hbm.at[at]),
            lambda: (lower_out, lower_hbm.at[flat]),
            lambda: (upper_out, upper_hbm.at[flat]),
            lambda: (middle_low, middle_hbm.at[flat]),
        )[k]()
        return pltpu.make_async_copy(source, target, ps.at[k])

    def puts(start, *pairs):
        for k, block in pairs:

            @pl.when((block >= 0) & (block < blocks))
            def _():
                if start:
                    put(k, block).start()
                else:
                    put(k, block).wait()

    def back(i, side):
        at = pl.ds(i * group, group)
        land = (pre_r, pre_l)[side]
        return remote(pre_keep.at[lax.rem(i, 2)], land.at[at], bs.at[i, side], br.at[i, side], other[side])

    def back_in(i, side):
        at = pl.ds(i * group, group)
        land = (pre_l, pre_r)[side]
        return remote(pre_keep.at[lax.rem(i, 2)], land.at[at], bs.at[i, side], br.at[i, 1 - side], other[side])

    conv_slot = lax.rem(step, 2)
    back_slot = lax.rem(step, 2)
    keep_slot = lax.rem(step, 2)
    fine_rows = [slice(k * fine, (k + 1) * fine) for k in range(rows // fine)]
    sides = halves(rows)
    tiles = halves(ff)
    outs = halves(width)

    def add_vec(k, values):
        vec_acc[k] += rows_in_eights(values)

    def build_ext(w):
        parts = (from_l, x_mid, from_r)

        def piece():
            for k in range(3):
                keep = keeps[k, step * group + w].astype(jnp.bfloat16)
                rows_of = x_mid[w] if k == 1 else parts[k][step * group + w]
                ext[w, k * rows_here : (k + 1) * rows_here, :] = rows_of * keep

        return piece

    def conv_units():
        units = []
        for m, side in enumerate(sides):
            for cols in outs:
                held = {}

                def unit(tap, m=m, side=side, cols=cols, held=held):
                    def run():
                        begin = tap * DILATION
                        taken = ext[m * per_side : (m + 1) * per_side, begin : begin + rows_here, :]
                        value = dot(taken.reshape(side_tile, width), conv_w[tap, :, cols])
                        held["acc"] = value if tap == 0 else held["acc"] + value
                        if tap == KERNEL - 1:
                            conv_acc[side, cols] = held["acc"]

                    return run

                units += [unit(tap) for tap in range(KERNEL)]
        return units

    def first_norm(r):
        def piece():
            act, slope1 = gelu_parts(conv_acc[r, :] + conv_b[...])
            n1, s1 = normalize(act)
            branch = (n1 * gain1[...] + bias1[...]).astype(jnp.bfloat16)
            w, at = r.start // rows_here, r.start % rows_here
            start = ext[w, rows_here + at : rows_here + at + fine, :]
            value = start.astype(jnp.float32) + branch.astype(jnp.float32)
            middle[r, :] = value
            low = value.astype(jnp.bfloat16)
            middle_low[r, :] = low
            n1_all[conv_slot, r, :] = n1
            q1_all[conv_slot, r, :] = s1 * slope1

        return piece

    def forward_slots(extra):
        ups, lowers = {}, {}

        def up(j, m):
            def run():
                ups[j, m] = dot(middle_low[sides[m], :], up_w[:, tiles[j]])

            return run

        def act(j, m, k):
            def run():
                at = slice(k * 64, (k + 1) * 64)
                r = slice(m * side_tile + k * 64, m * side_tile + (k + 1) * 64)
                h, sl = gelu_parts(ups[j, m][at] + up_b[:, tiles[j]])
                hidden[r, tiles[j]] = h.astype(jnp.bfloat16)
                slope[r, tiles[j]] = sl

            return run

        def down(j, m, n):
            def run():
                value = dot(hidden[sides[m], tiles[j]], down_w[tiles[j], outs[n]])
                lowers[m, n] = lowers[m, n] + value if j > 0 else value
                if j == len(tiles) - 1:
                    lower[sides[m], outs[n]] = lowers[m, n]

            return run

        count = len(tiles)
        for m in range(len(sides)):
            up(0, m)()
        taken = 0
        for j in range(count + 1):
            units, pieces = [], []
            if j >= 1:
                units += [down(j - 1, m, n) for m in range(len(sides)) for n in range(len(outs))]
            if j + 1 < count:
                units += [up(j + 1, m) for m in range(len(sides))]
            if j < count:
                pieces += [act(j, m, k) for m in range(len(sides)) for k in range(side_tile // 64)]
            upto = len(extra) * (j + 1) // (count + 1)
            pieces += extra[taken:upto]
            taken = upto
            interleave(units, pieces)

    def second_norm(r):
        def piece():
            w, at = r.start // rows_here, r.start % rows_here
            window = pl.ds(at, fine)
            keep = keeps[1, jnp.maximum(step - 1, 0) * group + w]
            n2, s2 = normalize(lower[r, :] + down_b[...])
            value = middle[r, :] + (n2 * gain2[...] + bias2[...])
            out[w, window, :] = (value * keep).astype(jnp.bfloat16)
            incoming = cot[w, window, :].astype(jnp.float32) * keep
            low = normalize_back(incoming, n2, s2, gain2[...]).astype(jnp.bfloat16)
            lower_out[r, :] = low
            mid_grad[r, :] = incoming
            add_vec(0, incoming * n2)
            add_vec(1, incoming)
            add_vec(2, low.astype(jnp.float32))

        return piece

    def backward_slots(extra):
        hids, mids = {}, {}

        def hid(j, m):
            def run():
                hids[j, m] = dot_nt(lower_out[sides[m], :], down_w[tiles[j], :])

            return run

        def act(j, m, k):
            def run():
                at = slice(k * 64, (k + 1) * 64)
                r = slice(m * side_tile + k * 64, m * side_tile + (k + 1) * 64)
                low = (hids[j, m][at] * slope[r, tiles[j]]).astype(jnp.bfloat16)
                upper_out[r, tiles[j]] = low
                upb_acc[:, tiles[j]] += rows_in_eights(low.astype(jnp.float32))

            return run

        def mid(j, m, n):
            def run():
                value = dot_nt(upper_out[sides[m], tiles[j]], up_w[outs[n], tiles[j]])
                mids[m, n] = mids[m, n] + value if j > 0 else value
                if j == len(tiles) - 1:
                    mid_grad[sides[m], outs[n]] += mids[m, n]

            return run

        count = len(tiles)
        for m in range(len(sides)):
            hid(0, m)()
        taken = 0
        for j in range(count + 1):
            units, pieces = [], []
            if j >= 1:
                units += [mid(j - 1, m, n) for m in range(len(sides)) for n in range(len(outs))]
            if j + 1 < count:
                units += [hid(j + 1, m) for m in range(len(sides))]
            if j < count:
                pieces += [act(j, m, k) for m in range(len(sides)) for k in range(side_tile // 64)]
            upto = len(extra) * (j + 1) // (count + 1)
            pieces += extra[taken:upto]
            taken = upto
            interleave(units, pieces)

    def first_back(r):
        def piece():
            w, at = r.start // rows_here, r.start % rows_here
            window = pl.ds(at, fine)
            low = mid_grad[r, :].astype(jnp.bfloat16)
            mid_out[w, window, :] = low
            grad = low.astype(jnp.float32)
            n1 = n1_all[back_slot, r, :]
            add_vec(3, grad * n1)
            add_vec(4, grad)
            pre_low = normalize_back(grad, n1, q1_all[back_slot, r, :], gain1[...]).astype(jnp.bfloat16)
            pre_keep[keep_slot, w, window, :] = pre_low
            add_vec(5, pre_low.astype(jnp.float32))

        return piece

    @pl.when(step == 0)
    def _():
        barrier = pltpu.get_barrier_semaphore()
        for side in range(2):

            @pl.when(has[side])
            def _():
                pl.semaphore_signal(barrier, inc=1, device_id=other[side], device_id_type=MESH)

        vec_acc[...] = jnp.zeros_like(vec_acc)
        upb_acc[...] = jnp.zeros_like(upb_acc)
        mid_grad[...] = jnp.zeros_like(mid_grad)
        n1_all[...] = jnp.zeros_like(n1_all)
        q1_all[...] = jnp.zeros_like(q1_all)
        pl.semaphore_wait(barrier, (s > 0).astype(jnp.int32) + (s < last).astype(jnp.int32))
        near_first(lambda side: halo(0, side, 0).start())
        near_first(lambda side: halo(0, side, 1).start())
        for i in range(1, AHEAD):
            near_first(lambda side: halo(i, side).start())
        for side in range(2):

            @pl.when(jnp.logical_not(has[side]))
            def _():
                land = (from_l, from_r)[side]
                land[...] = jnp.zeros_like(land)

    @pl.when(step + AHEAD < blocks)
    def _():
        near_first(lambda side: halo(step + AHEAD, side).start())

    for side in range(2):

        @pl.when(has[side] & (step > 0) & (step < blocks))
        def _():
            halo_in(step, side).wait_recv()

        @pl.when(has[side] & (step >= 4) & (step - 4 < EARLY))
        def _():
            back(step - 4, side).wait_send()

    puts(False, (0, step - 1), (1, step - 2), (2, step - 3), (3, step - 3))

    @pl.when((step > 0) & (step < blocks))
    def _():
        forward_slots([build_ext(w) for w in range(group)] + [first_back(r) for r in fine_rows])
        puts(True, (0, step), (1, step - 1), (2, step - 2), (3, step - 2))
        near_first(lambda side: pl.when((step >= 2) & (step - 2 < EARLY))(lambda: back(step - 2, side).start()))
        puts(False, (4, step - 2), (5, step - 2))
        interleave(conv_units(), [second_norm(r) for r in fine_rows])
        puts(True, (4, step - 1), (5, step - 1))
        puts(False, (6, step - 2), (7, step - 1))
        backward_slots([first_norm(r) for r in fine_rows])
        puts(True, (6, step - 1), (7, step))

    @pl.when(step == 0)
    def _():
        units = conv_units()
        for part in range(2):
            for side in range(2):
                pl.when(has[side])(lambda: halo_in(0, side, part).wait_recv())
            for w in range(part * per_side, (part + 1) * per_side):
                build_ext(w)()
            half = len(units) // 2
            pieces = [first_norm(r) for r in fine_rows[: len(fine_rows) // 2]] if part else []
            interleave(units[part * half : (part + 1) * half], pieces)
        for r in fine_rows[len(fine_rows) // 2 :]:
            first_norm(r)()
        puts(True, (0, step), (7, step))

    @pl.when(step == blocks)
    def _():
        forward_slots([first_back(r) for r in fine_rows])
        puts(True, (1, step - 1), (2, step - 2), (3, step - 2))
        puts(False, (4, step - 2), (5, step - 2))
        for r in fine_rows:
            second_norm(r)()
        puts(True, (4, step - 1), (5, step - 1))
        puts(False, (6, step - 2), (7, step - 1))
        backward_slots([])
        puts(True, (6, step - 1))

    @pl.when(step == blocks + 1)
    def _():
        for r in fine_rows:
            first_back(r)()
        puts(True, (2, step - 2), (3, step - 2))
        puts(False, (4, step - 2), (5, step - 2), (6, step - 2))

    @pl.when(step == blocks + 1)
    def _():
        for k in range(6):
            d_vec[k : k + 1, :] = col_sum(vec_acc[k])
        d_vec[6:8, :] = jnp.zeros((2, width), jnp.float32)
        for k in range(ff // width):
            d_vec[8 + k : 9 + k, :] = col_sum(upb_acc[:, k * width : (k + 1) * width])
        for k in range(8 + ff // width, d_vec.shape[0]):
            d_vec[k : k + 1, :] = jnp.zeros((1, width), jnp.float32)
        put(2, blocks - 1).wait()
        put(3, blocks - 1).wait()
        for side in range(2):

            @pl.when(has[side])
            def _():
                for part in range(2):
                    halo(0, side, part).wait_send()
                for i in range(1, blocks):
                    halo(i, side).wait_send()
                for i in range(EARLY):
                    back_in(i, side).wait_recv()


def block_params(conv_w, conv_b, gain1, bias1, up_w, up_b, down_w, down_b, gain2, bias2):
    row = lambda v: v.reshape(1, -1)
    return [conv_w, row(conv_b), row(gain1), row(bias1), up_w, row(up_b), down_w, row(down_b), row(gain2), row(bias2)]


def flat_specs(rows, ff, width):
    return [pl.BlockSpec((rows, w), lambda i: (i, 0)) for w in (ff, ff, width, width)]


def flat_shapes(rows, ff, width):
    return [jax.ShapeDtypeStruct((rows, w), jnp.bfloat16) for w in (ff, ff, width, width)]


def blocks_halo(keeps, x, cot, params):
    windows, rows_here, width = cot.shape
    ff = params[4].shape[1]
    group = TILE_ROWS // rows_here
    count = windows // group
    rows = group * rows_here

    def late(by):
        return lambda i: jnp.clip(i - by, 0, count - 1)

    def tile(by):
        return pl.BlockSpec((group, rows_here, width), lambda i: (late(by)(i), 0, 0))

    whole = pl.BlockSpec(memory_space=pltpu.VMEM)
    anywhere = pl.BlockSpec(memory_space=pl.ANY)
    like = jax.ShapeDtypeStruct(cot.shape, jnp.bfloat16)
    square = pltpu.VMEM((rows, width), jnp.float32)
    block = pltpu.VMEM((group, rows_here, width), jnp.bfloat16)
    dma = pltpu.SemaphoreType.DMA((count + 1, 2))
    return pl.pallas_call(
        functools.partial(block_halo_kernel, count),
        grid=(count + 2,),
        in_specs=[pl.BlockSpec(memory_space=pltpu.SMEM), anywhere, tile(0), tile(1)] + [whole] * len(params),
        out_specs=[anywhere] * 10 + [whole],
        out_shape=[like, jax.ShapeDtypeStruct((windows, 3 * rows_here, width), jnp.bfloat16), like, like]
        + flat_shapes(windows * rows_here, ff, width)
        + [like, like, jax.ShapeDtypeStruct((16, width), jnp.float32)],
        scratch_shapes=[
            block,
            pltpu.VMEM((group, 3 * rows_here, width), jnp.bfloat16),
            block,
            pltpu.VMEM((rows, ff), jnp.bfloat16),
            pltpu.VMEM((rows, ff), jnp.bfloat16),
            pltpu.VMEM((rows, width), jnp.bfloat16),
            pltpu.VMEM((rows, ff), jnp.float32),
            square,
            pltpu.VMEM((2, rows, width), jnp.float32),
            pltpu.VMEM((2, rows, width), jnp.float32),
            square,
            pltpu.VMEM((rows, width), jnp.bfloat16),
            square,
            square,
            pltpu.VMEM((6, 8, width), jnp.float32),
            pltpu.VMEM((8, ff), jnp.float32),
            pltpu.VMEM(cot.shape, jnp.bfloat16),
            pltpu.VMEM(cot.shape, jnp.bfloat16),
            pltpu.VMEM((2, group, rows_here, width), jnp.bfloat16),
            dma,
            dma,
            dma,
            dma,
            pltpu.SemaphoreType.DMA((8,)),
        ],
        compiler_params=pltpu.CompilerParams(
            vmem_limit_bytes=VMEM_BYTES, collective_id=0, has_side_effects=True
        ),
        name="block",
    )(keeps, x, x, cot, *params)


def blocks(keeps, parts, cot, params):
    windows, rows_here, width = cot.shape
    depth = len(parts) // 2
    ff = params[4].shape[1]
    group = max(1, TILE_ROWS // rows_here)
    rows = group * rows_here
    tile = pl.BlockSpec((group, rows_here, width), lambda i: (i, 0, 0))
    wide = pl.BlockSpec((group, (2 * depth + 1) * rows_here, width), lambda i: (i, 0, 0))
    whole = pl.BlockSpec(memory_space=pltpu.VMEM)
    like = jax.ShapeDtypeStruct(cot.shape, jnp.bfloat16)
    return pl.pallas_call(
        functools.partial(block_kernel, depth),
        grid=(windows // group,),
        in_specs=[pl.BlockSpec(memory_space=pltpu.SMEM)] + [tile] * (len(parts) + 1) + [whole] * len(params),
        out_specs=[tile, wide, tile, tile] + flat_specs(rows, ff, width) + [whole],
        out_shape=[like, jax.ShapeDtypeStruct((windows, (2 * depth + 1) * rows_here, width), jnp.bfloat16), like, like]
        + flat_shapes(windows * rows_here, ff, width)
        + [jax.ShapeDtypeStruct((16, width), jnp.float32)],
        scratch_shapes=[pltpu.VMEM((rows, ff), jnp.float32)],
        compiler_params=pltpu.CompilerParams(vmem_limit_bytes=VMEM_BYTES),
        name="block_general",
    )(keeps, *parts, cot, *params)


def back_kernel(depth, *refs):
    pieces = 2 * depth + 1
    keeps = refs[0]
    parts = refs[1 : 1 + pieces]
    start_in, mid_in, conv_w, out, d_conv, ext = refs[1 + pieces :]
    step = pl.program_id(0)
    group, rows_here, width = start_in.shape
    rows = group * rows_here
    base = depth * rows_here - REACH

    @pl.when(step == 0)
    def _():
        d_conv[...] = jnp.zeros_like(d_conv)

    start = []
    for g in range(group):
        start.append(start_in[g] * keeps[depth, step * group + g].astype(jnp.bfloat16))
        for i in range(pieces):
            ext[g, i * rows_here : (i + 1) * rows_here, :] = parts[i][g]
    start = jnp.concatenate(start, axis=0)
    grad = jnp.zeros((rows, width), jnp.float32)
    for tap in range(KERNEL):
        begin = base + (KERNEL - 1 - tap) * DILATION
        taken = ext[:, begin : begin + rows_here, :].reshape(rows, width)
        d_conv[tap] += dot_tn(start, taken)
        grad = grad + dot_nt(taken, conv_w[tap])
    grad = grad.astype(jnp.bfloat16).astype(jnp.float32) + mid_in[...].reshape(rows, width).astype(jnp.float32)
    grad = grad.reshape(group, rows_here, width)
    for g in range(group):
        out[g] = (grad[g] * keeps[depth, step * group + g]).astype(jnp.bfloat16)


def conv_back(keeps, parts, start, mid, conv_w):
    windows, rows_here, width = start.shape
    depth = len(parts) // 2
    group = max(1, TILE_ROWS // rows_here)
    tile = pl.BlockSpec((group, rows_here, width), lambda i: (i, 0, 0))
    whole = pl.BlockSpec(memory_space=pltpu.VMEM)
    return pl.pallas_call(
        functools.partial(back_kernel, depth),
        grid=(windows // group,),
        in_specs=[pl.BlockSpec(memory_space=pltpu.SMEM)] + [tile] * (len(parts) + 2) + [whole],
        out_specs=[tile, whole],
        out_shape=[
            jax.ShapeDtypeStruct(start.shape, jnp.bfloat16),
            jax.ShapeDtypeStruct((KERNEL, width, width), jnp.float32),
        ],
        scratch_shapes=[pltpu.VMEM((group, (2 * depth + 1) * rows_here, width), jnp.bfloat16)],
        compiler_params=pltpu.CompilerParams(vmem_limit_bytes=VMEM_BYTES),
        name="conv_back_general",
    )(keeps, *parts, start, mid, conv_w)


class Reducer:
    stages = 8
    gap = 2

    def __init__(self, count, acc, res, res_out, bufs, sems):
        self.count, self.acc, self.res, self.res_out = count, acc, res, res_out
        self.core_in, self.send1, self.recv1, self.kept1 = bufs[:4]
        self.send2, self.recv2, self.kept2 = bufs[4:7]
        self.send3, self.recv3, self.kept3, self.fin = bufs[7:11]
        (
            self.c_s, self.c_r, self.a_s, self.a_r, self.b_s, self.b_r, self.z_s, self.z_r,
            self.zg_s, self.zg_r, self.bg_s, self.bg_r, self.ag_s, self.ag_r, self.cg_s, self.cg_r, self.out_s,
        ) = sems
        s, b = lax.axis_index("seq"), lax.axis_index("batch")
        self.core, self.z = lax.rem(s, 2), lax.div(s, 2)
        self.x, self.y = lax.rem(b, 2), lax.div(b, 2)
        self.core_peer = (s + 1 - 2 * self.core, b)
        x_peer = (s, b + 1 - 2 * self.x)
        y_peer = (s, b + 2 - 4 * self.y)
        self.first_peer, self.second_peer = (x_peer, y_peer), (y_peer, x_peer)
        self.z_to = [(lax.rem(self.z + d, 4) * 2 + self.core, b) for d in (1, 2, 3)]
        self.z_of = [lax.rem(self.z + d, 4) for d in (1, 2, 3)]
        self.first, self.second = (self.x, self.y), (self.y, self.x)
        self.half = acc.shape[1] // 2
        self.own = self.core * self.half
        self.cols = (slice(0, 256), slice(256, 512))
        self.vec_peers = [
            self.core_peer,
            x_peer,
            y_peer,
            (s + 2 - 4 * lax.rem(self.z, 2), b),
            (s + 4 - 8 * lax.div(self.z, 2), b),
        ]

    def peers(self):
        return [self.core_peer, self.first_peer[0], self.first_peer[1]] + self.z_to

    def rows(self, base, count):
        return pl.ds(pl.multiple_of(base, 16), count)

    def core_copy(self, c):
        r = lax.rem(c, RING)
        away = self.rows((1 - self.core) * self.half, self.half)
        return remote(self.acc.at[r, away], self.core_in.at[r], self.c_s.at[r], self.c_r.at[r], self.core_peer)

    def copy1(self, c, h):
        r = lax.rem(c, RING)
        at = (r, slice(None), self.cols[h])
        return remote(self.send1.at[at], self.recv1.at[at], self.a_s.at[r, h], self.a_r.at[r, h], self.first_peer[h])

    def copy2(self, c, h):
        r = lax.rem(c, RING)
        at = (r, slice(None), self.cols[h])
        return remote(self.send2.at[at], self.recv2.at[at], self.b_s.at[r, h], self.b_r.at[r, h], self.second_peer[h])

    def copy3(self, c, d):
        r = lax.rem(c, RING)
        return remote(self.send3.at[r, d], self.recv3.at[r, d], self.z_s.at[r, d], self.z_r.at[r, d], self.z_to[d])

    def base1(self, h):
        return self.own + self.first[h] * 128

    def base2(self, h):
        return self.base1(h) + self.second[h] * 64

    def spread_z(self, c, d, h):
        r = lax.rem(c, RING)
        land = self.res.at[c, self.rows(self.base2(h) + self.z * 16, 16), self.cols[h]]
        return remote(
            self.fin.at[r, :, self.cols[h]], land, self.zg_s.at[r, d, h], self.zg_r.at[r, d, h], self.z_to[d]
        )

    def spread_same(self, c, base, count, cols, s, r, peer):
        part = self.res.at[c, self.rows(base, count), cols]
        return remote(part, part, s, r, peer)

    def spread2(self, c, h):
        r = lax.rem(c, RING)
        return self.spread_same(
            c, self.base2(h), 64, self.cols[h], self.bg_s.at[r, h], self.bg_r.at[r, h], self.second_peer[h]
        )

    def spread1(self, c, h):
        r = lax.rem(c, RING)
        return self.spread_same(
            c, self.base1(h), 128, self.cols[h], self.ag_s.at[r, h], self.ag_r.at[r, h], self.first_peer[h]
        )

    def spread_core(self, c):
        r = lax.rem(c, RING)
        return self.spread_same(
            c, self.own, self.half, slice(0, 512), self.cg_s.at[r], self.cg_r.at[r], self.core_peer
        )

    def write_out(self, c, act):
        up_out, down_out, conv_out = self.res_out
        width, tiles = self.acc.shape[1], up_out.shape[1] // self.acc.shape[1]
        wide = lambda i: pl.ds(pl.multiple_of(i * width, width), width)

        def copy(to):
            return lambda: act(pltpu.make_async_copy(self.res.at[c], to, self.out_s.at[lax.rem(c, 2)]))

        pl.when(c < tiles)(copy(up_out.at[:, wide(c)]))
        pl.when((c >= tiles) & (c < 2 * tiles))(copy(down_out.at[wide(c - tiles), :]))
        pl.when(c >= 2 * tiles)(copy(conv_out.at[c - 2 * tiles]))

    def stage0(self, c):
        self.core_copy(c).start()

    def stage1(self, c):
        self.core_copy(c).wait()
        r = lax.rem(c, RING)
        for h in range(2):
            cols = self.cols[h]
            keep, give = self.first[h] * 128, (1 - self.first[h]) * 128
            self.send1[r, :, cols] = (
                self.acc[r, self.rows(self.own + give, 128), cols] + self.core_in[r, self.rows(give, 128), cols]
            ).astype(jnp.bfloat16)
            self.copy1(c, h).start()
            self.kept1[r, :, cols] = (
                self.acc[r, self.rows(self.own + keep, 128), cols] + self.core_in[r, self.rows(keep, 128), cols]
            )

    def stage2(self, c):
        r = lax.rem(c, RING)
        for h in range(2):
            self.copy1(c, h).wait()
            cols = self.cols[h]
            keep, give = self.second[h] * 64, (1 - self.second[h]) * 64
            self.send2[r, :, cols] = (
                self.kept1[r, self.rows(give, 64), cols]
                + self.recv1[r, self.rows(give, 64), cols].astype(jnp.float32)
            ).astype(jnp.bfloat16)
            self.copy2(c, h).start()
            self.kept2[r, :, cols] = self.kept1[r, self.rows(keep, 64), cols] + self.recv1[
                r, self.rows(keep, 64), cols
            ].astype(jnp.float32)

    def stage3(self, c):
        r = lax.rem(c, RING)
        for h in range(2):
            self.copy2(c, h).wait()
        for d in range(3):
            at = self.rows(self.z_of[d] * 16, 16)
            self.send3[r, d] = (self.kept2[r, at, :] + self.recv2[r, at, :].astype(jnp.float32)).astype(jnp.bfloat16)
            self.copy3(c, d).start()
        at = self.rows(self.z * 16, 16)
        self.kept3[r] = self.kept2[r, at, :] + self.recv2[r, at, :].astype(jnp.float32)

    def stage4(self, c):
        r = lax.rem(c, RING)
        total = self.kept3[r]
        for d in range(3):
            self.copy3(c, d).wait()
            total = total + self.recv3[r, d].astype(jnp.float32)
        total = total.astype(jnp.bfloat16)
        self.fin[r] = total
        for h in range(2):
            for d in range(3):
                self.spread_z(c, d, h).start()
            self.res[c, self.rows(self.base2(h) + self.z * 16, 16), self.cols[h]] = total[:, self.cols[h]]

    def stage5(self, c):
        for h in range(2):
            for d in range(3):
                self.spread_z(c, d, h).wait()
            self.spread2(c, h).start()

    def stage6(self, c):
        for h in range(2):
            self.spread2(c, h).wait()
            self.spread1(c, h).start()

    def stage7(self, c):
        for h in range(2):
            self.spread1(c, h).wait()
        self.spread_core(c).start()

    def stage8(self, c):
        self.spread_core(c).wait()

        @pl.when(c >= 2)
        def _():
            self.write_out(c - 2, lambda copy: copy.wait())

        self.write_out(c, lambda copy: copy.start())

    def tick(self, t):
        for stage in range(self.stages, -1, -1):
            c = t - stage * self.gap

            @pl.when((c >= 0) & (c < self.count))
            def _():
                getattr(self, "stage%d" % stage)(c)

    def finish(self):
        for c in range(max(0, self.count - 2), self.count):
            self.write_out(jnp.int32(c), lambda copy: copy.wait())


def hidden_width(tiles):
    return tiles.shape[2]


def reduce_kernel(steps, *refs):
    (
        keeps, hidden, upper, lower_hbm, middle_hbm, vec_in, ext_hbm, pre_hbm, pre_l, pre_r, mid_hbm, conv_w,
        grad_out, up_out, down_out, conv_out, vec_out, late_l, late_r,
        ext, pre, lower, middle, tiles, acc, res, pext, midb, gout, vsend, vrecv,
    ) = refs[:31]
    bufs = refs[31:42]
    sems = refs[42:59]
    load_s, ffn_s, in_s, gout_s, v_s, v_r, late_s, late_q = refs[59:]
    ff_tiles = hidden.shape[1] // hidden_width(tiles)
    ffn_count = 2 * ff_tiles
    count = ffn_count + KERNEL
    group, rows_here, width = gout.shape[1:]
    rows = group * rows_here
    red = Reducer(count, acc, res, (up_out, down_out, conv_out), bufs, sems)
    s = lax.axis_index("seq")
    last = lax.axis_size("seq") - 1

    b = lax.axis_index("batch")
    has = (s > 0, s < last)
    other = ((s - 1, b), (s + 1, b))
    beyond = jnp.where(red.core == 0, s - 1, s + 1)
    has_beyond = (beyond >= 0) & (beyond <= last)

    barrier = pltpu.get_barrier_semaphore()
    for peer in red.peers():
        pl.semaphore_signal(barrier, inc=1, device_id=peer, device_id_type=MESH)

    @pl.when(has_beyond)
    def _():
        pl.semaphore_signal(barrier, inc=1, device_id=(beyond, b), device_id_type=MESH)

    def late(i, side):
        at = pl.ds((i - EARLY) * group, group)
        land = (late_r, late_l)[side]
        k = i - EARLY
        return remote(
            pre_hbm.at[pl.ds(i * group, group)], land.at[at], late_s.at[k, side], late_q.at[k, side], other[side]
        )

    def late_in(i, side):
        at = pl.ds((i - EARLY) * group, group)
        land = (late_l, late_r)[side]
        k = i - EARLY
        return remote(
            pre_hbm.at[pl.ds(i * group, group)], land.at[at], late_s.at[k, side], late_q.at[k, 1 - side], other[side]
        )

    load_ext = pltpu.make_async_copy(ext_hbm, ext, load_s.at[0])
    load_pre = pltpu.make_async_copy(pre_hbm, pre, load_s.at[1])

    load_lower = pltpu.make_async_copy(lower_hbm, lower, load_s.at[2])
    load_middle = pltpu.make_async_copy(middle_hbm, middle, load_s.at[3])
    tile_rows = tiles.shape[1]
    per_chunk = lower.shape[0] // tile_rows

    def load_tile(i, act):
        r = lax.rem(i, 2)
        c = lax.div(i, per_chunk)
        at = pl.ds(pl.multiple_of(lax.rem(i, per_chunk) * tile_rows, tile_rows), tile_rows)

        def copy(source, first):
            cols = pl.ds(pl.multiple_of((c - first) * width, width), width)
            return lambda: act(pltpu.make_async_copy(source.at[at, cols], tiles.at[r], ffn_s.at[r]))

        pl.when(c < ff_tiles)(copy(upper, 0))
        pl.when((c >= ff_tiles) & (c < ffn_count))(copy(hidden, ff_tiles))

    def ffn_grad(c):
        r = lax.rem(c, RING)

        def part(i):
            tile = c * per_chunk + i
            load_tile(tile, lambda copy: copy.wait())
            load_tile(tile + 1, lambda copy: copy.start())
            at = pl.ds(pl.multiple_of(i * tile_rows, tile_rows), tile_rows)
            slot = lax.rem(tile, 2)

            def add(value):
                @pl.when(i == 0)
                def _():
                    acc[r] = value

                @pl.when(i > 0)
                def _():
                    acc[r] += value

            pl.when(c < ff_tiles)(lambda: add(dot_tn(middle[at], tiles[slot])))
            pl.when(c >= ff_tiles)(lambda: add(dot_tn(tiles[slot], lower[at])))

        lax.fori_loop(0, per_chunk, lambda i, _: (part(i), 0)[1], 0)

    def each_load(i, act, fresh=False):
        slot = lax.rem(i, 2)
        at = pl.ds(i * group, group)
        at_late = pl.ds((i - EARLY) * group, group)
        for side, early_ref, late_ref in ((0, pre_l, late_l), (1, pre_r, late_r)):
            to = pext.at[slot, :, pl.ds(2 * side * rows_here, rows_here)]
            sem = in_s.at[slot, side]

            @pl.when(has[side] & (i < EARLY))
            def _():
                act(pltpu.make_async_copy(early_ref.at[at], to, sem))

            @pl.when(has[side] & (i >= EARLY))
            def _():
                if fresh:
                    late_in(i, side).wait_recv()
                act(pltpu.make_async_copy(late_ref.at[at_late], to, sem))

        act(pltpu.make_async_copy(pre_hbm.at[at], pext.at[slot, :, pl.ds(rows_here, rows_here)], in_s.at[slot, 2]))
        act(pltpu.make_async_copy(mid_hbm.at[at], midb.at[slot], in_s.at[slot, 3]))

    def store_rows(i):
        slot = lax.rem(i, 2)
        return pltpu.make_async_copy(gout.at[slot], grad_out.at[pl.ds(i * group, group)], gout_s.at[slot])

    load_middle.start()
    for i in range(1):
        load_tile(jnp.int32(i), lambda copy: copy.start())
    for side, at in ((s > 0, 0), (s < last, 2)):

        @pl.when(jnp.logical_not(side))
        def _():
            pext[:, :, at * rows_here : (at + 1) * rows_here, :] = jnp.zeros(
                (2, group, rows_here, width), jnp.bfloat16
            )

    pl.semaphore_wait(barrier, len(red.peers()) + has_beyond.astype(jnp.int32))
    for i in range(EARLY, steps):
        for side in range(2):
            pl.when(has[1 - side] & (red.core == 0))(lambda: late(i, 1 - side).start())
            pl.when(has[side] & (red.core == 1))(lambda: late(i, side).start())

    def vec_copy(q):
        return remote(vsend.at[q], vrecv.at[q], v_s.at[q], v_r.at[q], red.vec_peers[q])

    def row_block(i):
        each_load(i, lambda copy: copy.wait())

        @pl.when(i + 1 < steps)
        def _():
            each_load(i + 1, lambda copy: copy.start(), True)

        slot = lax.rem(i, 2)
        grad = jnp.zeros((rows, width), jnp.float32)
        for tap in range(KERNEL):
            begin = (KERNEL - 1 - tap) * DILATION
            taken = pext[slot, :, begin : begin + rows_here, :].reshape(rows, width)
            grad = grad + dot_nt(taken, conv_w[tap])
        grad = grad.astype(jnp.bfloat16).astype(jnp.float32)
        grad = (grad + midb[slot].reshape(rows, width).astype(jnp.float32)).reshape(group, rows_here, width)

        @pl.when(i >= 2)
        def _():
            store_rows(i - 2).wait()

        for g in range(group):
            gout[slot, g] = (grad[g] * keeps[1, i * group + g]).astype(jnp.bfloat16)
        store_rows(i).start()

    def tap_grad(tap):
        r = lax.rem(ffn_count + tap, RING)
        begin = pl.multiple_of(tap * DILATION, DILATION)

        taken = ext[:, pl.ds(begin, rows_here), :].reshape(steps * rows, width)
        acc[r] = dot_tn(taken, pre[...].reshape(steps * rows, width))

    load_middle.wait()

    def tick(t, _):
        red.tick(t)
        for q in range(6):

            @pl.when(t == q)
            def _():
                if q == 0:
                    value = vec_in[...]
                else:
                    vec_copy(q - 1).wait()
                    value = vsend[q - 1] + vrecv[q - 1]
                if q < 5:
                    vsend[q] = value
                    vec_copy(q).start()
                else:
                    vec_out[...] = value

        pl.when(t == 0)(lambda: load_lower.start())
        pl.when(t == 2)(lambda: load_pre.start())
        pl.when(t == 3)(lambda: load_ext.start())
        pl.when(t == ffn_count)(lambda: each_load(0, lambda copy: copy.start()))
        chunk = t + 1

        @pl.when(chunk == ff_tiles)
        def _():
            load_lower.wait()

        @pl.when(chunk < ffn_count)
        def _():
            ffn_grad(chunk)

        @pl.when(chunk == ffn_count)
        def _():
            load_ext.wait()
            load_pre.wait()

        rest = t - (count - 1)

        @pl.when((rest >= 0) & (rest < steps))
        def _():
            row_block(rest)

        tap = chunk - ffn_count

        @pl.when((tap >= 0) & (tap < KERNEL))
        def _():
            tap_grad(tap)

        return 0

    lax.fori_loop(-1, count + red.stages * red.gap, tick, 0)
    red.finish()
    for i in range(EARLY, steps):
        for side in range(2):
            pl.when(has[side])(lambda: late(i, side).wait_send())
    for i in range(max(0, steps - 2), steps):
        store_rows(i).wait()


def reduce_all(keeps, hidden, upper, lower, middle, vec, ext, pre, pre_l, pre_r, mid, conv_w):
    windows, rows_here, width = pre.shape
    ff = hidden.shape[1]
    group = TILE_ROWS // rows_here
    steps = windows // group
    count = 2 * ff // width + KERNEL
    whole = pl.BlockSpec(memory_space=pltpu.VMEM)
    anywhere = pl.BlockSpec(memory_space=pl.ANY)
    dma = pltpu.SemaphoreType.DMA
    half = width // 2
    rows = group * rows_here
    return pl.pallas_call(
        functools.partial(reduce_kernel, steps),
        in_specs=[pl.BlockSpec(memory_space=pltpu.SMEM), anywhere, anywhere, anywhere, anywhere, whole] + [anywhere] * 5 + [whole],
        out_specs=[anywhere] * 4 + [whole, anywhere, anywhere],
        out_shape=[
            jax.ShapeDtypeStruct(pre.shape, jnp.bfloat16),
            jax.ShapeDtypeStruct((width, ff), jnp.bfloat16),
            jax.ShapeDtypeStruct((ff, width), jnp.bfloat16),
            jax.ShapeDtypeStruct((KERNEL, width, width), jnp.bfloat16),
            jax.ShapeDtypeStruct(vec.shape, jnp.float32),
        ]
        + [jax.ShapeDtypeStruct(((steps - EARLY) * group, rows_here, width), jnp.bfloat16)] * 2,
        scratch_shapes=[
            pltpu.VMEM(ext.shape, jnp.bfloat16),
            pltpu.VMEM(pre.shape, jnp.bfloat16),
            pltpu.VMEM(lower.shape, jnp.bfloat16),
            pltpu.VMEM(middle.shape, jnp.bfloat16),
            pltpu.VMEM((2, 4 * rows, width), jnp.bfloat16),
            pltpu.VMEM((RING, width, width), jnp.float32),
            pltpu.VMEM((count, width, width), jnp.bfloat16),
            pltpu.VMEM((2, group, 3 * rows_here, width), jnp.bfloat16),
            pltpu.VMEM((2, group, rows_here, width), jnp.bfloat16),
            pltpu.VMEM((2, group, rows_here, width), jnp.bfloat16),
            pltpu.VMEM((5,) + vec.shape, jnp.float32),
            pltpu.VMEM((5,) + vec.shape, jnp.float32),
            pltpu.VMEM((RING, half, width), jnp.float32),
            pltpu.VMEM((RING, half // 2, width), jnp.bfloat16),
            pltpu.VMEM((RING, half // 2, width), jnp.bfloat16),
            pltpu.VMEM((RING, half // 2, width), jnp.float32),
            pltpu.VMEM((RING, half // 4, width), jnp.bfloat16),
            pltpu.VMEM((RING, half // 4, width), jnp.bfloat16),
            pltpu.VMEM((RING, half // 4, width), jnp.float32),
            pltpu.VMEM((RING, 3, half // 16, width), jnp.bfloat16),
            pltpu.VMEM((RING, 3, half // 16, width), jnp.bfloat16),
            pltpu.VMEM((RING, half // 16, width), jnp.float32),
            pltpu.VMEM((RING, half // 16, width), jnp.bfloat16),
        ]
        + [
            dma((RING,)), dma((RING,)), dma((RING, 2)), dma((RING, 2)), dma((RING, 2)), dma((RING, 2)),
            dma((RING, 3)), dma((RING, 3)), dma((RING, 3, 2)), dma((RING, 3, 2)), dma((RING, 2)), dma((RING, 2)),
            dma((RING, 2)), dma((RING, 2)), dma((RING,)), dma((RING,)), dma((2,)),
        ]
        + [dma((4,)), dma((RING,)), dma((2, 4)), dma((2,)), dma((5,)), dma((5,))]
        + [dma((steps - EARLY, 2)), dma((steps - EARLY, 2))],
        compiler_params=pltpu.CompilerParams(
            vmem_limit_bytes=VMEM_BYTES, collective_id=1, has_side_effects=True
        ),
        name="reduce",
    )(keeps, hidden, upper, lower, middle, vec, ext, pre, pre_l, pre_r, mid, conv_w)


def widen_kernel(*refs):
    for source, target in zip(refs[:3], refs[3:]):
        target[...] = source[...].astype(jnp.float32)


def widened(d_up, d_down, d_conv):
    taps, width, _ = d_conv.shape
    ff = d_down.shape[0]
    parts = taps - 1
    at = lambda i: (jnp.minimum(i, parts - 1), 0)
    specs = [
        pl.BlockSpec((width // parts, ff), at),
        pl.BlockSpec((ff // parts, width), at),
        pl.BlockSpec((1, width, width), lambda i: (i, 0, 0)),
    ]
    return pl.pallas_call(
        widen_kernel,
        grid=(taps,),
        in_specs=specs,
        out_specs=specs,
        out_shape=[jax.ShapeDtypeStruct(d.shape, jnp.float32) for d in (d_up, d_down, d_conv)],
        compiler_params=pltpu.CompilerParams(vmem_limit_bytes=VMEM_BYTES),
        name="tail",
    )(d_up, d_down, d_conv)


def spread(shard, depth):
    return [
        shard if offset == 0 else passed_along(shard, "seq", offset)
        for offset in range(depth, -depth - 1, -1)
    ]


def per_device(
    block_input,
    window_lengths,
    conv_weight,
    conv_bias,
    norm1_gain,
    norm1_bias,
    up_weight,
    up_bias,
    down_weight,
    down_bias,
    norm2_gain,
    norm2_bias,
    out_cotangent,
):
    windows, rows_here, width = block_input.shape
    ff = up_weight.shape[1]
    depth = -(-REACH // rows_here)
    first = (lax.axis_index("seq") + jnp.arange(-depth, depth + 1, dtype=jnp.int32)) * rows_here
    keeps = (first[:, None] < window_lengths[None, :]).astype(jnp.float32)
    params = block_params(
        conv_weight, conv_bias, norm1_gain, norm1_bias, up_weight, up_bias, down_weight, down_bias, norm2_gain, norm2_bias
    )
    tiles = ff // FF_TILE
    if (lax.axis_size("seq"), lax.axis_size("batch"), rows_here) == (8, 4, REACH):
        out, ext, pre_low, mid_low, hidden, upper, lower, middle, pre_l, pre_r, d_vec = blocks_halo(
            keeps, block_input, out_cotangent, params
        )
        input_grad, d_up, d_down, d_conv, d_vec, _, _ = reduce_all(
            keeps, hidden, upper, lower, middle, d_vec, ext, pre_low, pre_l, pre_r, mid_low, conv_weight
        )
        d_up, d_down, d_conv = widened(d_up, d_down, d_conv)
    else:
        parts = spread(block_input, depth)
        out, _, pre_low, mid_low, hidden, upper, lower, middle, d_vec = blocks(keeps, parts, out_cotangent, params)
        input_grad, d_conv = conv_back(keeps, spread(pre_low, depth), block_input, mid_low, conv_weight)
        d_up, d_down = dot_tn(middle, upper), dot_tn(hidden, lower)
        d_up, d_down, d_conv, d_vec = lax.psum((d_up, d_down, d_conv, d_vec), ("seq", "batch"))
    return (
        out,
        input_grad,
        d_conv,
        d_vec[5],
        d_vec[3],
        d_vec[4],
        d_up,
        d_vec[8 : 8 + tiles].reshape(ff),
        d_down,
        d_vec[2],
        d_vec[0],
        d_vec[1],
    )


def solution(mesh):
    rows = P("batch", "seq", None)
    return jax.shard_map(
        per_device,
        mesh=mesh,
        in_specs=(rows, P("batch")) + (P(),) * 10 + (rows,),
        out_specs=(rows, rows) + (P(),) * 10,
        check_vma=False,
    )
```

```python
import functools
import math

import jax
import jax.numpy as jnp
from jax import lax
from jax.experimental import pallas as pl
from jax.experimental.pallas import tpu as pltpu
from jax.sharding import PartitionSpec as P

KERNEL = 9
DILATION = 32
REACH = DILATION * (KERNEL // 2)
TILE_ROWS = 512
FF_TILE = 512
EPS = 1e-05
VMEM_BYTES = 63 * 2**20
MESH = pl.DeviceIdType.MESH
RING = 4
EARLY = 4
AHEAD = 3


def passed_along(shard, axis, by):
    size = lax.axis_size(axis)
    pairs = [(i, i + by) for i in range(size) if 0 <= i + by < size]
    return lax.ppermute(shard, axis, pairs)


def product(left, right, over_left, over_right):
    return lax.dot_general(
        left, right, (((over_left,), (over_right,)), ((), ())), preferred_element_type=jnp.float32
    )


def dot(left, right):
    return product(left, right, 1, 0)


def dot_nt(left, right):
    return product(left, right, 1, 1)


def dot_tn(left, right):
    return product(left, right, 0, 0)


def gelu_parts(values):
    cumulative = 0.5 + 0.5 * lax.erf(values * (1.0 / math.sqrt(2.0)))
    density = jnp.exp(-0.5 * values * values) * (1.0 / math.sqrt(2.0 * math.pi))
    return values * cumulative, cumulative + values * density


def normalize(values):
    center = jnp.mean(values, axis=-1, keepdims=True)
    centered = values - center
    inverse = lax.rsqrt(jnp.mean(centered * centered, axis=-1, keepdims=True) + EPS)
    return centered * inverse, inverse


def normalize_back(upstream, normed, inverse, gain):
    inner = upstream * gain
    return inverse * (
        inner
        - jnp.mean(inner, axis=-1, keepdims=True)
        - normed * jnp.mean(inner * normed, axis=-1, keepdims=True)
    )


def col_sum(values):
    return jnp.sum(values, axis=0, keepdims=True)


def remote(src, dst, send_sem, recv_sem, device):
    return pltpu.make_async_remote_copy(
        src_ref=src,
        dst_ref=dst,
        send_sem=send_sem,
        recv_sem=recv_sem,
        device_id=device,
        device_id_type=MESH,
    )


def block_compute(step, depth, keeps, parts, refs):
    (
        cot,
        conv_w,
        conv_b,
        gain1,
        bias1,
        up_w,
        up_b,
        down_w,
        down_b,
        gain2,
        bias2,
        out,
        ext,
        pre_out,
        mid_out,
        hidden,
        upper_out,
        lower_out,
        middle_out,
        d_vec,
        slope,
    ) = refs
    pieces = 2 * depth + 1
    group, rows_here, width = cot.shape
    rows = group * rows_here
    ff = up_w.shape[1]
    tile = min(FF_TILE, ff)
    tiles = ff // tile
    base = depth * rows_here - REACH

    @pl.when(step == 0)
    def _():
        d_vec[...] = jnp.zeros_like(d_vec)

    keep_here = []
    for g in range(group):
        window = step * group + g
        for i in range(pieces):
            keep = keeps[i, window]
            if i == depth:
                keep_here.append(keep)
            ext[g, i * rows_here : (i + 1) * rows_here, :] = parts[i][g] * keep.astype(jnp.bfloat16)

    pre = jnp.broadcast_to(conv_b[...], (rows, width))
    for tap in range(KERNEL):
        begin = base + tap * DILATION
        taken = ext[:, begin : begin + rows_here, :].reshape(rows, width)
        pre = pre + dot(taken, conv_w[tap])
    act, slope1 = gelu_parts(pre)
    n1, s1 = normalize(act)
    branch = (n1 * gain1[...] + bias1[...]).astype(jnp.bfloat16)
    start = ext[:, depth * rows_here : (depth + 1) * rows_here, :].reshape(rows, width)
    middle = start.astype(jnp.float32) + branch.astype(jnp.float32)
    middle_low = middle.astype(jnp.bfloat16)
    middle_out[...] = middle_low

    lower = jnp.broadcast_to(down_b[...], (rows, width))
    for j in range(tiles):
        cols = slice(j * tile, (j + 1) * tile)
        upper = dot(middle_low, up_w[:, cols]) + up_b[:, cols]
        h, sl = gelu_parts(upper)
        h = h.astype(jnp.bfloat16)
        hidden[:, cols] = h
        slope[:, cols] = sl
        lower = lower + dot(h, down_w[cols, :])
    n2, s2 = normalize(lower)
    shaped = (n2 * gain2[...] + bias2[...] + middle).reshape(group, rows_here, width)
    incoming = []
    for g in range(group):
        out[g] = (shaped[g] * keep_here[g]).astype(jnp.bfloat16)
        incoming.append(cot[g].astype(jnp.float32) * keep_here[g])
    incoming = jnp.concatenate(incoming, axis=0)
    d_vec[0:1, :] += col_sum(incoming * n2)
    d_vec[1:2, :] += col_sum(incoming)
    lower_low = normalize_back(incoming, n2, s2, gain2[...]).astype(jnp.bfloat16)
    lower_out[...] = lower_low
    d_vec[2:3, :] += col_sum(lower_low.astype(jnp.float32))
    middle_grad = incoming
    for j in range(tiles):
        cols = slice(j * tile, (j + 1) * tile)
        hidden_grad = dot_nt(lower_low, down_w[cols, :])
        upper_low = (hidden_grad * slope[:, cols]).astype(jnp.bfloat16)
        d_vec[8 + j : 9 + j, :] += col_sum(upper_low.astype(jnp.float32))
        upper_out[:, cols] = upper_low
        middle_grad = middle_grad + dot_nt(upper_low, up_w[:, cols])
    branch_low = middle_grad.astype(jnp.bfloat16)
    mid_out[...] = branch_low.reshape(group, rows_here, width)
    branch_grad = branch_low.astype(jnp.float32)
    d_vec[3:4, :] += col_sum(branch_grad * n1)
    d_vec[4:5, :] += col_sum(branch_grad)
    pre_low = (normalize_back(branch_grad, n1, s1, gain1[...]) * slope1).astype(jnp.bfloat16)
    d_vec[5:6, :] += col_sum(pre_low.astype(jnp.float32))
    pre_low = pre_low.reshape(group, rows_here, width)
    pre_out[...] = pre_low
    return pre_low


def block_kernel(depth, *refs):
    pieces = 2 * depth + 1
    block_compute(pl.program_id(0), depth, refs[0], refs[1 : 1 + pieces], refs[1 + pieces :])


def interleave(units, pieces):
    done = 0
    for n, unit in enumerate(units):
        unit()
        upto = (n + 1) * len(pieces) // len(units)
        for piece in pieces[done:upto]:
            piece()
        done = upto
    for piece in pieces[done:]:
        piece()


def halves(count, size=256):
    return [slice(k * size, (k + 1) * size) for k in range(count // size)]


def rows_in_eights(values):
    return jnp.sum(values.reshape(-1, 8, values.shape[-1]), axis=0)


def block_halo_kernel(blocks, *refs):
    (
        keeps, x_hbm, x_mid, cot, conv_hbm, conv_b, gain1, bias1, up_hbm, up_b, down_hbm, down_b, gain2, bias2,
        out_hbm, ext_hbm, pre_hbm, mid_hbm, hidden_hbm, upper_hbm, lower_hbm, middle_hbm, pre_l, pre_r, d_vec,
        out, ext, mid_out, hidden, upper_out, lower_out,
        slope, conv_acc, n1_all, q1_all, middle, middle_low, lower, mid_grad, vec_acc, upb_acc,
        from_l, from_r, pre_keep, fs, fr, bs, br, ps, conv_w, up_w, down_w, ws,
    ) = refs
    weight_loads = [
        pltpu.make_async_copy(source, target, ws.at[k])
        for k, (source, target) in enumerate(((conv_hbm, conv_w), (up_hbm, up_w), (down_hbm, down_w)))
    ]
    group, rows_here, width = cot.shape
    rows = group * rows_here
    ff = up_w.shape[1]
    fine, side_tile = 16, 256
    per_side = side_tile // rows_here
    step = pl.program_id(0)
    s = lax.axis_index("seq")
    b = lax.axis_index("batch")
    last = lax.axis_size("seq") - 1
    has = (s > 0, s < last)
    other = ((s - 1, b), (s + 1, b))

    core = lax.rem(s, 2)

    def near_first(act):
        for side in range(2):
            pl.when(has[1 - side] & (core == 0))(lambda side=1 - side: act(side))
            pl.when(has[side] & (core == 1))(lambda side=side: act(side))

    def place(i, part):
        if part is None:
            return pl.ds(i * group, group), i + 1
        return pl.ds(part * (group // 2), group // 2), part

    def halo(i, side, part=None):
        at, k = place(i, part)
        land = (from_r, from_l)[side]
        return remote(x_hbm.at[at], land.at[at], fs.at[k, side], fr.at[k, side], other[side])

    def halo_in(i, side, part=None):
        at, k = place(i, part)
        land = (from_l, from_r)[side]
        return remote(x_hbm.at[at], land.at[at], fs.at[k, side], fr.at[k, 1 - side], other[side])

    def put(k, block):
        at = pl.ds(block * group, group)
        flat = pl.ds(block * rows, rows)
        source, target = (
            lambda: (ext, ext_hbm.at[at]),
            lambda: (hidden, hidden_hbm.at[flat]),
            lambda: (pre_keep.at[lax.rem(block, 2)], pre_hbm.at[at]),
            lambda: (mid_out, mid_hbm.at[at]),
            lambda: (out, out_hbm.at[at]),
            lambda: (lower_out, lower_hbm.at[flat]),
            lambda: (upper_out, upper_hbm.at[flat]),
            lambda: (middle_low, middle_hbm.at[flat]),
        )[k]()
        return pltpu.make_async_copy(source, target, ps.at[k])

    def puts(start, *pairs):
        for k, block in pairs:

            @pl.when((block >= 0) & (block < blocks))
            def _():
                if start:
                    put(k, block).start()
                else:
                    put(k, block).wait()

    def back(i, side):
        at = pl.ds(i * group, group)
        land = (pre_r, pre_l)[side]
        return remote(pre_keep.at[lax.rem(i, 2)], land.at[at], bs.at[i, side], br.at[i, side], other[side])

    def back_in(i, side):
        at = pl.ds(i * group, group)
        land = (pre_l, pre_r)[side]
        return remote(pre_keep.at[lax.rem(i, 2)], land.at[at], bs.at[i, side], br.at[i, 1 - side], other[side])

    conv_slot = lax.rem(step, 2)
    back_slot = lax.rem(step, 2)
    keep_slot = lax.rem(step, 2)
    fine_rows = [slice(k * fine, (k + 1) * fine) for k in range(rows // fine)]
    sides = halves(rows)
    tiles = halves(ff)
    outs = halves(width)

    def add_vec(k, values):
        vec_acc[k] += rows_in_eights(values)

    def build_ext(w):
        parts = (from_l, x_mid, from_r)

        def piece():
            for k in range(3):
                keep = keeps[k, step * group + w].astype(jnp.bfloat16)
                rows_of = x_mid[w] if k == 1 else parts[k][step * group + w]
                ext[w, k * rows_here : (k + 1) * rows_here, :] = rows_of * keep

        return piece

    def conv_units():
        units = []
        for m, side in enumerate(sides):
            for cols in outs:
                held = {}

                def unit(tap, m=m, side=side, cols=cols, held=held):
                    def run():
                        begin = tap * DILATION
                        taken = ext[m * per_side : (m + 1) * per_side, begin : begin + rows_here, :]
                        value = dot(taken.reshape(side_tile, width), conv_w[tap, :, cols])
                        held["acc"] = value if tap == 0 else held["acc"] + value
                        if tap == KERNEL - 1:
                            conv_acc[side, cols] = held["acc"]

                    return run

                units += [unit(tap) for tap in range(KERNEL)]
        return units

    def first_norm(r):
        def piece():
            act, slope1 = gelu_parts(conv_acc[r, :] + conv_b[...])
            n1, s1 = normalize(act)
            branch = (n1 * gain1[...] + bias1[...]).astype(jnp.bfloat16)
            w, at = r.start // rows_here, r.start % rows_here
            start = ext[w, rows_here + at : rows_here + at + fine, :]
            value = start.astype(jnp.float32) + branch.astype(jnp.float32)
            middle[r, :] = value
            low = value.astype(jnp.bfloat16)
            middle_low[r, :] = low
            n1_all[conv_slot, r, :] = n1
            q1_all[conv_slot, r, :] = s1 * slope1

        return piece

    def forward_slots(extra):
        ups, lowers = {}, {}

        def up(j, m):
            def run():
                ups[j, m] = dot(middle_low[sides[m], :], up_w[:, tiles[j]])

            return run

        def act(j, m, k):
            def run():
                at = slice(k * 64, (k + 1) * 64)
                r = slice(m * side_tile + k * 64, m * side_tile + (k + 1) * 64)
                h, sl = gelu_parts(ups[j, m][at] + up_b[:, tiles[j]])
                hidden[r, tiles[j]] = h.astype(jnp.bfloat16)
                slope[r, tiles[j]] = sl

            return run

        def down(j, m, n):
            def run():
                value = dot(hidden[sides[m], tiles[j]], down_w[tiles[j], outs[n]])
                lowers[m, n] = lowers[m, n] + value if j > 0 else value
                if j == len(tiles) - 1:
                    lower[sides[m], outs[n]] = lowers[m, n]

            return run

        count = len(tiles)
        for m in range(len(sides)):
            up(0, m)()
        taken = 0
        for j in range(count + 1):
            units, pieces = [], []
            if j >= 1:
                units += [down(j - 1, m, n) for m in range(len(sides)) for n in range(len(outs))]
            if j + 1 < count:
                units += [up(j + 1, m) for m in range(len(sides))]
            if j < count:
                pieces += [act(j, m, k) for m in range(len(sides)) for k in range(side_tile // 64)]
            upto = len(extra) * (j + 1) // (count + 1)
            pieces += extra[taken:upto]
            taken = upto
            interleave(units, pieces)

    def second_norm(r):
        def piece():
            w, at = r.start // rows_here, r.start % rows_here
            window = pl.ds(at, fine)
            keep = keeps[1, jnp.maximum(step - 1, 0) * group + w]
            n2, s2 = normalize(lower[r, :] + down_b[...])
            value = middle[r, :] + (n2 * gain2[...] + bias2[...])
            out[w, window, :] = (value * keep).astype(jnp.bfloat16)
            incoming = cot[w, window, :].astype(jnp.float32) * keep
            low = normalize_back(incoming, n2, s2, gain2[...]).astype(jnp.bfloat16)
            lower_out[r, :] = low
            mid_grad[r, :] = incoming
            add_vec(0, incoming * n2)
            add_vec(1, incoming)
            add_vec(2, low.astype(jnp.float32))

        return piece

    def backward_slots(extra):
        hids, mids = {}, {}

        def hid(j, m):
            def run():
                hids[j, m] = dot_nt(lower_out[sides[m], :], down_w[tiles[j], :])

            return run

        def act(j, m, k):
            def run():
                at = slice(k * 64, (k + 1) * 64)
                r = slice(m * side_tile + k * 64, m * side_tile + (k + 1) * 64)
                low = (hids[j, m][at] * slope[r, tiles[j]]).astype(jnp.bfloat16)
                upper_out[r, tiles[j]] = low
                upb_acc[:, tiles[j]] += rows_in_eights(low.astype(jnp.float32))

            return run

        def mid(j, m, n):
            def run():
                value = dot_nt(upper_out[sides[m], tiles[j]], up_w[outs[n], tiles[j]])
                mids[m, n] = mids[m, n] + value if j > 0 else value
                if j == len(tiles) - 1:
                    mid_grad[sides[m], outs[n]] += mids[m, n]

            return run

        count = len(tiles)
        for m in range(len(sides)):
            hid(0, m)()
        taken = 0
        for j in range(count + 1):
            units, pieces = [], []
            if j >= 1:
                units += [mid(j - 1, m, n) for m in range(len(sides)) for n in range(len(outs))]
            if j + 1 < count:
                units += [hid(j + 1, m) for m in range(len(sides))]
            if j < count:
                pieces += [act(j, m, k) for m in range(len(sides)) for k in range(side_tile // 64)]
            upto = len(extra) * (j + 1) // (count + 1)
            pieces += extra[taken:upto]
            taken = upto
            interleave(units, pieces)

    def first_back(r):
        def piece():
            w, at = r.start // rows_here, r.start % rows_here
            window = pl.ds(at, fine)
            low = mid_grad[r, :].astype(jnp.bfloat16)
            mid_out[w, window, :] = low
            grad = low.astype(jnp.float32)
            n1 = n1_all[back_slot, r, :]
            add_vec(3, grad * n1)
            add_vec(4, grad)
            pre_low = normalize_back(grad, n1, q1_all[back_slot, r, :], gain1[...]).astype(jnp.bfloat16)
            pre_keep[keep_slot, w, window, :] = pre_low
            add_vec(5, pre_low.astype(jnp.float32))

        return piece

    @pl.when(step == 0)
    def _():
        barrier = pltpu.get_barrier_semaphore()
        for side in range(2):

            @pl.when(has[side])
            def _():
                pl.semaphore_signal(barrier, inc=1, device_id=other[side], device_id_type=MESH)

        vec_acc[...] = jnp.zeros_like(vec_acc)
        upb_acc[...] = jnp.zeros_like(upb_acc)
        mid_grad[...] = jnp.zeros_like(mid_grad)
        n1_all[...] = jnp.zeros_like(n1_all)
        q1_all[...] = jnp.zeros_like(q1_all)
        pl.semaphore_wait(barrier, (s > 0).astype(jnp.int32) + (s < last).astype(jnp.int32))
        near_first(lambda side: halo(0, side, 0).start())
        for load in weight_loads:
            load.start()
        near_first(lambda side: halo(0, side, 1).start())
        for i in range(1, AHEAD):
            near_first(lambda side: halo(i, side).start())
        for side in range(2):

            @pl.when(jnp.logical_not(has[side]))
            def _():
                land = (from_l, from_r)[side]
                land[...] = jnp.zeros_like(land)

    @pl.when(step + AHEAD < blocks)
    def _():
        near_first(lambda side: halo(step + AHEAD, side).start())

    for side in range(2):

        @pl.when(has[side] & (step > 0) & (step < blocks))
        def _():
            halo_in(step, side).wait_recv()

        @pl.when(has[side] & (step >= 4) & (step - 4 < EARLY))
        def _():
            back(step - 4, side).wait_send()

    puts(False, (0, step - 1), (1, step - 2), (2, step - 3), (3, step - 3))

    @pl.when((step > 0) & (step < blocks))
    def _():
        forward_slots([build_ext(w) for w in range(group)] + [first_back(r) for r in fine_rows])
        puts(True, (0, step), (1, step - 1), (2, step - 2), (3, step - 2))
        near_first(lambda side: pl.when((step >= 2) & (step - 2 < EARLY))(lambda: back(step - 2, side).start()))
        puts(False, (4, step - 2), (5, step - 2))
        interleave(conv_units(), [second_norm(r) for r in fine_rows])
        puts(True, (4, step - 1), (5, step - 1))
        puts(False, (6, step - 2), (7, step - 1))
        backward_slots([first_norm(r) for r in fine_rows])
        puts(True, (6, step - 1), (7, step))

    @pl.when(step == 0)
    def _():
        weight_loads[0].wait()
        units = conv_units()
        for part in range(2):
            for side in range(2):
                pl.when(has[side])(lambda: halo_in(0, side, part).wait_recv())
            for w in range(part * per_side, (part + 1) * per_side):
                build_ext(w)()
            half = len(units) // 2
            pieces = [first_norm(r) for r in fine_rows[: len(fine_rows) // 2]] if part else []
            interleave(units[part * half : (part + 1) * half], pieces)
        for r in fine_rows[len(fine_rows) // 2 :]:
            first_norm(r)()
        puts(True, (0, step), (7, step))
        for load in weight_loads[1:]:
            load.wait()

    @pl.when(step == blocks)
    def _():
        forward_slots([first_back(r) for r in fine_rows])
        puts(True, (1, step - 1), (2, step - 2), (3, step - 2))
        puts(False, (4, step - 2), (5, step - 2))
        for r in fine_rows:
            second_norm(r)()
        puts(True, (4, step - 1), (5, step - 1))
        puts(False, (6, step - 2), (7, step - 1))
        backward_slots([])
        puts(True, (6, step - 1))

    @pl.when(step == blocks + 1)
    def _():
        for r in fine_rows:
            first_back(r)()
        puts(True, (2, step - 2), (3, step - 2))
        puts(False, (4, step - 2), (5, step - 2), (6, step - 2))

    @pl.when(step == blocks + 1)
    def _():
        for k in range(6):
            d_vec[k : k + 1, :] = col_sum(vec_acc[k])
        d_vec[6:8, :] = jnp.zeros((2, width), jnp.float32)
        for k in range(ff // width):
            d_vec[8 + k : 9 + k, :] = col_sum(upb_acc[:, k * width : (k + 1) * width])
        for k in range(8 + ff // width, d_vec.shape[0]):
            d_vec[k : k + 1, :] = jnp.zeros((1, width), jnp.float32)
        put(2, blocks - 1).wait()
        put(3, blocks - 1).wait()
        for side in range(2):

            @pl.when(has[side])
            def _():
                for part in range(2):
                    halo(0, side, part).wait_send()
                for i in range(1, blocks):
                    halo(i, side).wait_send()
                for i in range(EARLY):
                    back_in(i, side).wait_recv()


def block_params(conv_w, conv_b, gain1, bias1, up_w, up_b, down_w, down_b, gain2, bias2):
    row = lambda v: v.reshape(1, -1)
    return [conv_w, row(conv_b), row(gain1), row(bias1), up_w, row(up_b), down_w, row(down_b), row(gain2), row(bias2)]


def flat_specs(rows, ff, width):
    return [pl.BlockSpec((rows, w), lambda i: (i, 0)) for w in (ff, ff, width, width)]


def flat_shapes(rows, ff, width):
    return [jax.ShapeDtypeStruct((rows, w), jnp.bfloat16) for w in (ff, ff, width, width)]


def blocks_halo(keeps, x, cot, params):
    windows, rows_here, width = cot.shape
    ff = params[4].shape[1]
    group = TILE_ROWS // rows_here
    count = windows // group
    rows = group * rows_here

    def late(by):
        return lambda i: jnp.clip(i - by, 0, count - 1)

    def tile(by):
        return pl.BlockSpec((group, rows_here, width), lambda i: (late(by)(i), 0, 0))

    whole = pl.BlockSpec(memory_space=pltpu.VMEM)
    anywhere = pl.BlockSpec(memory_space=pl.ANY)
    like = jax.ShapeDtypeStruct(cot.shape, jnp.bfloat16)
    square = pltpu.VMEM((rows, width), jnp.float32)
    block = pltpu.VMEM((group, rows_here, width), jnp.bfloat16)
    dma = pltpu.SemaphoreType.DMA((count + 1, 2))
    return pl.pallas_call(
        functools.partial(block_halo_kernel, count),
        grid=(count + 2,),
        in_specs=[pl.BlockSpec(memory_space=pltpu.SMEM), anywhere, tile(0), tile(1)]
        + [anywhere if p.shape[0] > 1 else whole for p in params],
        out_specs=[anywhere] * 10 + [whole],
        out_shape=[like, jax.ShapeDtypeStruct((windows, 3 * rows_here, width), jnp.bfloat16), like, like]
        + flat_shapes(windows * rows_here, ff, width)
        + [like, like, jax.ShapeDtypeStruct((16, width), jnp.float32)],
        scratch_shapes=[
            block,
            pltpu.VMEM((group, 3 * rows_here, width), jnp.bfloat16),
            block,
            pltpu.VMEM((rows, ff), jnp.bfloat16),
            pltpu.VMEM((rows, ff), jnp.bfloat16),
            pltpu.VMEM((rows, width), jnp.bfloat16),
            pltpu.VMEM((rows, ff), jnp.float32),
            square,
            pltpu.VMEM((2, rows, width), jnp.float32),
            pltpu.VMEM((2, rows, width), jnp.float32),
            square,
            pltpu.VMEM((rows, width), jnp.bfloat16),
            square,
            square,
            pltpu.VMEM((6, 8, width), jnp.float32),
            pltpu.VMEM((8, ff), jnp.float32),
            pltpu.VMEM(cot.shape, jnp.bfloat16),
            pltpu.VMEM(cot.shape, jnp.bfloat16),
            pltpu.VMEM((2, group, rows_here, width), jnp.bfloat16),
            dma,
            dma,
            dma,
            dma,
            pltpu.SemaphoreType.DMA((8,)),
        ]
        + [pltpu.VMEM(p.shape, jnp.bfloat16) for p in params if p.shape[0] > 1]
        + [pltpu.SemaphoreType.DMA((3,))],
        compiler_params=pltpu.CompilerParams(
            vmem_limit_bytes=VMEM_BYTES, collective_id=0, has_side_effects=True
        ),
        name="block",
    )(keeps, x, x, cot, *params)


def blocks(keeps, parts, cot, params):
    windows, rows_here, width = cot.shape
    depth = len(parts) // 2
    ff = params[4].shape[1]
    group = max(1, TILE_ROWS // rows_here)
    rows = group * rows_here
    tile = pl.BlockSpec((group, rows_here, width), lambda i: (i, 0, 0))
    wide = pl.BlockSpec((group, (2 * depth + 1) * rows_here, width), lambda i: (i, 0, 0))
    whole = pl.BlockSpec(memory_space=pltpu.VMEM)
    like = jax.ShapeDtypeStruct(cot.shape, jnp.bfloat16)
    return pl.pallas_call(
        functools.partial(block_kernel, depth),
        grid=(windows // group,),
        in_specs=[pl.BlockSpec(memory_space=pltpu.SMEM)] + [tile] * (len(parts) + 1) + [whole] * len(params),
        out_specs=[tile, wide, tile, tile] + flat_specs(rows, ff, width) + [whole],
        out_shape=[like, jax.ShapeDtypeStruct((windows, (2 * depth + 1) * rows_here, width), jnp.bfloat16), like, like]
        + flat_shapes(windows * rows_here, ff, width)
        + [jax.ShapeDtypeStruct((16, width), jnp.float32)],
        scratch_shapes=[pltpu.VMEM((rows, ff), jnp.float32)],
        compiler_params=pltpu.CompilerParams(vmem_limit_bytes=VMEM_BYTES),
        name="block_general",
    )(keeps, *parts, cot, *params)


def back_kernel(depth, *refs):
    pieces = 2 * depth + 1
    keeps = refs[0]
    parts = refs[1 : 1 + pieces]
    start_in, mid_in, conv_w, out, d_conv, ext = refs[1 + pieces :]
    step = pl.program_id(0)
    group, rows_here, width = start_in.shape
    rows = group * rows_here
    base = depth * rows_here - REACH

    @pl.when(step == 0)
    def _():
        d_conv[...] = jnp.zeros_like(d_conv)

    start = []
    for g in range(group):
        start.append(start_in[g] * keeps[depth, step * group + g].astype(jnp.bfloat16))
        for i in range(pieces):
            ext[g, i * rows_here : (i + 1) * rows_here, :] = parts[i][g]
    start = jnp.concatenate(start, axis=0)
    grad = jnp.zeros((rows, width), jnp.float32)
    for tap in range(KERNEL):
        begin = base + (KERNEL - 1 - tap) * DILATION
        taken = ext[:, begin : begin + rows_here, :].reshape(rows, width)
        d_conv[tap] += dot_tn(start, taken)
        grad = grad + dot_nt(taken, conv_w[tap])
    grad = grad.astype(jnp.bfloat16).astype(jnp.float32) + mid_in[...].reshape(rows, width).astype(jnp.float32)
    grad = grad.reshape(group, rows_here, width)
    for g in range(group):
        out[g] = (grad[g] * keeps[depth, step * group + g]).astype(jnp.bfloat16)


def conv_back(keeps, parts, start, mid, conv_w):
    windows, rows_here, width = start.shape
    depth = len(parts) // 2
    group = max(1, TILE_ROWS // rows_here)
    tile = pl.BlockSpec((group, rows_here, width), lambda i: (i, 0, 0))
    whole = pl.BlockSpec(memory_space=pltpu.VMEM)
    return pl.pallas_call(
        functools.partial(back_kernel, depth),
        grid=(windows // group,),
        in_specs=[pl.BlockSpec(memory_space=pltpu.SMEM)] + [tile] * (len(parts) + 2) + [whole],
        out_specs=[tile, whole],
        out_shape=[
            jax.ShapeDtypeStruct(start.shape, jnp.bfloat16),
            jax.ShapeDtypeStruct((KERNEL, width, width), jnp.float32),
        ],
        scratch_shapes=[pltpu.VMEM((group, (2 * depth + 1) * rows_here, width), jnp.bfloat16)],
        compiler_params=pltpu.CompilerParams(vmem_limit_bytes=VMEM_BYTES),
        name="conv_back_general",
    )(keeps, *parts, start, mid, conv_w)


class Reducer:
    stages = 8
    gap = 2

    def __init__(self, count, acc, res, res_out, bufs, sems):
        self.count, self.acc, self.res, self.res_out = count, acc, res, res_out
        self.core_in, self.send1, self.recv1, self.kept1 = bufs[:4]
        self.send2, self.recv2, self.kept2 = bufs[4:7]
        self.send3, self.recv3, self.kept3, self.fin = bufs[7:11]
        (
            self.c_s, self.c_r, self.a_s, self.a_r, self.b_s, self.b_r, self.z_s, self.z_r,
            self.zg_s, self.zg_r, self.bg_s, self.bg_r, self.ag_s, self.ag_r, self.cg_s, self.cg_r, self.out_s,
        ) = sems
        s, b = lax.axis_index("seq"), lax.axis_index("batch")
        self.core, self.z = lax.rem(s, 2), lax.div(s, 2)
        self.x, self.y = lax.rem(b, 2), lax.div(b, 2)
        self.core_peer = (s + 1 - 2 * self.core, b)
        x_peer = (s, b + 1 - 2 * self.x)
        y_peer = (s, b + 2 - 4 * self.y)
        self.first_peer, self.second_peer = (x_peer, y_peer), (y_peer, x_peer)
        self.z_to = [(lax.rem(self.z + d, 4) * 2 + self.core, b) for d in (1, 2, 3)]
        self.z_of = [lax.rem(self.z + d, 4) for d in (1, 2, 3)]
        self.first, self.second = (self.x, self.y), (self.y, self.x)
        self.half = acc.shape[1] // 2
        self.own = self.core * self.half
        self.cols = (slice(0, 256), slice(256, 512))
        self.vec_peers = [
            self.core_peer,
            x_peer,
            y_peer,
            (s + 2 - 4 * lax.rem(self.z, 2), b),
            (s + 4 - 8 * lax.div(self.z, 2), b),
        ]

    def peers(self):
        return [self.core_peer, self.first_peer[0], self.first_peer[1]] + self.z_to

    def rows(self, base, count):
        return pl.ds(pl.multiple_of(base, 16), count)

    def core_copy(self, c):
        r = lax.rem(c, RING)
        away = self.rows((1 - self.core) * self.half, self.half)
        return remote(self.acc.at[r, away], self.core_in.at[r], self.c_s.at[r], self.c_r.at[r], self.core_peer)

    def copy1(self, c, h):
        r = lax.rem(c, RING)
        at = (r, slice(None), self.cols[h])
        return remote(self.send1.at[at], self.recv1.at[at], self.a_s.at[r, h], self.a_r.at[r, h], self.first_peer[h])

    def copy2(self, c, h):
        r = lax.rem(c, RING)
        at = (r, slice(None), self.cols[h])
        return remote(self.send2.at[at], self.recv2.at[at], self.b_s.at[r, h], self.b_r.at[r, h], self.second_peer[h])

    def copy3(self, c, d):
        r = lax.rem(c, RING)
        return remote(self.send3.at[r, d], self.recv3.at[r, d], self.z_s.at[r, d], self.z_r.at[r, d], self.z_to[d])

    def base1(self, h):
        return self.own + self.first[h] * 128

    def base2(self, h):
        return self.base1(h) + self.second[h] * 64

    def spread_z(self, c, d, h):
        r = lax.rem(c, RING)
        land = self.res.at[c, self.rows(self.base2(h) + self.z * 16, 16), self.cols[h]]
        return remote(
            self.fin.at[r, :, self.cols[h]], land, self.zg_s.at[r, d, h], self.zg_r.at[r, d, h], self.z_to[d]
        )

    def spread_same(self, c, base, count, cols, s, r, peer):
        part = self.res.at[c, self.rows(base, count), cols]
        return remote(part, part, s, r, peer)

    def spread2(self, c, h):
        r = lax.rem(c, RING)
        return self.spread_same(
            c, self.base2(h), 64, self.cols[h], self.bg_s.at[r, h], self.bg_r.at[r, h], self.second_peer[h]
        )

    def spread1(self, c, h):
        r = lax.rem(c, RING)
        return self.spread_same(
            c, self.base1(h), 128, self.cols[h], self.ag_s.at[r, h], self.ag_r.at[r, h], self.first_peer[h]
        )

    def spread_core(self, c):
        r = lax.rem(c, RING)
        return self.spread_same(
            c, self.own, self.half, slice(0, 512), self.cg_s.at[r], self.cg_r.at[r], self.core_peer
        )

    def write_out(self, c, act):
        up_out, down_out, conv_out = self.res_out
        width, tiles = self.acc.shape[1], up_out.shape[1] // self.acc.shape[1]
        wide = lambda i: pl.ds(pl.multiple_of(i * width, width), width)

        def copy(to):
            return lambda: act(pltpu.make_async_copy(self.res.at[c], to, self.out_s.at[lax.rem(c, 2)]))

        pl.when(c < tiles)(copy(up_out.at[:, wide(c)]))
        pl.when((c >= tiles) & (c < 2 * tiles))(copy(down_out.at[wide(c - tiles), :]))
        pl.when(c >= 2 * tiles)(copy(conv_out.at[c - 2 * tiles]))

    def stage0(self, c):
        self.core_copy(c).start()

    def stage1(self, c):
        self.core_copy(c).wait()
        r = lax.rem(c, RING)
        for h in range(2):
            cols = self.cols[h]
            keep, give = self.first[h] * 128, (1 - self.first[h]) * 128
            self.send1[r, :, cols] = (
                self.acc[r, self.rows(self.own + give, 128), cols] + self.core_in[r, self.rows(give, 128), cols]
            ).astype(jnp.bfloat16)
            self.copy1(c, h).start()
            self.kept1[r, :, cols] = (
                self.acc[r, self.rows(self.own + keep, 128), cols] + self.core_in[r, self.rows(keep, 128), cols]
            )

    def stage2(self, c):
        r = lax.rem(c, RING)
        for h in range(2):
            self.copy1(c, h).wait()
            cols = self.cols[h]
            keep, give = self.second[h] * 64, (1 - self.second[h]) * 64
            self.send2[r, :, cols] = (
                self.kept1[r, self.rows(give, 64), cols]
                + self.recv1[r, self.rows(give, 64), cols].astype(jnp.float32)
            ).astype(jnp.bfloat16)
            self.copy2(c, h).start()
            self.kept2[r, :, cols] = self.kept1[r, self.rows(keep, 64), cols] + self.recv1[
                r, self.rows(keep, 64), cols
            ].astype(jnp.float32)

    def stage3(self, c):
        r = lax.rem(c, RING)
        for h in range(2):
            self.copy2(c, h).wait()
        for d in range(3):
            at = self.rows(self.z_of[d] * 16, 16)
            self.send3[r, d] = (self.kept2[r, at, :] + self.recv2[r, at, :].astype(jnp.float32)).astype(jnp.bfloat16)
            self.copy3(c, d).start()
        at = self.rows(self.z * 16, 16)
        self.kept3[r] = self.kept2[r, at, :] + self.recv2[r, at, :].astype(jnp.float32)

    def stage4(self, c):
        r = lax.rem(c, RING)
        total = self.kept3[r]
        for d in range(3):
            self.copy3(c, d).wait()
            total = total + self.recv3[r, d].astype(jnp.float32)
        total = total.astype(jnp.bfloat16)
        self.fin[r] = total
        for h in range(2):
            for d in range(3):
                self.spread_z(c, d, h).start()
            self.res[c, self.rows(self.base2(h) + self.z * 16, 16), self.cols[h]] = total[:, self.cols[h]]

    def stage5(self, c):
        for h in range(2):
            for d in range(3):
                self.spread_z(c, d, h).wait()
            self.spread2(c, h).start()

    def stage6(self, c):
        for h in range(2):
            self.spread2(c, h).wait()
            self.spread1(c, h).start()

    def stage7(self, c):
        for h in range(2):
            self.spread1(c, h).wait()
        self.spread_core(c).start()

    def stage8(self, c):
        self.spread_core(c).wait()

        @pl.when(c >= 2)
        def _():
            self.write_out(c - 2, lambda copy: copy.wait())

        self.write_out(c, lambda copy: copy.start())

    def tick(self, t):
        for stage in range(self.stages, -1, -1):
            c = t - stage * self.gap

            @pl.when((c >= 0) & (c < self.count))
            def _():
                getattr(self, "stage%d" % stage)(c)

    def finish(self):
        for c in range(max(0, self.count - 2), self.count):
            self.write_out(jnp.int32(c), lambda copy: copy.wait())


def hidden_width(tiles):
    return tiles.shape[2]


def reduce_kernel(steps, *refs):
    (
        keeps, hidden, upper, lower_hbm, middle_hbm, vec_in, ext_hbm, pre_hbm, pre_l, pre_r, mid_hbm, conv_hbm,
        grad_out, up_out, down_out, conv_out, vec_out, late_l, late_r,
        ext, pre, lower, middle, tiles, acc, res, pext, midb, gout, vsend, vrecv,
    ) = refs[:31]
    bufs = refs[31:42]
    sems = refs[42:59]
    load_s, ffn_s, in_s, gout_s, v_s, v_r, late_s, late_q, conv_w = refs[59:]
    load_conv = pltpu.make_async_copy(conv_hbm, conv_w, load_s.at[4])
    ff_tiles = hidden.shape[1] // hidden_width(tiles)
    ffn_count = 2 * ff_tiles
    count = ffn_count + KERNEL
    group, rows_here, width = gout.shape[1:]
    rows = group * rows_here
    red = Reducer(count, acc, res, (up_out, down_out, conv_out), bufs, sems)
    s = lax.axis_index("seq")
    last = lax.axis_size("seq") - 1

    b = lax.axis_index("batch")
    has = (s > 0, s < last)
    other = ((s - 1, b), (s + 1, b))
    beyond = jnp.where(red.core == 0, s - 1, s + 1)
    has_beyond = (beyond >= 0) & (beyond <= last)

    barrier = pltpu.get_barrier_semaphore()
    for peer in red.peers():
        pl.semaphore_signal(barrier, inc=1, device_id=peer, device_id_type=MESH)

    @pl.when(has_beyond)
    def _():
        pl.semaphore_signal(barrier, inc=1, device_id=(beyond, b), device_id_type=MESH)

    def late(i, side):
        at = pl.ds((i - EARLY) * group, group)
        land = (late_r, late_l)[side]
        k = i - EARLY
        return remote(
            pre_hbm.at[pl.ds(i * group, group)], land.at[at], late_s.at[k, side], late_q.at[k, side], other[side]
        )

    def late_in(i, side):
        at = pl.ds((i - EARLY) * group, group)
        land = (late_l, late_r)[side]
        k = i - EARLY
        return remote(
            pre_hbm.at[pl.ds(i * group, group)], land.at[at], late_s.at[k, side], late_q.at[k, 1 - side], other[side]
        )

    load_ext = pltpu.make_async_copy(ext_hbm, ext, load_s.at[0])
    load_pre = pltpu.make_async_copy(pre_hbm, pre, load_s.at[1])

    load_lower = pltpu.make_async_copy(lower_hbm, lower, load_s.at[2])
    load_middle = pltpu.make_async_copy(middle_hbm, middle, load_s.at[3])
    tile_rows = tiles.shape[1]
    per_chunk = lower.shape[0] // tile_rows

    def load_tile(i, act):
        r = lax.rem(i, 2)
        c = lax.div(i, per_chunk)
        at = pl.ds(pl.multiple_of(lax.rem(i, per_chunk) * tile_rows, tile_rows), tile_rows)

        def copy(source, first):
            cols = pl.ds(pl.multiple_of((c - first) * width, width), width)
            return lambda: act(pltpu.make_async_copy(source.at[at, cols], tiles.at[r], ffn_s.at[r]))

        pl.when(c < ff_tiles)(copy(upper, 0))
        pl.when((c >= ff_tiles) & (c < ffn_count))(copy(hidden, ff_tiles))

    def ffn_grad(c):
        r = lax.rem(c, RING)

        def part(i):
            tile = c * per_chunk + i
            load_tile(tile, lambda copy: copy.wait())
            load_tile(tile + 1, lambda copy: copy.start())
            at = pl.ds(pl.multiple_of(i * tile_rows, tile_rows), tile_rows)
            slot = lax.rem(tile, 2)

            def add(value):
                @pl.when(i == 0)
                def _():
                    acc[r] = value

                @pl.when(i > 0)
                def _():
                    acc[r] += value

            pl.when(c < ff_tiles)(lambda: add(dot_tn(middle[at], tiles[slot])))
            pl.when(c >= ff_tiles)(lambda: add(dot_tn(tiles[slot], lower[at])))

        lax.fori_loop(0, per_chunk, lambda i, _: (part(i), 0)[1], 0)

    def each_load(i, act, fresh=False):
        slot = lax.rem(i, 2)
        at = pl.ds(i * group, group)
        at_late = pl.ds((i - EARLY) * group, group)
        for side, early_ref, late_ref in ((0, pre_l, late_l), (1, pre_r, late_r)):
            to = pext.at[slot, :, pl.ds(2 * side * rows_here, rows_here)]
            sem = in_s.at[slot, side]

            @pl.when(has[side] & (i < EARLY))
            def _():
                act(pltpu.make_async_copy(early_ref.at[at], to, sem))

            @pl.when(has[side] & (i >= EARLY))
            def _():
                if fresh:
                    late_in(i, side).wait_recv()
                act(pltpu.make_async_copy(late_ref.at[at_late], to, sem))

        act(pltpu.make_async_copy(pre_hbm.at[at], pext.at[slot, :, pl.ds(rows_here, rows_here)], in_s.at[slot, 2]))
        act(pltpu.make_async_copy(mid_hbm.at[at], midb.at[slot], in_s.at[slot, 3]))

    def store_rows(i):
        slot = lax.rem(i, 2)
        return pltpu.make_async_copy(gout.at[slot], grad_out.at[pl.ds(i * group, group)], gout_s.at[slot])

    load_middle.start()
    for i in range(1):
        load_tile(jnp.int32(i), lambda copy: copy.start())
    for side, at in ((s > 0, 0), (s < last, 2)):

        @pl.when(jnp.logical_not(side))
        def _():
            pext[:, :, at * rows_here : (at + 1) * rows_here, :] = jnp.zeros(
                (2, group, rows_here, width), jnp.bfloat16
            )

    pl.semaphore_wait(barrier, len(red.peers()) + has_beyond.astype(jnp.int32))
    for i in range(EARLY, steps):
        for side in range(2):
            pl.when(has[1 - side] & (red.core == 0))(lambda: late(i, 1 - side).start())
            pl.when(has[side] & (red.core == 1))(lambda: late(i, side).start())

    def vec_copy(q):
        return remote(vsend.at[q], vrecv.at[q], v_s.at[q], v_r.at[q], red.vec_peers[q])

    def row_block(i):
        each_load(i, lambda copy: copy.wait())

        @pl.when(i + 1 < steps)
        def _():
            each_load(i + 1, lambda copy: copy.start(), True)

        slot = lax.rem(i, 2)
        grad = jnp.zeros((rows, width), jnp.float32)
        for tap in range(KERNEL):
            begin = (KERNEL - 1 - tap) * DILATION
            taken = pext[slot, :, begin : begin + rows_here, :].reshape(rows, width)
            grad = grad + dot_nt(taken, conv_w[tap])
        grad = grad.astype(jnp.bfloat16).astype(jnp.float32)
        grad = (grad + midb[slot].reshape(rows, width).astype(jnp.float32)).reshape(group, rows_here, width)

        @pl.when(i >= 2)
        def _():
            store_rows(i - 2).wait()

        for g in range(group):
            gout[slot, g] = (grad[g] * keeps[1, i * group + g]).astype(jnp.bfloat16)
        store_rows(i).start()

    def tap_grad(tap):
        r = lax.rem(ffn_count + tap, RING)
        begin = pl.multiple_of(tap * DILATION, DILATION)

        taken = ext[:, pl.ds(begin, rows_here), :].reshape(steps * rows, width)
        acc[r] = dot_tn(taken, pre[...].reshape(steps * rows, width))

    load_middle.wait()

    def tick(t, _):
        red.tick(t)
        for q in range(6):

            @pl.when(t == q)
            def _():
                if q == 0:
                    value = vec_in[...]
                else:
                    vec_copy(q - 1).wait()
                    value = vsend[q - 1] + vrecv[q - 1]
                if q < 5:
                    vsend[q] = value
                    vec_copy(q).start()
                else:
                    vec_out[...] = value

        pl.when(t == 0)(lambda: load_lower.start())
        pl.when(t == 2)(lambda: load_pre.start())
        pl.when(t == 3)(lambda: load_ext.start())
        pl.when(t == 4)(lambda: load_conv.start())
        pl.when(t == ffn_count)(lambda: each_load(0, lambda copy: copy.start()))
        chunk = t + 1

        @pl.when(chunk == ff_tiles)
        def _():
            load_lower.wait()

        @pl.when(chunk < ffn_count)
        def _():
            ffn_grad(chunk)

        @pl.when(chunk == ffn_count)
        def _():
            load_ext.wait()
            load_pre.wait()
            load_conv.wait()

        rest = t - (count - 1)

        @pl.when((rest >= 0) & (rest < steps))
        def _():
            row_block(rest)

        tap = chunk - ffn_count

        @pl.when((tap >= 0) & (tap < KERNEL))
        def _():
            tap_grad(tap)

        return 0

    lax.fori_loop(-1, count + red.stages * red.gap, tick, 0)
    red.finish()
    for i in range(EARLY, steps):
        for side in range(2):
            pl.when(has[side])(lambda: late(i, side).wait_send())
    for i in range(max(0, steps - 2), steps):
        store_rows(i).wait()


def reduce_all(keeps, hidden, upper, lower, middle, vec, ext, pre, pre_l, pre_r, mid, conv_w):
    windows, rows_here, width = pre.shape
    ff = hidden.shape[1]
    group = TILE_ROWS // rows_here
    steps = windows // group
    count = 2 * ff // width + KERNEL
    whole = pl.BlockSpec(memory_space=pltpu.VMEM)
    anywhere = pl.BlockSpec(memory_space=pl.ANY)
    dma = pltpu.SemaphoreType.DMA
    half = width // 2
    rows = group * rows_here
    return pl.pallas_call(
        functools.partial(reduce_kernel, steps),
        in_specs=[pl.BlockSpec(memory_space=pltpu.SMEM), anywhere, anywhere, anywhere, anywhere, whole] + [anywhere] * 6,
        out_specs=[anywhere] * 4 + [whole, anywhere, anywhere],
        out_shape=[
            jax.ShapeDtypeStruct(pre.shape, jnp.bfloat16),
            jax.ShapeDtypeStruct((width, ff), jnp.bfloat16),
            jax.ShapeDtypeStruct((ff, width), jnp.bfloat16),
            jax.ShapeDtypeStruct((KERNEL, width, width), jnp.bfloat16),
            jax.ShapeDtypeStruct(vec.shape, jnp.float32),
        ]
        + [jax.ShapeDtypeStruct(((steps - EARLY) * group, rows_here, width), jnp.bfloat16)] * 2,
        scratch_shapes=[
            pltpu.VMEM(ext.shape, jnp.bfloat16),
            pltpu.VMEM(pre.shape, jnp.bfloat16),
            pltpu.VMEM(lower.shape, jnp.bfloat16),
            pltpu.VMEM(middle.shape, jnp.bfloat16),
            pltpu.VMEM((2, 4 * rows, width), jnp.bfloat16),
            pltpu.VMEM((RING, width, width), jnp.float32),
            pltpu.VMEM((count, width, width), jnp.bfloat16),
            pltpu.VMEM((2, group, 3 * rows_here, width), jnp.bfloat16),
            pltpu.VMEM((2, group, rows_here, width), jnp.bfloat16),
            pltpu.VMEM((2, group, rows_here, width), jnp.bfloat16),
            pltpu.VMEM((5,) + vec.shape, jnp.float32),
            pltpu.VMEM((5,) + vec.shape, jnp.float32),
            pltpu.VMEM((RING, half, width), jnp.float32),
            pltpu.VMEM((RING, half // 2, width), jnp.bfloat16),
            pltpu.VMEM((RING, half // 2, width), jnp.bfloat16),
            pltpu.VMEM((RING, half // 2, width), jnp.float32),
            pltpu.VMEM((RING, half // 4, width), jnp.bfloat16),
            pltpu.VMEM((RING, half // 4, width), jnp.bfloat16),
            pltpu.VMEM((RING, half // 4, width), jnp.float32),
            pltpu.VMEM((RING, 3, half // 16, width), jnp.bfloat16),
            pltpu.VMEM((RING, 3, half // 16, width), jnp.bfloat16),
            pltpu.VMEM((RING, half // 16, width), jnp.float32),
            pltpu.VMEM((RING, half // 16, width), jnp.bfloat16),
        ]
        + [
            dma((RING,)), dma((RING,)), dma((RING, 2)), dma((RING, 2)), dma((RING, 2)), dma((RING, 2)),
            dma((RING, 3)), dma((RING, 3)), dma((RING, 3, 2)), dma((RING, 3, 2)), dma((RING, 2)), dma((RING, 2)),
            dma((RING, 2)), dma((RING, 2)), dma((RING,)), dma((RING,)), dma((2,)),
        ]
        + [dma((5,)), dma((RING,)), dma((2, 4)), dma((2,)), dma((5,)), dma((5,))]
        + [dma((steps - EARLY, 2)), dma((steps - EARLY, 2))]
        + [pltpu.VMEM(conv_w.shape, jnp.bfloat16)],
        compiler_params=pltpu.CompilerParams(
            vmem_limit_bytes=VMEM_BYTES, collective_id=1, has_side_effects=True
        ),
        name="reduce",
    )(keeps, hidden, upper, lower, middle, vec, ext, pre, pre_l, pre_r, mid, conv_w)


def widen_kernel(*refs):
    for source, target in zip(refs[:3], refs[3:]):
        target[...] = source[...].astype(jnp.float32)


def widened(d_up, d_down, d_conv):
    taps, width, _ = d_conv.shape
    ff = d_down.shape[0]
    parts = taps - 1
    at = lambda i: (jnp.minimum(i, parts - 1), 0)
    specs = [
        pl.BlockSpec((width // parts, ff), at),
        pl.BlockSpec((ff // parts, width), at),
        pl.BlockSpec((1, width, width), lambda i: (i, 0, 0)),
    ]
    return pl.pallas_call(
        widen_kernel,
        grid=(taps,),
        in_specs=specs,
        out_specs=specs,
        out_shape=[jax.ShapeDtypeStruct(d.shape, jnp.float32) for d in (d_up, d_down, d_conv)],
        compiler_params=pltpu.CompilerParams(vmem_limit_bytes=VMEM_BYTES),
        name="tail",
    )(d_up, d_down, d_conv)


def spread(shard, depth):
    return [
        shard if offset == 0 else passed_along(shard, "seq", offset)
        for offset in range(depth, -depth - 1, -1)
    ]


def per_device(
    block_input,
    window_lengths,
    conv_weight,
    conv_bias,
    norm1_gain,
    norm1_bias,
    up_weight,
    up_bias,
    down_weight,
    down_bias,
    norm2_gain,
    norm2_bias,
    out_cotangent,
):
    windows, rows_here, width = block_input.shape
    ff = up_weight.shape[1]
    depth = -(-REACH // rows_here)
    first = (lax.axis_index("seq") + jnp.arange(-depth, depth + 1, dtype=jnp.int32)) * rows_here
    keeps = (first[:, None] < window_lengths[None, :]).astype(jnp.float32)
    params = block_params(
        conv_weight, conv_bias, norm1_gain, norm1_bias, up_weight, up_bias, down_weight, down_bias, norm2_gain, norm2_bias
    )
    tiles = ff // FF_TILE
    if (lax.axis_size("seq"), lax.axis_size("batch"), rows_here) == (8, 4, REACH):
        out, ext, pre_low, mid_low, hidden, upper, lower, middle, pre_l, pre_r, d_vec = blocks_halo(
            keeps, block_input, out_cotangent, params
        )
        input_grad, d_up, d_down, d_conv, d_vec, _, _ = reduce_all(
            keeps, hidden, upper, lower, middle, d_vec, ext, pre_low, pre_l, pre_r, mid_low, conv_weight
        )
        d_up, d_down, d_conv = widened(d_up, d_down, d_conv)
    else:
        parts = spread(block_input, depth)
        out, _, pre_low, mid_low, hidden, upper, lower, middle, d_vec = blocks(keeps, parts, out_cotangent, params)
        input_grad, d_conv = conv_back(keeps, spread(pre_low, depth), block_input, mid_low, conv_weight)
        d_up, d_down = dot_tn(middle, upper), dot_tn(hidden, lower)
        d_up, d_down, d_conv, d_vec = lax.psum((d_up, d_down, d_conv, d_vec), ("seq", "batch"))
    return (
        out,
        input_grad,
        d_conv,
        d_vec[5],
        d_vec[3],
        d_vec[4],
        d_up,
        d_vec[8 : 8 + tiles].reshape(ff),
        d_down,
        d_vec[2],
        d_vec[0],
        d_vec[1],
    )


def solution(mesh):
    rows = P("batch", "seq", None)
    return jax.shard_map(
        per_device,
        mesh=mesh,
        in_specs=(rows, P("batch")) + (P(),) * 10 + (rows,),
        out_specs=(rows, rows) + (P(),) * 10,
        check_vma=False,
    )
```
